32 devices in a mesh: chan: 4 (over z), lag: 4 (over x, core), seg: 2 (over y).
Axes of the slice: x: 2, y: 2, z: 4, core: 2. Of those that a mesh axis runs over, the one named last changes fastest.
Arguments:
- records_owned: float32 [512, 2, 1024], P('chan', 'seg', 'lag'), may hold values from -6 to 6
- section_list: int32 [512], replicated, may hold values from 0 to 511, as said below
- ref_index: int32 [64], replicated, may hold values from 0 to 511, as said below
Outputs:
- correlations: float32 [512, 8192], P(('chan', 'seg'), 'lag')
The draws below stay inside these ranges and needn't reach their ends.
Inputs may be any that keep to these rules, and one draw needn't show every extreme that they name: `section_list`: each value names a channel once. The 128 rows of each owner name exactly 32 channels of every channel block (channels b*128 to (b+1)*128 - 1). `ref_index`: distinct channel numbers.
All inputs are finite; a program needn't handle non-finite values.
Results may differ from the reference program's by a relative error of at most 0.000098.
Values sent between devices are 32-bit elements; how exact they have to be, the bound alone decides.
No kernel may reach another device: no remote copies, remote signals or barrier semaphores. Data moves between devices by JAX's collectives and lax.ppermute only.
A program may use at most 64 MiB of HBM per device.

```python
import math
import jax
import jax.numpy as jnp
from jax import lax

CH_DEV = 128
REF = 64
LAGS = 128
SAMPLES = 2048
CHANNELS = 512
SEGS = 2
SEG_LEN = 1024
NTERMS = 1920


def draw_section_list(key, part):
    blocks = CHANNELS // CH_DEV
    peers = CH_DEV // blocks
    first_key, second_key = jax.random.split(jax.random.fold_in(key, 11))
    positions = jnp.arange(CH_DEV, dtype=jnp.int32)[None, :]
    scores = jax.random.randint(first_key, (blocks, CH_DEV), 0, 1 << 16) * CH_DEV + positions
    ordering = jnp.argsort(scores, axis=1).astype(jnp.int32)
    channel_ids = ordering + (jnp.arange(blocks, dtype=jnp.int32) * CH_DEV)[:, None]
    channel_ids = channel_ids.reshape(blocks, blocks, peers).transpose(1, 0, 2).reshape(blocks, CH_DEV)
    mixing = jax.random.randint(second_key, (blocks, CH_DEV), 0, 1 << 16) * CH_DEV + positions
    shuffle = jnp.argsort(mixing, axis=1).astype(jnp.int32)
    channel_ids = jnp.take_along_axis(channel_ids, shuffle, axis=1)
    return channel_ids.reshape(CHANNELS).astype(jnp.int32)


def draw_ref_index(key, part):
    chosen = jax.random.permutation(jax.random.fold_in(key, 23), CHANNELS)
    return chosen[:REF].astype(jnp.int32)


def steps_of(own_key, dims, cuts, least, largest):
    factor_of, own = 1.0, jax.random.fold_in(own_key, 6)
    for position, blocks in cuts:
        draws = jnp.exp(jax.random.uniform(jax.random.fold_in(own, position), (blocks,), jnp.float32, least / len(cuts), largest / len(cuts)))
        factor_of = factor_of * jnp.repeat(draws, dims[position] // blocks).reshape([-1 if axis == position else 1 for axis in range(len(dims))])
    return factor_of


def centred(stream_key, extent, deviation, limit, pieces=(), held_as=jnp.bfloat16):
    level = steps_of(stream_key, extent, pieces, -0.22, 0.18) if pieces else 1.0
    values = jax.random.normal(stream_key, extent, jnp.float32) * deviation * level
    return jnp.minimum(jnp.maximum(values, -limit), limit).astype(held_as)


def setup_inputs(seed: int = 0) -> dict:
    arg_keys = jax.random.split(jax.random.key(seed), 4)
    records_owned = centred(arg_keys[0], (CHANNELS, SEGS, SEG_LEN), 1.0, 6.0, ((0, 4), (1, 2), (2, 4)), jnp.float32)
    section_list = draw_section_list(jax.random.fold_in(arg_keys[3], 71), 0)
    ref_index = draw_ref_index(jax.random.fold_in(arg_keys[3], 71), 0)
    return dict(records_owned=records_owned, section_list=section_list, ref_index=ref_index)


def reference(records_owned, section_list, ref_index):
    flat = records_owned.reshape(CHANNELS, SAMPLES)
    series = flat[jnp.argsort(section_list).astype(jnp.int32)]
    panel = series[ref_index][:, :NTERMS]

    def one_lag(lag_value):
        window = lax.dynamic_slice_in_dim(series, lag_value, NTERMS, 1)
        return jnp.dot(window, panel.T, precision=lax.Precision.HIGHEST, preferred_element_type=jnp.float32)
    stacked = lax.map(one_lag, jnp.arange(LAGS, dtype=jnp.int32))
    result = jnp.transpose(stacked, (1, 0, 2)).reshape(CHANNELS, LAGS * REF)
    return result / math.sqrt(NTERMS)
```

```python
import functools
import math

import jax
import jax.numpy as jnp
from jax import lax
from jax.experimental import pallas as pl
from jax.experimental.pallas import tpu as pltpu
from jax.sharding import PartitionSpec as P

LAGS = 128
SAMPLES = 2048
PHASES = 4


def halves(value):
    high = value.astype(jnp.bfloat16)
    low = (value - high.astype(jnp.float32)).astype(jnp.bfloat16)
    return high, low


def product(left, right):
    return jnp.dot(left, right, preferred_element_type=jnp.float32)


def product_nt(left, right):
    return lax.dot_general(
        left, right, (((1,), (1,)), ((), ())), preferred_element_type=jnp.float32
    )


def pack_kernel(peers, records_ref, lists_ref, refs_ref, out_ref):
    rows = records_ref.shape[0]
    refs = refs_ref.shape[1]
    share = rows // peers
    width = share + refs
    own = jnp.broadcast_to(lists_ref[pl.ds(lax.axis_index("chan"), 1), :], (rows, rows))
    rank = jnp.sum((own.T < own).astype(jnp.int32), axis=0, keepdims=True)
    target = lax.div(rank, share) * width + lax.rem(rank, share)
    wanted = jnp.broadcast_to(refs_ref[...], (rows, refs)).T
    lines = lax.broadcasted_iota(jnp.int32, (peers * width, rows), 0)
    place = lax.broadcasted_iota(jnp.int32, (refs, rows), 0) + 1
    hit = jnp.sum(jnp.where(wanted == own[:refs], place, 0), axis=0, keepdims=True)
    within = lax.rem(lines, width)
    choose = ((lines == target) | (within - share + 1 == jnp.where(hit > 0, hit, -width))).astype(
        jnp.bfloat16
    )
    high, low = halves(records_ref[:, 0, :])
    out_ref[...] = product(choose, high) + product(choose, low)


def place_kernel(peers, half_count, arrived_ref, lists_ref, out_ref):
    rows = lists_ref.shape[1]
    share = rows // peers
    kept = rows // half_count
    channel = lax.broadcasted_iota(jnp.int32, (rows, rows), 0) + lax.axis_index("chan") * rows
    lane = lax.broadcasted_iota(jnp.int32, (rows, rows), 1)
    line = lax.broadcasted_iota(jnp.int32, (rows, rows), 0)
    owner = jnp.zeros((rows, 1), jnp.int32)
    for peer in range(peers):
        found = (lists_ref[pl.ds(peer, 1), :] == channel).astype(jnp.int32)
        owner = owner + jnp.sum(found, axis=1, keepdims=True) * peer
    same = lane == owner
    earlier = (lane < line).astype(jnp.bfloat16)
    before = product(earlier, same.astype(jnp.bfloat16))
    rank = jnp.sum(jnp.where(same, before, 0.0), axis=1, keepdims=True).astype(jnp.int32)
    source = owner * share + rank
    pick = (lane == source).astype(jnp.bfloat16)
    series = jnp.concatenate([arrived_ref[peer, :share, :] for peer in range(peers)], axis=0)
    high, low = halves(series)
    series = product(pick, high) + product(pick, low)
    panel = arrived_ref[0, share:, :]
    for peer in range(1, peers):
        panel = panel + arrived_ref[peer, share:, :]
    for target in range(out_ref.shape[0]):
        half = target % half_count
        out_ref[target, :kept, :] = series[half * kept : (half + 1) * kept]
        out_ref[target, kept:, :] = panel


def corr_kernel(refs, lag_width, segments, gathered_ref, out_ref):
    chunks = gathered_ref.shape[0]
    kept = out_ref.shape[0]
    order = [i for segment in range(segments) for i in range(segment, chunks, segments)]
    series = jnp.concatenate([gathered_ref[i, :kept, :] for i in order], axis=1)
    panel = jnp.concatenate([gathered_ref[i, kept:, :] for i in order], axis=1)
    samples = panel.shape[1]
    terms = SAMPLES - LAGS
    times = lax.broadcasted_iota(jnp.int32, panel.shape, 1)
    panel = jnp.where(times < terms, panel, 0.0)
    series = pltpu.roll(series, samples - lax.axis_index("lag") * lag_width, 1)
    shifted_panel = jnp.concatenate(
        [panel] + [pltpu.roll(panel, phase, 1) for phase in range(1, PHASES)], axis=0
    )
    panel_high, panel_low = halves(shifted_panel)
    groups = lag_width // PHASES
    shifted = jnp.concatenate(
        [series] + [pltpu.roll(series, samples - PHASES * group, 1) for group in range(1, groups)],
        axis=0,
    )
    series_high, series_low = halves(shifted)
    total = (
        product_nt(series_high, panel_high)
        + product_nt(series_low, panel_high)
        + product_nt(series_high, panel_low)
    )
    total = total * (1.0 / math.sqrt(terms))
    width = PHASES * refs
    for group in range(groups):
        out_ref[:, group * width : (group + 1) * width] = total[group * kept : (group + 1) * kept]


def shards(records_owned, section_list, ref_index):
    peers = lax.axis_size("chan")
    segments = lax.axis_size("seg")
    rows, _, samples = records_owned.shape
    refs = ref_index.shape[0]
    share = rows // peers
    kept = rows // segments
    plane = lax.axis_size("lag") * segments
    lag_width = LAGS // lax.axis_size("lag")
    lists = section_list.reshape(peers, rows)
    params = pltpu.CompilerParams(vmem_limit_bytes=48 * 1024 * 1024)
    packed = pl.pallas_call(
        functools.partial(pack_kernel, peers),
        out_shape=jax.ShapeDtypeStruct((peers * (share + refs), samples), jnp.float32),
        compiler_params=params,
        name="pack",
    )(records_owned, lists, ref_index.reshape(1, refs))
    arrived = lax.all_to_all(
        packed.reshape(peers, share + refs, samples), "chan", split_axis=0, concat_axis=0, tiled=True
    )
    placed = pl.pallas_call(
        functools.partial(place_kernel, peers, segments),
        out_shape=jax.ShapeDtypeStruct((plane, kept + refs, samples), jnp.float32),
        compiler_params=params,
        name="place",
    )(arrived, lists)
    gathered = lax.all_to_all(placed, ("lag", "seg"), split_axis=0, concat_axis=0, tiled=True)
    return pl.pallas_call(
        functools.partial(corr_kernel, refs, lag_width, segments),
        out_shape=jax.ShapeDtypeStruct((kept, lag_width * refs), jnp.float32),
        compiler_params=params,
        name="correlate",
    )(gathered)


def solution(mesh):
    return jax.shard_map(
        shards,
        mesh=mesh,
        in_specs=(P("chan", "seg", "lag"), P(), P()),
        out_specs=P(("chan", "seg"), "lag"),
        check_vma=False,
    )
```

```python
import functools
import math

import jax
import jax.numpy as jnp
from jax import lax
from jax.experimental import pallas as pl
from jax.experimental.pallas import tpu as pltpu
from jax.sharding import PartitionSpec as P

LAGS = 128
SAMPLES = 2048
PHASES = 4


def halves(value):
    high = value.astype(jnp.bfloat16)
    low = (value - high.astype(jnp.float32)).astype(jnp.bfloat16)
    return high, low


def product(left, right):
    return jnp.dot(left, right, preferred_element_type=jnp.float32)


def product_nt(left, right):
    return lax.dot_general(
        left, right, (((1,), (1,)), ((), ())), preferred_element_type=jnp.float32
    )


def steps(lags, segments):
    return [(lag, segment) for lag in range(lags) for segment in range(segments)]


def swapped(value, lag_step, segment_step):
    lags, segments = lax.axis_size("lag"), lax.axis_size("seg")
    pairs = [
        (lag * segments + segment, (lag ^ lag_step) * segments + (segment ^ segment_step))
        for lag, segment in steps(lags, segments)
    ]
    return lax.ppermute(value, ("lag", "seg"), pairs)


def pack_kernel(peers, records_ref, lists_ref, refs_ref, out_ref):
    rows = records_ref.shape[0]
    refs = refs_ref.shape[1]
    share = rows // peers
    width = share + refs
    own = jnp.broadcast_to(lists_ref[pl.ds(lax.axis_index("chan"), 1), :], (rows, rows))
    rank = jnp.sum((own.T < own).astype(jnp.int32), axis=0, keepdims=True)
    target = lax.div(rank, share) * width + lax.rem(rank, share)
    wanted = jnp.broadcast_to(refs_ref[...], (rows, refs)).T
    lines = lax.broadcasted_iota(jnp.int32, (peers * width, rows), 0)
    place = lax.broadcasted_iota(jnp.int32, (refs, rows), 0) + 1
    hit = jnp.sum(jnp.where(wanted == own[:refs], place, 0), axis=0, keepdims=True)
    within = lax.rem(lines, width)
    choose = ((lines == target) | (within - share + 1 == jnp.where(hit > 0, hit, -width))).astype(
        jnp.bfloat16
    )
    high, low = halves(records_ref[:, 0, :])
    out_ref[...] = product(choose, high) + product(choose, low)


def place_kernel(peers, half_count, arrived_ref, lists_ref, *out_refs):
    rows = lists_ref.shape[1]
    share = rows // peers
    kept = rows // half_count
    channel = lax.broadcasted_iota(jnp.int32, (rows, rows), 0) + lax.axis_index("chan") * rows
    lane = lax.broadcasted_iota(jnp.int32, (rows, rows), 1)
    line = lax.broadcasted_iota(jnp.int32, (rows, rows), 0)
    owner = jnp.zeros((rows, 1), jnp.int32)
    for peer in range(peers):
        found = (lists_ref[pl.ds(peer, 1), :] == channel).astype(jnp.int32)
        owner = owner + jnp.sum(found, axis=1, keepdims=True) * peer
    same = lane == owner
    earlier = (lane < line).astype(jnp.bfloat16)
    before = product(earlier, same.astype(jnp.bfloat16))
    rank = jnp.sum(jnp.where(same, before, 0.0), axis=1, keepdims=True).astype(jnp.int32)
    source = owner * share + rank
    pick = (lane == source).astype(jnp.bfloat16)
    series = jnp.concatenate([arrived_ref[peer, :share, :] for peer in range(peers)], axis=0)
    high, low = halves(series)
    series = product(pick, high) + product(pick, low)
    panel = arrived_ref[0, share:, :]
    for peer in range(1, peers):
        panel = panel + arrived_ref[peer, share:, :]
    own = lax.axis_index("seg")
    for part in range(half_count):
        half = lax.bitwise_xor(own, part)
        chosen = series[:kept]
        for other in range(1, half_count):
            chosen = jnp.where(half == other, series[other * kept : (other + 1) * kept], chosen)
        out_refs[part][:kept, :] = chosen
        out_refs[part][kept:, :] = panel


def corr_kernel(refs, lag_width, *rest):
    *chunk_refs, out_ref, joined_ref = rest
    kept = out_ref.shape[0]
    lags, segments = lax.axis_size("lag"), lax.axis_size("seg")
    width = chunk_refs[0].shape[1]
    for (lag_step, segment_step), chunk_ref in zip(steps(lags, segments), chunk_refs):
        lag = lax.bitwise_xor(lax.axis_index("lag"), lag_step)
        segment = lax.bitwise_xor(lax.axis_index("seg"), segment_step)
        start = pl.multiple_of((segment * lags + lag) * width, width)
        joined_ref[:, pl.ds(start, width)] = chunk_ref[...]
    series = joined_ref[:kept, :]
    panel = joined_ref[kept:, :]
    samples = panel.shape[1]
    terms = SAMPLES - LAGS
    times = lax.broadcasted_iota(jnp.int32, panel.shape, 1)
    panel = jnp.where(times < terms, panel, 0.0)
    series = pltpu.roll(series, samples - lax.axis_index("lag") * lag_width, 1)
    shifted_panel = jnp.concatenate(
        [panel] + [pltpu.roll(panel, phase, 1) for phase in range(1, PHASES)], axis=0
    )
    panel_high, panel_low = halves(shifted_panel)
    groups = lag_width // PHASES
    shifted = jnp.concatenate(
        [series] + [pltpu.roll(series, samples - PHASES * group, 1) for group in range(1, groups)],
        axis=0,
    )
    series_high, series_low = halves(shifted)
    total = (
        product_nt(series_high, panel_high)
        + product_nt(series_low, panel_high)
        + product_nt(series_high, panel_low)
    )
    total = total * (1.0 / math.sqrt(terms))
    columns = PHASES * refs
    for group in range(groups):
        out_ref[:, group * columns : (group + 1) * columns] = total[group * kept : (group + 1) * kept]


def shards(records_owned, section_list, ref_index):
    peers = lax.axis_size("chan")
    segments = lax.axis_size("seg")
    rows, _, samples = records_owned.shape
    refs = ref_index.shape[0]
    share = rows // peers
    kept = rows // segments
    lags = lax.axis_size("lag")
    lag_width = LAGS // lags
    lists = section_list.reshape(peers, rows)
    params = pltpu.CompilerParams(vmem_limit_bytes=48 * 1024 * 1024)
    packed = pl.pallas_call(
        functools.partial(pack_kernel, peers),
        out_shape=jax.ShapeDtypeStruct((peers * (share + refs), samples), jnp.float32),
        compiler_params=params,
        name="pack",
    )(records_owned, lists, ref_index.reshape(1, refs))
    arrived = lax.all_to_all(
        packed.reshape(peers, share + refs, samples), "chan", split_axis=0, concat_axis=0, tiled=True
    )
    placed = pl.pallas_call(
        functools.partial(place_kernel, peers, segments),
        out_shape=[jax.ShapeDtypeStruct((kept + refs, samples), jnp.float32)] * segments,
        compiler_params=params,
        name="place",
    )(arrived, lists)
    held = {(0, 0): placed[0]}
    for lag_step in range(0, lags, 2):
        for segment_step in range(segments):
            if lag_step or segment_step:
                held[lag_step, segment_step] = swapped(placed[segment_step], lag_step, segment_step)
    for lag_step, segment_step in list(held):
        held[lag_step + 1, segment_step] = swapped(held[lag_step, segment_step], 1, 0)
    return pl.pallas_call(
        functools.partial(corr_kernel, refs, lag_width),
        out_shape=jax.ShapeDtypeStruct((kept, lag_width * refs), jnp.float32),
        scratch_shapes=[pltpu.VMEM((kept + refs, lags * segments * samples), jnp.float32)],
        compiler_params=params,
        name="correlate",
    )(*[held[step] for step in steps(lags, segments)])


def solution(mesh):
    return jax.shard_map(
        shards,
        mesh=mesh,
        in_specs=(P("chan", "seg", "lag"), P(), P()),
        out_specs=P(("chan", "seg"), "lag"),
        check_vma=False,
    )
```

```python
import functools
import math

import jax
import jax.numpy as jnp
from jax import lax
from jax.experimental import pallas as pl
from jax.experimental.pallas import tpu as pltpu
from jax.sharding import PartitionSpec as P

LAGS = 128
SAMPLES = 2048
PHASES = 4
MOST_PERMUTES = 8


def halves(value):
    high = value.astype(jnp.bfloat16)
    low = (value - high.astype(jnp.float32)).astype(jnp.bfloat16)
    return high, low


def product(left, right):
    return jnp.dot(left, right, preferred_element_type=jnp.float32)


def product_nt(left, right):
    return lax.dot_general(
        left, right, (((1,), (1,)), ((), ())), preferred_element_type=jnp.float32
    )


def steps(lags, segments):
    return [(lag, segment) for lag in range(lags) for segment in range(segments)]


def swapped(value, lag_step, segment_step):
    lags, segments = lax.axis_size("lag"), lax.axis_size("seg")
    pairs = [
        (lag * segments + segment, (lag ^ lag_step) * segments + (segment ^ segment_step))
        for lag, segment in steps(lags, segments)
    ]
    return lax.ppermute(value, ("lag", "seg"), pairs)


def across(value, step):
    return lax.ppermute(value, "chan", [(i, i ^ step) for i in range(lax.axis_size("chan"))])


def pack_kernel(peers, base, records_ref, lists_ref, refs_ref, panel_ref, *out_refs):
    rows = records_ref.shape[0]
    refs = refs_ref.shape[1]
    share = rows // peers
    me = lax.axis_index("chan")
    own = jnp.broadcast_to(lists_ref[pl.ds(me, 1), :], (rows, rows))
    rank = jnp.sum((own.T < own).astype(jnp.int32), axis=0, keepdims=True)
    peer = lax.div(rank, share)
    if base:
        peer = lax.bitwise_xor(peer, me)
    target = peer * share + lax.rem(rank, share)
    line = lax.broadcasted_iota(jnp.int32, (rows, rows), 0)
    wanted = jnp.broadcast_to(refs_ref[...], (rows, refs)).T
    high, low = halves(records_ref[:, 0, :])
    panel_pick = (wanted == own[:refs]).astype(jnp.bfloat16)
    panel_ref[...] = product(panel_pick, high) + product(panel_pick, low)
    pick = (line == target).astype(jnp.bfloat16)
    sent = product(pick, high) + product(pick, low)
    each = rows // len(out_refs)
    for i, out_ref in enumerate(out_refs):
        out_ref[...] = sent[i * each : (i + 1) * each]


def choose_kernel(peers, base, lists_ref, pick_ref):
    rows = lists_ref.shape[1]
    share = rows // peers
    me = lax.axis_index("chan")
    lane = lax.broadcasted_iota(jnp.int32, (rows, rows), 1)
    line = lax.broadcasted_iota(jnp.int32, (rows, rows), 0)
    channel = line + me * rows
    owner = jnp.zeros((rows, 1), jnp.int32)
    for peer in range(peers):
        found = (lists_ref[pl.ds(peer, 1), :] == channel).astype(jnp.int32)
        owner = owner + jnp.sum(found, axis=1, keepdims=True) * peer
    same = lane == owner
    earlier = (lane < line).astype(jnp.bfloat16)
    before = product(earlier, same.astype(jnp.bfloat16))
    rank = jnp.sum(jnp.where(same, before, 0.0), axis=1, keepdims=True).astype(jnp.int32)
    if base:
        owner = lax.bitwise_xor(owner, me)
    pick_ref[...] = (lane == owner * share + rank).astype(jnp.bfloat16)


def place_kernel(pick_ref, panel_ref, arrived_panel_ref, *rest):
    segments = lax.axis_size("seg")
    arrived_refs, out_refs = rest[:-segments], rest[-segments:]
    kept = pick_ref.shape[0] // segments
    series = jnp.concatenate([arrived_ref[...] for arrived_ref in arrived_refs], axis=0)
    high, low = halves(series)
    series = product(pick_ref[...], high) + product(pick_ref[...], low)
    panel = panel_ref[...] + arrived_panel_ref[...]
    own = lax.axis_index("seg")
    for part in range(segments):
        half = lax.bitwise_xor(own, part)
        chosen = series[:kept]
        for other in range(1, segments):
            chosen = jnp.where(half == other, series[other * kept : (other + 1) * kept], chosen)
        out_refs[part][:kept, :] = chosen
        out_refs[part][kept:, :] = panel


def corr_kernel(refs, lag_width, *rest):
    *chunk_refs, out_ref, joined_ref = rest
    kept = out_ref.shape[0]
    lags, segments = lax.axis_size("lag"), lax.axis_size("seg")
    width = chunk_refs[0].shape[1]
    for (lag_step, segment_step), chunk_ref in zip(steps(lags, segments), chunk_refs):
        lag = lax.bitwise_xor(lax.axis_index("lag"), lag_step)
        segment = lax.bitwise_xor(lax.axis_index("seg"), segment_step)
        start = pl.multiple_of((segment * lags + lag) * width, width)
        joined_ref[:, pl.ds(start, width)] = chunk_ref[...]
    series = joined_ref[:kept, :]
    panel = joined_ref[kept:, :]
    samples = panel.shape[1]
    terms = SAMPLES - LAGS
    times = lax.broadcasted_iota(jnp.int32, panel.shape, 1)
    panel = jnp.where(times < terms, panel, 0.0)
    series = pltpu.roll(series, samples - lax.axis_index("lag") * lag_width, 1)
    shifted_panel = jnp.concatenate(
        [panel] + [pltpu.roll(panel, phase, 1) for phase in range(1, PHASES)], axis=0
    )
    panel_high, panel_low = halves(shifted_panel)
    groups = lag_width // PHASES
    shifted = jnp.concatenate(
        [series] + [pltpu.roll(series, samples - PHASES * group, 1) for group in range(1, groups)],
        axis=0,
    )
    series_high, series_low = halves(shifted)
    total = (
        product_nt(series_high, panel_high)
        + product_nt(series_low, panel_high)
        + product_nt(series_high, panel_low)
    )
    total = total * (1.0 / math.sqrt(terms))
    columns = PHASES * refs
    for group in range(groups):
        out_ref[:, group * columns : (group + 1) * columns] = total[group * kept : (group + 1) * kept]


def shards(records_owned, section_list, ref_index):
    peers = lax.axis_size("chan")
    segments = lax.axis_size("seg")
    rows, _, samples = records_owned.shape
    refs = ref_index.shape[0]
    share = rows // peers
    kept = rows // segments
    lags = lax.axis_size("lag")
    lag_width = LAGS // lags
    lists = section_list.reshape(peers, rows)
    params = pltpu.CompilerParams(vmem_limit_bytes=48 * 1024 * 1024)
    direct = peers <= MOST_PERMUTES
    buffers = peers if direct else 1
    part = jax.ShapeDtypeStruct((rows // buffers, samples), jnp.float32)
    panel, *sent = pl.pallas_call(
        functools.partial(pack_kernel, peers, direct),
        out_shape=[jax.ShapeDtypeStruct((refs, samples), jnp.float32)] + [part] * buffers,
        compiler_params=params,
        name="pack",
    )(records_owned, lists, ref_index.reshape(1, refs))
    step = peers // 2
    arrived_panel = across(panel, step)
    if direct:
        arrived = [sent[0]] + [across(sent[i], i) for i in range(1, peers)]
    else:
        blocks = sent[0].reshape(peers, share, samples)
        blocks = lax.all_to_all(blocks, "chan", split_axis=0, concat_axis=0, tiled=True)
        arrived = [blocks.reshape(rows, samples)]
    while step > 1:
        step //= 2
        panel = panel + arrived_panel
        arrived_panel = across(panel, step)
    pick = pl.pallas_call(
        functools.partial(choose_kernel, peers, direct),
        out_shape=jax.ShapeDtypeStruct((rows, rows), jnp.bfloat16),
        compiler_params=params,
        name="choose",
    )(lists)
    placed = pl.pallas_call(
        place_kernel,
        out_shape=[jax.ShapeDtypeStruct((kept + refs, samples), jnp.float32)] * segments,
        compiler_params=params,
        name="place",
    )(pick, panel, arrived_panel, *arrived)
    held = {(0, 0): placed[0]}
    for lag_step in range(0, lags, 2):
        for segment_step in range(segments):
            if lag_step or segment_step:
                held[lag_step, segment_step] = swapped(placed[segment_step], lag_step, segment_step)
    for lag_step, segment_step in list(held):
        held[lag_step + 1, segment_step] = swapped(held[lag_step, segment_step], 1, 0)
    return pl.pallas_call(
        functools.partial(corr_kernel, refs, lag_width),
        out_shape=jax.ShapeDtypeStruct((kept, lag_width * refs), jnp.float32),
        scratch_shapes=[pltpu.VMEM((kept + refs, lags * segments * samples), jnp.float32)],
        compiler_params=params,
        name="correlate",
    )(*[held[step] for step in steps(lags, segments)])


def solution(mesh):
    return jax.shard_map(
        shards,
        mesh=mesh,
        in_specs=(P("chan", "seg", "lag"), P(), P()),
        out_specs=P(("chan", "seg"), "lag"),
        check_vma=False,
    )
```

```python
import functools
import math

import jax
import jax.numpy as jnp
from jax import lax
from jax.experimental import pallas as pl
from jax.experimental.pallas import tpu as pltpu
from jax.sharding import PartitionSpec as P

LAGS = 128
SAMPLES = 2048
PHASES = 4
MOST_PERMUTES = 8


def halves(value):
    high = value.astype(jnp.bfloat16)
    low = (value - high.astype(jnp.float32)).astype(jnp.bfloat16)
    return high, low


def product(left, right):
    return jnp.dot(left, right, preferred_element_type=jnp.float32)


def product_nt(left, right):
    return lax.dot_general(
        left, right, (((1,), (1,)), ((), ())), preferred_element_type=jnp.float32
    )


def steps(lags, segments):
    return [(lag, segment) for lag in range(lags) for segment in range(segments)]


def swapped(value, lag_step, segment_step):
    lags, segments = lax.axis_size("lag"), lax.axis_size("seg")
    pairs = [
        (lag * segments + segment, (lag ^ lag_step) * segments + (segment ^ segment_step))
        for lag, segment in steps(lags, segments)
    ]
    return lax.ppermute(value, ("lag", "seg"), pairs)


def across(value, step):
    return lax.ppermute(value, "chan", [(i, i ^ step) for i in range(lax.axis_size("chan"))])


def pack_kernel(peers, base, records_ref, lists_ref, refs_ref, *out_refs):
    rows = records_ref.shape[0]
    refs = refs_ref.shape[1]
    share = rows // peers
    me = lax.axis_index("chan")
    own = jnp.broadcast_to(lists_ref[pl.ds(me, 1), :], (rows, rows))
    rank = jnp.sum((own.T < own).astype(jnp.int32), axis=0, keepdims=True)
    peer = lax.div(rank, share)
    if base:
        peer = lax.bitwise_xor(peer, me)
    target = peer * share + lax.rem(rank, share)
    line = lax.broadcasted_iota(jnp.int32, (rows, rows), 0)
    wanted = jnp.broadcast_to(refs_ref[...], (rows, refs)).T
    high, low = halves(records_ref[:, 0, :])
    panel_pick = (wanted == own[:refs]).astype(jnp.bfloat16)
    panel = product(panel_pick, high) + product(panel_pick, low)
    pick = (line == target).astype(jnp.bfloat16)
    sent = product(pick, high) + product(pick, low)
    each = rows // peers if base else rows
    for i in range(rows // each):
        out_refs[i][:each, :] = sent[i * each : (i + 1) * each]
    out_refs[1][-refs:, :] = panel


def add_kernel(panel_ref, arrived_ref, series_ref, out_ref):
    share = series_ref.shape[0]
    refs = out_ref.shape[0] - share
    out_ref[:share, :] = series_ref[...]
    out_ref[share:, :] = panel_ref[-refs:, :] + arrived_ref[-refs:, :]


def choose_kernel(peers, base, lists_ref, pick_ref):
    rows = lists_ref.shape[1]
    share = rows // peers
    me = lax.axis_index("chan")
    lane = lax.broadcasted_iota(jnp.int32, (rows, rows), 1)
    line = lax.broadcasted_iota(jnp.int32, (rows, rows), 0)
    channel = line + me * rows
    owner = jnp.zeros((rows, 1), jnp.int32)
    for peer in range(peers):
        found = (lists_ref[pl.ds(peer, 1), :] == channel).astype(jnp.int32)
        owner = owner + jnp.sum(found, axis=1, keepdims=True) * peer
    same = lane == owner
    earlier = (lane < line).astype(jnp.bfloat16)
    before = product(earlier, same.astype(jnp.bfloat16))
    rank = jnp.sum(jnp.where(same, before, 0.0), axis=1, keepdims=True).astype(jnp.int32)
    if base:
        owner = lax.bitwise_xor(owner, me)
    pick_ref[...] = (lane == owner * share + rank).astype(jnp.bfloat16)


def place_kernel(refs, pick_ref, panel_ref, arrived_panel_ref, *rest):
    segments = lax.axis_size("seg")
    arrived_refs, out_refs = rest[:-segments], rest[-segments:]
    rows = pick_ref.shape[0]
    kept = rows // segments
    share = rows // len(arrived_refs)
    series = jnp.concatenate([arrived_ref[:share, :] for arrived_ref in arrived_refs], axis=0)
    high, low = halves(series)
    series = product(pick_ref[...], high) + product(pick_ref[...], low)
    panel = panel_ref[-refs:, :] + arrived_panel_ref[-refs:, :]
    own = lax.axis_index("seg")
    for part in range(segments):
        half = lax.bitwise_xor(own, part)
        chosen = series[:kept]
        for other in range(1, segments):
            chosen = jnp.where(half == other, series[other * kept : (other + 1) * kept], chosen)
        out_refs[part][:kept, :] = chosen
        out_refs[part][kept:, :] = panel


def corr_kernel(refs, lag_width, *rest):
    *chunk_refs, out_ref, joined_ref = rest
    kept = out_ref.shape[0]
    lags, segments = lax.axis_size("lag"), lax.axis_size("seg")
    width = chunk_refs[0].shape[1]
    for (lag_step, segment_step), chunk_ref in zip(steps(lags, segments), chunk_refs):
        lag = lax.bitwise_xor(lax.axis_index("lag"), lag_step)
        segment = lax.bitwise_xor(lax.axis_index("seg"), segment_step)
        start = pl.multiple_of((segment * lags + lag) * width, width)
        joined_ref[:, pl.ds(start, width)] = chunk_ref[...]
    series = joined_ref[:kept, :]
    panel = joined_ref[kept:, :]
    samples = panel.shape[1]
    terms = SAMPLES - LAGS
    times = lax.broadcasted_iota(jnp.int32, panel.shape, 1)
    panel = jnp.where(times < terms, panel, 0.0)
    series = pltpu.roll(series, samples - lax.axis_index("lag") * lag_width, 1)
    shifted_panel = jnp.concatenate(
        [panel] + [pltpu.roll(panel, phase, 1) for phase in range(1, PHASES)], axis=0
    )
    panel_high, panel_low = halves(shifted_panel)
    groups = lag_width // PHASES
    shifted = jnp.concatenate(
        [series] + [pltpu.roll(series, samples - PHASES * group, 1) for group in range(1, groups)],
        axis=0,
    )
    series_high, series_low = halves(shifted)
    total = (
        product_nt(series_high, panel_high)
        + product_nt(series_low, panel_high)
        + product_nt(series_high, panel_low)
    )
    total = total * (1.0 / math.sqrt(terms))
    columns = PHASES * refs
    for group in range(groups):
        out_ref[:, group * columns : (group + 1) * columns] = total[group * kept : (group + 1) * kept]


def shards(records_owned, section_list, ref_index):
    peers = lax.axis_size("chan")
    segments = lax.axis_size("seg")
    rows, _, samples = records_owned.shape
    refs = ref_index.shape[0]
    share = rows // peers
    kept = rows // segments
    lags = lax.axis_size("lag")
    lag_width = LAGS // lags
    lists = section_list.reshape(peers, rows)
    params = pltpu.CompilerParams(vmem_limit_bytes=48 * 1024 * 1024)
    direct = peers <= MOST_PERMUTES

    def block(count):
        return jax.ShapeDtypeStruct((count, samples), jnp.float32)

    if direct:
        shapes = [block(share + refs if i == 1 else share) for i in range(peers)]
    else:
        shapes = [block(rows), block(refs)]
    sent = pl.pallas_call(
        functools.partial(pack_kernel, peers, direct),
        out_shape=shapes,
        compiler_params=params,
        name="pack",
    )(records_owned, lists, ref_index.reshape(1, refs))
    if not direct:
        blocks = sent[0].reshape(peers, share, samples)
        blocks = lax.all_to_all(blocks, "chan", split_axis=0, concat_axis=0, tiled=True)
        arrived = {0: blocks.reshape(rows, samples)}
    else:
        arrived = {0: sent[0]}
        arrived.update({i: across(sent[i], i) for i in range(3, peers) if i & (i - 1)})
    panel, step = sent[1], 1
    arrived_panel = across(panel, step)
    while step < peers // 2:
        if direct:
            arrived[step] = arrived_panel
        step *= 2
        if not direct:
            panel = panel + arrived_panel
        else:
            panel = pl.pallas_call(
                add_kernel,
                out_shape=block(share + refs),
                compiler_params=params,
                name="add",
            )(panel, arrived_panel, sent[step])
        arrived_panel = across(panel, step)
    if direct:
        arrived[step] = arrived_panel
    pick = pl.pallas_call(
        functools.partial(choose_kernel, peers, direct),
        out_shape=jax.ShapeDtypeStruct((rows, rows), jnp.bfloat16),
        compiler_params=params,
        name="choose",
    )(lists)
    placed = pl.pallas_call(
        functools.partial(place_kernel, refs),
        out_shape=[block(kept + refs)] * segments,
        compiler_params=params,
        name="place",
    )(pick, panel, arrived_panel, *[arrived[i] for i in sorted(arrived)])
    held = {(0, 0): placed[0]}
    for lag_step in range(0, lags, 2):
        for segment_step in range(segments):
            if lag_step or segment_step:
                held[lag_step, segment_step] = swapped(placed[segment_step], lag_step, segment_step)
    for lag_step, segment_step in list(held):
        held[lag_step + 1, segment_step] = swapped(held[lag_step, segment_step], 1, 0)
    return pl.pallas_call(
        functools.partial(corr_kernel, refs, lag_width),
        out_shape=jax.ShapeDtypeStruct((kept, lag_width * refs), jnp.float32),
        scratch_shapes=[pltpu.VMEM((kept + refs, lags * segments * samples), jnp.float32)],
        compiler_params=params,
        name="correlate",
    )(*[held[step] for step in steps(lags, segments)])


def solution(mesh):
    return jax.shard_map(
        shards,
        mesh=mesh,
        in_specs=(P("chan", "seg", "lag"), P(), P()),
        out_specs=P(("chan", "seg"), "lag"),
        check_vma=False,
    )
```

```python
import functools
import math

import jax
import jax.numpy as jnp
from jax import lax
from jax.experimental import pallas as pl
from jax.experimental.pallas import tpu as pltpu
from jax.sharding import PartitionSpec as P

LAGS = 128
SAMPLES = 2048
PHASES = 4
MOST_PERMUTES = 8


def halves(value):
    high = value.astype(jnp.bfloat16)
    low = (value - high.astype(jnp.float32)).astype(jnp.bfloat16)
    return high, low


def product(left, right):
    return jnp.dot(left, right, preferred_element_type=jnp.float32)


def product_nt(left, right):
    return lax.dot_general(
        left, right, (((1,), (1,)), ((), ())), preferred_element_type=jnp.float32
    )


def steps(lags, segments):
    return [(lag, segment) for lag in range(lags) for segment in range(segments)]


def swapped(value, lag_step, segment_step):
    lags, segments = lax.axis_size("lag"), lax.axis_size("seg")
    pairs = [
        (lag * segments + segment, (lag ^ lag_step) * segments + (segment ^ segment_step))
        for lag, segment in steps(lags, segments)
    ]
    return lax.ppermute(value, ("lag", "seg"), pairs)


def across(value, step):
    return lax.ppermute(value, "chan", [(i, i ^ step) for i in range(lax.axis_size("chan"))])


def pack_kernel(peers, base, records_ref, lists_ref, refs_ref, *out_refs):
    rows = records_ref.shape[0]
    refs = refs_ref.shape[1]
    share = rows // peers
    me = lax.axis_index("chan")
    own = jnp.broadcast_to(lists_ref[pl.ds(me, 1), :], (rows, rows))
    rank = jnp.sum((own.T < own).astype(jnp.int32), axis=0, keepdims=True)
    peer = lax.div(rank, share)
    if base:
        peer = lax.bitwise_xor(peer, me)
    target = peer * share + lax.rem(rank, share)
    line = lax.broadcasted_iota(jnp.int32, (rows, rows), 0)
    wanted = jnp.broadcast_to(refs_ref[...], (rows, refs)).T
    high, low = halves(records_ref[:, 0, :])
    panel_pick = (wanted == own[:refs]).astype(jnp.bfloat16)
    panel = product(panel_pick, high) + product(panel_pick, low)
    pick = (line == target).astype(jnp.bfloat16)
    sent = product(pick, high) + product(pick, low)
    each = rows // peers if base else rows
    for i in range(rows // each):
        out_refs[i][:each, :] = sent[i * each : (i + 1) * each]
    out_refs[1][-refs:, :] = panel


def add_kernel(panel_ref, arrived_ref, series_ref, out_ref):
    share = series_ref.shape[0]
    refs = out_ref.shape[0] - share
    out_ref[:share, :] = series_ref[...]
    out_ref[share:, :] = panel_ref[-refs:, :] + arrived_ref[-refs:, :]


def choose_kernel(peers, base, lists_ref, pick_ref):
    rows = lists_ref.shape[1]
    share = rows // peers
    me = lax.axis_index("chan")
    lane = lax.broadcasted_iota(jnp.int32, (rows, rows), 1)
    line = lax.broadcasted_iota(jnp.int32, (rows, rows), 0)
    channel = line + me * rows
    owner = jnp.zeros((rows, 1), jnp.int32)
    for peer in range(peers):
        found = (lists_ref[pl.ds(peer, 1), :] == channel).astype(jnp.int32)
        owner = owner + jnp.sum(found, axis=1, keepdims=True) * peer
    same = lane == owner
    earlier = (lane < line).astype(jnp.bfloat16)
    before = product(earlier, same.astype(jnp.bfloat16))
    rank = jnp.sum(jnp.where(same, before, 0.0), axis=1, keepdims=True).astype(jnp.int32)
    if base:
        owner = lax.bitwise_xor(owner, me)
    pick_ref[...] = (lane == owner * share + rank).astype(jnp.bfloat16)


def place_kernel(refs, pick_ref, panel_ref, arrived_panel_ref, *rest):
    segments = lax.axis_size("seg")
    arrived_refs, out_refs = rest[:-segments], rest[-segments:]
    rows = pick_ref.shape[0]
    kept = rows // segments
    share = rows // len(arrived_refs)
    series = jnp.concatenate([arrived_ref[:share, :] for arrived_ref in arrived_refs], axis=0)
    high, low = halves(series)
    series = product(pick_ref[...], high) + product(pick_ref[...], low)
    panel = panel_ref[-refs:, :] + arrived_panel_ref[-refs:, :]
    own = lax.axis_index("seg")
    for part in range(segments):
        half = lax.bitwise_xor(own, part)
        chosen = series[:kept]
        for other in range(1, segments):
            chosen = jnp.where(half == other, series[other * kept : (other + 1) * kept], chosen)
        out_refs[part][:kept, :] = chosen
        out_refs[part][kept:, :] = panel


def corr_kernel(refs, lag_width, *rest):
    *chunk_refs, out_ref, joined_ref = rest
    kept = out_ref.shape[0]
    lags, segments = lax.axis_size("lag"), lax.axis_size("seg")
    width = chunk_refs[0].shape[1]
    for (lag_step, segment_step), chunk_ref in zip(steps(lags, segments), chunk_refs):
        lag = lax.bitwise_xor(lax.axis_index("lag"), lag_step)
        segment = lax.bitwise_xor(lax.axis_index("seg"), segment_step)
        start = pl.multiple_of((segment * lags + lag) * width, width)
        joined_ref[:, pl.ds(start, width)] = chunk_ref[...]
    series = joined_ref[:kept, :]
    panel = joined_ref[kept:, :]
    samples = panel.shape[1]
    terms = SAMPLES - LAGS
    times = lax.broadcasted_iota(jnp.int32, panel.shape, 1)
    panel = jnp.where(times < terms, panel, 0.0)
    series = pltpu.roll(series, samples - lax.axis_index("lag") * lag_width, 1)
    groups = lag_width // PHASES

    def shifted(value, count, step):
        parts = [value] + [pltpu.roll(value, (i * step) % samples, 1) for i in range(1, count)]
        return jnp.concatenate(parts, axis=0)

    panel_high, panel_low = (shifted(half, PHASES, 1) for half in halves(panel))
    series_high, series_low = (shifted(half, groups, -PHASES) for half in halves(series))
    total = product_nt(
        jnp.concatenate([series_high, series_low, series_high], axis=1),
        jnp.concatenate([panel_high, panel_high, panel_low], axis=1),
    )
    total = total * (1.0 / math.sqrt(terms))
    columns = PHASES * refs
    for group in range(groups):
        out_ref[:, group * columns : (group + 1) * columns] = total[group * kept : (group + 1) * kept]


def shards(records_owned, section_list, ref_index):
    peers = lax.axis_size("chan")
    segments = lax.axis_size("seg")
    rows, _, samples = records_owned.shape
    refs = ref_index.shape[0]
    share = rows // peers
    kept = rows // segments
    lags = lax.axis_size("lag")
    lag_width = LAGS // lags
    lists = section_list.reshape(peers, rows)
    params = pltpu.CompilerParams(vmem_limit_bytes=48 * 1024 * 1024)
    direct = peers <= MOST_PERMUTES

    def block(count):
        return jax.ShapeDtypeStruct((count, samples), jnp.float32)

    if direct:
        shapes = [block(share + refs if i == 1 else share) for i in range(peers)]
    else:
        shapes = [block(rows), block(refs)]
    sent = pl.pallas_call(
        functools.partial(pack_kernel, peers, direct),
        out_shape=shapes,
        compiler_params=params,
        name="pack",
    )(records_owned, lists, ref_index.reshape(1, refs))
    if not direct:
        blocks = sent[0].reshape(peers, share, samples)
        blocks = lax.all_to_all(blocks, "chan", split_axis=0, concat_axis=0, tiled=True)
        arrived = {0: blocks.reshape(rows, samples)}
    else:
        arrived = {0: sent[0]}
        arrived.update({i: across(sent[i], i) for i in range(3, peers) if i & (i - 1)})
    panel, step = sent[1], 1
    arrived_panel = across(panel, step)
    while step < peers // 2:
        if direct:
            arrived[step] = arrived_panel
        step *= 2
        if not direct:
            panel = panel + arrived_panel
        else:
            panel = pl.pallas_call(
                add_kernel,
                out_shape=block(share + refs),
                compiler_params=params,
                name="add",
            )(panel, arrived_panel, sent[step])
        arrived_panel = across(panel, step)
    if direct:
        arrived[step] = arrived_panel
    pick = pl.pallas_call(
        functools.partial(choose_kernel, peers, direct),
        out_shape=jax.ShapeDtypeStruct((rows, rows), jnp.bfloat16),
        compiler_params=params,
        name="choose",
    )(lists)
    placed = pl.pallas_call(
        functools.partial(place_kernel, refs),
        out_shape=[block(kept + refs)] * segments,
        compiler_params=params,
        name="place",
    )(pick, panel, arrived_panel, *[arrived[i] for i in sorted(arrived)])
    held = {(0, 0): placed[0]}
    for lag_step in range(0, lags, 2):
        for segment_step in range(segments):
            if lag_step or segment_step:
                held[lag_step, segment_step] = swapped(placed[segment_step], lag_step, segment_step)
    for lag_step, segment_step in list(held):
        held[lag_step + 1, segment_step] = swapped(held[lag_step, segment_step], 1, 0)
    return pl.pallas_call(
        functools.partial(corr_kernel, refs, lag_width),
        out_shape=jax.ShapeDtypeStruct((kept, lag_width * refs), jnp.float32),
        scratch_shapes=[pltpu.VMEM((kept + refs, lags * segments * samples), jnp.float32)],
        compiler_params=params,
        name="correlate",
    )(*[held[step] for step in steps(lags, segments)])


def solution(mesh):
    return jax.shard_map(
        shards,
        mesh=mesh,
        in_specs=(P("chan", "seg", "lag"), P(), P()),
        out_specs=P(("chan", "seg"), "lag"),
        check_vma=False,
    )
```

```python
import functools
import math

import jax
import jax.numpy as jnp
from jax import lax
from jax.experimental import pallas as pl
from jax.experimental.pallas import tpu as pltpu
from jax.sharding import PartitionSpec as P

LAGS = 128
SAMPLES = 2048
PHASES = 4
MOST_PERMUTES = 8


def halves(value):
    high = value.astype(jnp.bfloat16)
    low = (value - high.astype(jnp.float32)).astype(jnp.bfloat16)
    return high, low


def product(left, right):
    return jnp.dot(left, right, preferred_element_type=jnp.float32)


def product_nt(left, right):
    return lax.dot_general(
        left, right, (((1,), (1,)), ((), ())), preferred_element_type=jnp.float32
    )


def steps(lags, segments):
    return [(lag, segment) for lag in range(lags) for segment in range(segments)]


def swapped(value, lag_step, segment_step):
    lags, segments = lax.axis_size("lag"), lax.axis_size("seg")
    pairs = [
        (lag * segments + segment, (lag ^ lag_step) * segments + (segment ^ segment_step))
        for lag, segment in steps(lags, segments)
    ]
    return lax.ppermute(value, ("lag", "seg"), pairs)


def across(value, step):
    return lax.ppermute(value, "chan", [(i, i ^ step) for i in range(lax.axis_size("chan"))])


def pack_kernel(peers, base, records_ref, lists_ref, refs_ref, *out_refs):
    rows = records_ref.shape[0]
    refs = refs_ref.shape[1]
    share = rows // peers
    me = lax.axis_index("chan")
    own = jnp.broadcast_to(lists_ref[pl.ds(me, 1), :], (rows, rows))
    rank = jnp.sum((own.T < own).astype(jnp.int32), axis=0, keepdims=True)
    peer = lax.div(rank, share)
    if base:
        peer = lax.bitwise_xor(peer, me)
    target = peer * share + lax.rem(rank, share)
    line = lax.broadcasted_iota(jnp.int32, (rows, rows), 0)
    wanted = jnp.broadcast_to(refs_ref[...], (rows, refs)).T
    high, low = halves(records_ref[:, 0, :])
    panel_pick = (wanted == own[:refs]).astype(jnp.bfloat16)
    panel = product(panel_pick, high) + product(panel_pick, low)
    pick = (line == target).astype(jnp.bfloat16)
    sent = product(pick, high) + product(pick, low)
    each = rows // peers if base else rows
    for i in range(rows // each):
        out_refs[i][:each, :] = sent[i * each : (i + 1) * each]
    out_refs[1][-refs:, :] = panel


def add_kernel(panel_ref, arrived_ref, *rest):
    rest[-1][...] = panel_ref[...] + arrived_ref[...]


def choose_kernel(peers, base, lists_ref, pick_ref):
    rows = lists_ref.shape[1]
    share = rows // peers
    me = lax.axis_index("chan")
    lane = lax.broadcasted_iota(jnp.int32, (rows, rows), 1)
    line = lax.broadcasted_iota(jnp.int32, (rows, rows), 0)
    channel = line + me * rows
    owner = jnp.zeros((rows, 1), jnp.int32)
    for peer in range(peers):
        found = (lists_ref[pl.ds(peer, 1), :] == channel).astype(jnp.int32)
        owner = owner + jnp.sum(found, axis=1, keepdims=True) * peer
    same = lane == owner
    earlier = (lane < line).astype(jnp.bfloat16)
    before = product(earlier, same.astype(jnp.bfloat16))
    rank = jnp.sum(jnp.where(same, before, 0.0), axis=1, keepdims=True).astype(jnp.int32)
    if base:
        owner = lax.bitwise_xor(owner, me)
    pick_ref[...] = (lane == owner * share + rank).astype(jnp.bfloat16)


def place_kernel(refs, pick_ref, panel_ref, arrived_panel_ref, *rest):
    segments = lax.axis_size("seg")
    arrived_refs, out_refs = rest[: -segments - 1], rest[-segments - 1 :]
    rows = pick_ref.shape[0]
    kept = rows // segments
    share = rows // len(arrived_refs)
    series = jnp.concatenate([arrived_ref[:share, :] for arrived_ref in arrived_refs], axis=0)
    high, low = halves(series)
    series = product(pick_ref[...], high) + product(pick_ref[...], low)
    own = lax.axis_index("seg")
    for part in range(segments):
        half = lax.bitwise_xor(own, part)
        chosen = series[:kept]
        for other in range(1, segments):
            chosen = jnp.where(half == other, series[other * kept : (other + 1) * kept], chosen)
        out_refs[part][...] = chosen
    out_refs[segments][...] = panel_ref[-refs:, :] + arrived_panel_ref[-refs:, :]


def join(chunk_refs, joined_ref):
    lags, segments = lax.axis_size("lag"), lax.axis_size("seg")
    width = chunk_refs[0].shape[1]
    for (lag_step, segment_step), chunk_ref in zip(steps(lags, segments), chunk_refs):
        lag = lax.bitwise_xor(lax.axis_index("lag"), lag_step)
        segment = lax.bitwise_xor(lax.axis_index("seg"), segment_step)
        start = pl.multiple_of((segment * lags + lag) * width, width)
        joined_ref[:, pl.ds(start, width)] = chunk_ref[...]


def shifted(value, count, step):
    samples = value.shape[1]
    parts = [value] + [pltpu.roll(value, (i * step) % samples, 1) for i in range(1, count)]
    return jnp.concatenate(parts, axis=0)


def shift_kernel(lag_width, *rest):
    *chunk_refs, high_ref, low_ref, joined_ref = rest
    join(chunk_refs, joined_ref)
    samples = joined_ref.shape[1]
    series = pltpu.roll(joined_ref[...], samples - lax.axis_index("lag") * lag_width, 1)
    for half, out_ref in zip(halves(series), (high_ref, low_ref)):
        out_ref[...] = shifted(half, lag_width // PHASES, -PHASES)


def corr_kernel(series_high_ref, series_low_ref, *rest):
    *chunk_refs, out_ref, joined_ref = rest
    join(chunk_refs, joined_ref)
    kept = out_ref.shape[0]
    terms = SAMPLES - LAGS
    times = lax.broadcasted_iota(jnp.int32, joined_ref.shape, 1)
    panel = jnp.where(times < terms, joined_ref[...], 0.0)
    panel_high, panel_low = (shifted(half, PHASES, 1) for half in halves(panel))
    series_high, series_low = series_high_ref[...], series_low_ref[...]
    total = product_nt(
        jnp.concatenate([series_high, series_low, series_high], axis=1),
        jnp.concatenate([panel_high, panel_high, panel_low], axis=1),
    )
    total = total * (1.0 / math.sqrt(terms))
    columns = panel_high.shape[0]
    for group in range(total.shape[0] // kept):
        out_ref[:, group * columns : (group + 1) * columns] = total[
            group * kept : (group + 1) * kept
        ]


def shards(records_owned, section_list, ref_index):
    peers = lax.axis_size("chan")
    segments = lax.axis_size("seg")
    rows, _, samples = records_owned.shape
    refs = ref_index.shape[0]
    share = rows // peers
    kept = rows // segments
    lags = lax.axis_size("lag")
    lag_width = LAGS // lags
    lists = section_list.reshape(peers, rows)
    params = pltpu.CompilerParams(vmem_limit_bytes=48 * 1024 * 1024)
    direct = peers <= MOST_PERMUTES

    def block(count):
        return jax.ShapeDtypeStruct((count, samples), jnp.float32)

    if direct:
        shapes = [block(share + refs if i == 1 else share) for i in range(peers)]
    else:
        shapes = [block(rows), block(refs)]
    sent = pl.pallas_call(
        functools.partial(pack_kernel, peers, direct),
        out_shape=shapes,
        compiler_params=params,
        name="pack",
    )(records_owned, lists, ref_index.reshape(1, refs))
    first = across(sent[1], 1)
    if direct:
        arrived = [sent[0], first] + [across(sent[i], i) for i in range(2, peers)]
    else:
        blocks = sent[0].reshape(peers, share, samples)
        blocks = lax.all_to_all(blocks, "chan", split_axis=0, concat_axis=0, tiled=True)
        arrived = [blocks.reshape(rows, samples)]
    pick = pl.pallas_call(
        functools.partial(choose_kernel, peers, direct),
        out_shape=jax.ShapeDtypeStruct((rows, rows), jnp.bfloat16),
        compiler_params=params,
        name="choose",
    )(lists)
    *placed, panel = pl.pallas_call(
        functools.partial(place_kernel, refs),
        out_shape=[block(kept)] * segments + [block(refs)],
        compiler_params=params,
        name="place",
    )(pick, sent[1], first, *arrived)

    def over_chips(parts):
        held = {(0, 0): parts[0]}
        for lag_step in range(0, lags, 2):
            for segment_step in range(segments):
                if lag_step or segment_step:
                    held[lag_step, segment_step] = swapped(parts[segment_step], lag_step, segment_step)
        return held

    def over_cores(held):
        for lag_step, segment_step in list(held):
            held[lag_step + 1, segment_step] = swapped(held[lag_step, segment_step], 1, 0)
        return [held[step] for step in steps(lags, segments)]

    series = over_chips(placed)
    step = 1
    while step < peers // 2:
        step *= 2
        ties = [series[i] for i in series if i != (0, 0)] if step == peers // 2 else []
        whole = pl.BlockSpec(memory_space=pltpu.VMEM)
        panel = pl.pallas_call(
            add_kernel,
            out_shape=block(refs),
            in_specs=[whole] * 2 + [pl.BlockSpec(memory_space=pl.ANY)] * len(ties),
            compiler_params=params,
            name="add",
        )(panel, across(panel, step), *ties)
    panels = over_cores(over_chips([panel] * segments))
    length = lags * segments * samples
    part = jax.ShapeDtypeStruct((lag_width // PHASES * kept, length), jnp.bfloat16)
    series_parts = pl.pallas_call(
        functools.partial(shift_kernel, lag_width),
        out_shape=[part, part],
        scratch_shapes=[pltpu.VMEM((kept, length), jnp.float32)],
        compiler_params=params,
        name="shift",
    )(*over_cores(series))
    return pl.pallas_call(
        corr_kernel,
        out_shape=jax.ShapeDtypeStruct((kept, lag_width * refs), jnp.float32),
        scratch_shapes=[pltpu.VMEM((refs, length), jnp.float32)],
        compiler_params=params,
        name="correlate",
    )(*series_parts, *panels)


def solution(mesh):
    return jax.shard_map(
        shards,
        mesh=mesh,
        in_specs=(P("chan", "seg", "lag"), P(), P()),
        out_specs=P(("chan", "seg"), "lag"),
        check_vma=False,
    )
```

```python
import functools
import math

import jax
import jax.numpy as jnp
from jax import lax
from jax.experimental import pallas as pl
from jax.experimental.pallas import tpu as pltpu
from jax.sharding import PartitionSpec as P

LAGS = 128
SAMPLES = 2048
PHASES = 4


def halves(value):
    high = value.astype(jnp.bfloat16)
    low = (value - high.astype(jnp.float32)).astype(jnp.bfloat16)
    return high, low


def product(left, right):
    return jnp.dot(left, right, preferred_element_type=jnp.float32)


def product_nt(left, right):
    return lax.dot_general(
        left, right, (((1,), (1,)), ((), ())), preferred_element_type=jnp.float32
    )


def steps(lags, segments):
    return [(lag, segment) for lag in range(lags) for segment in range(segments)]


def swapped(value, lag_step, segment_step):
    lags, segments = lax.axis_size("lag"), lax.axis_size("seg")
    pairs = [
        (lag * segments + segment, (lag ^ lag_step) * segments + (segment ^ segment_step))
        for lag, segment in steps(lags, segments)
    ]
    return lax.ppermute(value, ("lag", "seg"), pairs)


def across(value, step):
    return lax.ppermute(value, "chan", [(i, i ^ step) for i in range(lax.axis_size("chan"))])


def paired(value, order):
    lags = lax.axis_size("lag")
    pairs = [
        (chan * lags + lag, (chan ^ order[lag % 2]) * lags + lag)
        for chan in range(lax.axis_size("chan"))
        for lag in range(lags)
    ]
    return lax.ppermute(value, ("chan", "lag"), pairs)


def choice(pick, rows):
    high, low = halves(rows)
    return product(pick, high) + product(pick, low)


def counts_before(present):
    rows = present.shape[0]
    line = lax.broadcasted_iota(jnp.int32, (rows, rows), 0)
    lane = lax.broadcasted_iota(jnp.int32, (rows, rows), 1)
    return product((lane < line).astype(jnp.bfloat16), present.astype(jnp.bfloat16))


def columns(refs_ref, width):
    return jnp.broadcast_to(refs_ref[...], (width, refs_ref.shape[1])).T


def choose_four_kernel(lists_ref, refs_ref, send_ref, keep_ref, take_ref):
    rows = lists_ref.shape[1]
    kept = take_ref.shape[1]
    refs = refs_ref.shape[1]
    me = lax.axis_index("chan")
    odd = lax.rem(lax.axis_index("lag"), 2)
    near, far = 1 + odd, 2 - odd
    line = lax.broadcasted_iota(jnp.int32, (rows, 2 * rows), 0)

    def pool(owner):
        lists = [lists_ref[pl.ds(lax.bitwise_xor(owner, i), 1), :] for i in (0, near)]
        return jnp.concatenate(lists, axis=1)

    def where(owner, block):
        return pool(owner) == line + block * rows

    def ranks(found):
        present = jnp.max(found.astype(jnp.float32), axis=1, keepdims=True)
        return present, counts_before(jnp.broadcast_to(present, (rows, rows)))

    other = lax.bitwise_xor(me, far)
    found = where(me, other)
    _, rank = ranks(found)
    rank = jnp.concatenate([rank, rank], axis=1)
    slot = jnp.sum(jnp.where(found, rank + 1.0, 0.0), axis=0, keepdims=True).astype(jnp.int32)
    send_ref[:kept, :] = (line[:kept] + 1 == slot).astype(jnp.bfloat16)
    send_ref[kept:, :] = (columns(refs_ref, 2 * rows) == pool(me)).astype(jnp.bfloat16)
    keep_ref[...] = where(me, me).astype(jnp.bfloat16)
    present, rank = ranks(where(other, me))
    lane = lax.broadcasted_iota(jnp.int32, (rows, kept), 1)
    slot = jnp.where(present > 0.0, rank[:, :kept], -1.0).astype(jnp.int32)
    take_ref[...] = (lane == slot).astype(jnp.bfloat16)


def pick_kernel(records_ref, arrived_ref, send_ref, keep_ref, sent_ref, base_ref):
    rows = jnp.concatenate([records_ref[:, 0, :], arrived_ref[:, 0, :]], axis=0)
    high, low = halves(rows)
    sent_ref[...] = product(send_ref[...], high) + product(send_ref[...], low)
    base_ref[...] = product(keep_ref[...], high) + product(keep_ref[...], low)


def put(series, panel, out_refs):
    segments = len(out_refs)
    kept = series.shape[0] // segments
    own = lax.axis_index("seg")
    for part in range(segments):
        half = lax.bitwise_xor(own, part)
        chosen = series[:kept]
        for other in range(1, segments):
            chosen = jnp.where(half == other, series[other * kept : (other + 1) * kept], chosen)
        out_refs[part][:kept, :] = chosen
        out_refs[part][kept:, :] = panel


def place_four_kernel(base_ref, take_ref, sent_ref, arrived_ref, *out_refs):
    kept = take_ref.shape[1]
    series = base_ref[...] + choice(take_ref[...], arrived_ref[:kept, :])
    put(series, sent_ref[kept:, :] + arrived_ref[kept:, :], out_refs)


def pack_kernel(records_ref, lists_ref, refs_ref, out_ref, panel_ref):
    rows = records_ref.shape[0]
    refs = refs_ref.shape[1]
    own = jnp.broadcast_to(lists_ref[pl.ds(lax.axis_index("chan"), 1), :], (rows, rows))
    rank = jnp.sum((own.T < own).astype(jnp.int32), axis=0, keepdims=True)
    line = lax.broadcasted_iota(jnp.int32, (rows, rows), 0)
    records = records_ref[:, 0, :]
    panel_ref[...] = choice((columns(refs_ref, rows) == own[:refs]).astype(jnp.bfloat16), records)
    out_ref[...] = choice((line == rank).astype(jnp.bfloat16), records)


def choose_kernel(peers, lists_ref, pick_ref):
    rows = lists_ref.shape[1]
    share = rows // peers
    lane = lax.broadcasted_iota(jnp.int32, (rows, rows), 1)
    channel = lax.broadcasted_iota(jnp.int32, (rows, rows), 0) + lax.axis_index("chan") * rows
    owner = jnp.zeros((rows, 1), jnp.int32)
    for peer in range(peers):
        found = (lists_ref[pl.ds(peer, 1), :] == channel).astype(jnp.int32)
        owner = owner + jnp.sum(found, axis=1, keepdims=True) * peer
    same = lane == owner
    before = counts_before(same.astype(jnp.float32))
    rank = jnp.sum(jnp.where(same, before, 0.0), axis=1, keepdims=True).astype(jnp.int32)
    pick_ref[...] = (lane == owner * share + rank).astype(jnp.bfloat16)


def place_kernel(pick_ref, panel_ref, arrived_ref, *out_refs):
    put(choice(pick_ref[...], arrived_ref[...]), panel_ref[...], out_refs)


def corr_kernel(refs, lag_width, *rest):
    *chunk_refs, out_ref, joined_ref = rest
    kept = out_ref.shape[0]
    lags, segments = lax.axis_size("lag"), lax.axis_size("seg")
    width = chunk_refs[0].shape[1]
    for (lag_step, segment_step), chunk_ref in zip(steps(lags, segments), chunk_refs):
        lag = lax.bitwise_xor(lax.axis_index("lag"), lag_step)
        segment = lax.bitwise_xor(lax.axis_index("seg"), segment_step)
        start = pl.multiple_of((segment * lags + lag) * width, width)
        joined_ref[:, pl.ds(start, width)] = chunk_ref[...]
    series = joined_ref[:kept, :]
    panel = joined_ref[kept:, :]
    samples = panel.shape[1]
    terms = SAMPLES - LAGS
    times = lax.broadcasted_iota(jnp.int32, panel.shape, 1)
    panel = jnp.where(times < terms, panel, 0.0)
    series = pltpu.roll(series, samples - lax.axis_index("lag") * lag_width, 1)
    groups = lag_width // PHASES

    def shifted(value, count, step):
        parts = [value] + [pltpu.roll(value, (i * step) % samples, 1) for i in range(1, count)]
        return jnp.concatenate(parts, axis=0)

    panel_high, panel_low = (shifted(half, PHASES, 1) for half in halves(panel))
    series_high, series_low = (shifted(half, groups, -PHASES) for half in halves(series))
    total = product_nt(
        jnp.concatenate([series_high, series_low, series_high], axis=1),
        jnp.concatenate([panel_high, panel_high, panel_low], axis=1),
    )
    total = total * (1.0 / math.sqrt(terms))
    columns = PHASES * refs
    for group in range(groups):
        out_ref[:, group * columns : (group + 1) * columns] = total[group * kept : (group + 1) * kept]


def shards(records_owned, section_list, ref_index):
    peers = lax.axis_size("chan")
    segments = lax.axis_size("seg")
    rows, _, samples = records_owned.shape
    refs = ref_index.shape[0]
    share = rows // peers
    kept = rows // segments
    lags = lax.axis_size("lag")
    lag_width = LAGS // lags
    lists = section_list.reshape(peers, rows)
    params = pltpu.CompilerParams(vmem_limit_bytes=48 * 1024 * 1024)
    wanted = ref_index.reshape(1, refs)

    def block(*shape, dtype=jnp.float32):
        return jax.ShapeDtypeStruct(shape, dtype)

    def call(kernel, name, shapes, *operands):
        return pl.pallas_call(kernel, out_shape=shapes, compiler_params=params, name=name)(*operands)

    shapes = [block(kept + refs, samples)] * segments
    if peers == 4:
        first = paired(records_owned, (1, 2))
        half = rows // 2
        send, keep, take = call(
            choose_four_kernel,
            "choose",
            [
                block(half + refs, 2 * rows, dtype=jnp.bfloat16),
                block(rows, 2 * rows, dtype=jnp.bfloat16),
                block(rows, half, dtype=jnp.bfloat16),
            ],
            lists,
            wanted,
        )
        sent, base = call(
            pick_kernel,
            "pick",
            [block(half + refs, samples), block(rows, samples)],
            records_owned,
            first,
            send,
            keep,
        )
        placed = call(place_four_kernel, "place", shapes, base, take, sent, paired(sent, (2, 1)))
    else:
        packed, panel = call(
            pack_kernel,
            "pack",
            [block(rows, samples), block(refs, samples)],
            records_owned,
            lists,
            wanted,
        )
        blocks = packed.reshape(peers, share, samples)
        blocks = lax.all_to_all(blocks, "chan", split_axis=0, concat_axis=0, tiled=True)
        step = 1
        while step < peers:
            panel = panel + across(panel, step)
            step *= 2
        pick = call(
            functools.partial(choose_kernel, peers),
            "choose",
            block(rows, rows, dtype=jnp.bfloat16),
            lists,
        )
        placed = call(place_kernel, "place", shapes, pick, panel, blocks.reshape(rows, samples))
    held = {(0, 0): placed[0]}
    for lag_step in range(0, lags, 2):
        for segment_step in range(segments):
            if lag_step or segment_step:
                held[lag_step, segment_step] = swapped(placed[segment_step], lag_step, segment_step)
    for lag_step, segment_step in list(held):
        held[lag_step + 1, segment_step] = swapped(held[lag_step, segment_step], 1, 0)
    return pl.pallas_call(
        functools.partial(corr_kernel, refs, lag_width),
        out_shape=jax.ShapeDtypeStruct((kept, lag_width * refs), jnp.float32),
        scratch_shapes=[pltpu.VMEM((kept + refs, lags * segments * samples), jnp.float32)],
        compiler_params=params,
        name="correlate",
    )(*[held[step] for step in steps(lags, segments)])


def solution(mesh):
    return jax.shard_map(
        shards,
        mesh=mesh,
        in_specs=(P("chan", "seg", "lag"), P(), P()),
        out_specs=P(("chan", "seg"), "lag"),
        check_vma=False,
    )
```

```python
import functools
import math

import jax
import jax.numpy as jnp
from jax import lax
from jax.experimental import pallas as pl
from jax.experimental.pallas import tpu as pltpu
from jax.sharding import PartitionSpec as P

LAGS = 128
SAMPLES = 2048
PHASES = 4


def halves(value):
    high = value.astype(jnp.bfloat16)
    low = (value - high.astype(jnp.float32)).astype(jnp.bfloat16)
    return high, low


def product(left, right):
    return jnp.dot(left, right, preferred_element_type=jnp.float32)


def product_nt(left, right):
    return lax.dot_general(
        left, right, (((1,), (1,)), ((), ())), preferred_element_type=jnp.float32
    )


def steps(lags, segments):
    return [(lag, segment) for lag in range(lags) for segment in range(segments)]


def swapped(value, lag_step, segment_step):
    lags, segments = lax.axis_size("lag"), lax.axis_size("seg")
    pairs = [
        (lag * segments + segment, (lag ^ lag_step) * segments + (segment ^ segment_step))
        for lag, segment in steps(lags, segments)
    ]
    return lax.ppermute(value, ("lag", "seg"), pairs)


def across(value, step):
    return lax.ppermute(value, "chan", [(i, i ^ step) for i in range(lax.axis_size("chan"))])


def paired(value, order):
    lags = lax.axis_size("lag")
    pairs = [
        (chan * lags + lag, (chan ^ order[lag % 2]) * lags + lag)
        for chan in range(lax.axis_size("chan"))
        for lag in range(lags)
    ]
    return lax.ppermute(value, ("chan", "lag"), pairs)


def choice(pick, rows):
    high, low = halves(rows)
    return product(pick, high) + product(pick, low)


def counts_before(present):
    rows = present.shape[0]
    line = lax.broadcasted_iota(jnp.int32, (rows, rows), 0)
    lane = lax.broadcasted_iota(jnp.int32, (rows, rows), 1)
    return product((lane < line).astype(jnp.bfloat16), present.astype(jnp.bfloat16))


def columns(refs_ref, width):
    return jnp.broadcast_to(refs_ref[...], (width, refs_ref.shape[1])).T


def choose_four_kernel(lists_ref, refs_ref, send_ref, keep_ref, take_ref):
    rows = lists_ref.shape[1]
    kept = take_ref.shape[1]
    refs = refs_ref.shape[1]
    me = lax.axis_index("chan")
    odd = lax.rem(lax.axis_index("lag"), 2)
    near, far = 1 + odd, 2 - odd
    line = lax.broadcasted_iota(jnp.int32, (rows, 2 * rows), 0)

    def pool(owner):
        lists = [lists_ref[pl.ds(lax.bitwise_xor(owner, i), 1), :] for i in (0, near)]
        return jnp.concatenate(lists, axis=1)

    def where(owner, block):
        return pool(owner) == line + block * rows

    def ranks(found):
        present = jnp.max(found.astype(jnp.float32), axis=1, keepdims=True)
        return present, counts_before(jnp.broadcast_to(present, (rows, rows)))

    other = lax.bitwise_xor(me, far)
    found = where(me, other)
    _, rank = ranks(found)
    rank = jnp.concatenate([rank, rank], axis=1)
    slot = jnp.sum(jnp.where(found, rank + 1.0, 0.0), axis=0, keepdims=True).astype(jnp.int32)
    send_ref[:kept, :] = (line[:kept] + 1 == slot).astype(jnp.bfloat16)
    send_ref[kept:, :] = (columns(refs_ref, 2 * rows) == pool(me)).astype(jnp.bfloat16)
    keep_ref[...] = where(me, me).astype(jnp.bfloat16)
    present, rank = ranks(where(other, me))
    lane = lax.broadcasted_iota(jnp.int32, (rows, kept), 1)
    slot = jnp.where(present > 0.0, rank[:, :kept], -1.0).astype(jnp.int32)
    take_ref[...] = (lane == slot).astype(jnp.bfloat16)


def load_kernel(records_ref, out_ref):
    out_ref[...] = records_ref[:, 0, :]


def pick_kernel(records_ref, arrived_ref, send_ref, keep_ref, sent_ref, base_ref):
    rows = jnp.concatenate([records_ref[...], arrived_ref[...]], axis=0)
    high, low = halves(rows)
    sent_ref[...] = product(send_ref[...], high) + product(send_ref[...], low)
    base_ref[...] = product(keep_ref[...], high) + product(keep_ref[...], low)


def put(series, panel, out_refs):
    segments = len(out_refs)
    kept = series.shape[0] // segments
    own = lax.axis_index("seg")
    for part in range(segments):
        half = lax.bitwise_xor(own, part)
        chosen = series[:kept]
        for other in range(1, segments):
            chosen = jnp.where(half == other, series[other * kept : (other + 1) * kept], chosen)
        out_refs[part][:kept, :] = chosen
        out_refs[part][kept:, :] = panel


def place_four_kernel(base_ref, take_ref, sent_ref, arrived_ref, *out_refs):
    kept = take_ref.shape[1]
    series = base_ref[...] + choice(take_ref[...], arrived_ref[:kept, :])
    put(series, sent_ref[kept:, :] + arrived_ref[kept:, :], out_refs)


def pack_kernel(records_ref, lists_ref, refs_ref, out_ref, panel_ref):
    rows = records_ref.shape[0]
    refs = refs_ref.shape[1]
    own = jnp.broadcast_to(lists_ref[pl.ds(lax.axis_index("chan"), 1), :], (rows, rows))
    rank = jnp.sum((own.T < own).astype(jnp.int32), axis=0, keepdims=True)
    line = lax.broadcasted_iota(jnp.int32, (rows, rows), 0)
    records = records_ref[:, 0, :]
    panel_ref[...] = choice((columns(refs_ref, rows) == own[:refs]).astype(jnp.bfloat16), records)
    out_ref[...] = choice((line == rank).astype(jnp.bfloat16), records)


def choose_kernel(peers, lists_ref, pick_ref):
    rows = lists_ref.shape[1]
    share = rows // peers
    lane = lax.broadcasted_iota(jnp.int32, (rows, rows), 1)
    channel = lax.broadcasted_iota(jnp.int32, (rows, rows), 0) + lax.axis_index("chan") * rows
    owner = jnp.zeros((rows, 1), jnp.int32)
    for peer in range(peers):
        found = (lists_ref[pl.ds(peer, 1), :] == channel).astype(jnp.int32)
        owner = owner + jnp.sum(found, axis=1, keepdims=True) * peer
    same = lane == owner
    before = counts_before(same.astype(jnp.float32))
    rank = jnp.sum(jnp.where(same, before, 0.0), axis=1, keepdims=True).astype(jnp.int32)
    pick_ref[...] = (lane == owner * share + rank).astype(jnp.bfloat16)


def place_kernel(pick_ref, panel_ref, arrived_ref, *out_refs):
    put(choice(pick_ref[...], arrived_ref[...]), panel_ref[...], out_refs)


def corr_kernel(refs, lag_width, *rest):
    *chunk_refs, out_ref, joined_ref = rest
    kept = out_ref.shape[0]
    lags, segments = lax.axis_size("lag"), lax.axis_size("seg")
    width = chunk_refs[0].shape[1]
    for (lag_step, segment_step), chunk_ref in zip(steps(lags, segments), chunk_refs):
        lag = lax.bitwise_xor(lax.axis_index("lag"), lag_step)
        segment = lax.bitwise_xor(lax.axis_index("seg"), segment_step)
        start = pl.multiple_of((segment * lags + lag) * width, width)
        joined_ref[:, pl.ds(start, width)] = chunk_ref[...]
    series = joined_ref[:kept, :]
    panel = joined_ref[kept:, :]
    samples = panel.shape[1]
    terms = SAMPLES - LAGS
    times = lax.broadcasted_iota(jnp.int32, panel.shape, 1)
    panel = jnp.where(times < terms, panel, 0.0)
    series = pltpu.roll(series, samples - lax.axis_index("lag") * lag_width, 1)
    groups = lag_width // PHASES

    def shifted(value, count, step):
        parts = [value] + [pltpu.roll(value, (i * step) % samples, 1) for i in range(1, count)]
        return jnp.concatenate(parts, axis=0)

    panel_high, panel_low = (shifted(half, PHASES, 1) for half in halves(panel))
    series_high, series_low = (shifted(half, groups, -PHASES) for half in halves(series))
    total = product_nt(
        jnp.concatenate([series_high, series_low, series_high], axis=1),
        jnp.concatenate([panel_high, panel_high, panel_low], axis=1),
    )
    total = total * (1.0 / math.sqrt(terms))
    columns = PHASES * refs
    for group in range(groups):
        out_ref[:, group * columns : (group + 1) * columns] = total[group * kept : (group + 1) * kept]


def shards(records_owned, section_list, ref_index):
    peers = lax.axis_size("chan")
    segments = lax.axis_size("seg")
    rows, _, samples = records_owned.shape
    refs = ref_index.shape[0]
    share = rows // peers
    kept = rows // segments
    lags = lax.axis_size("lag")
    lag_width = LAGS // lags
    lists = section_list.reshape(peers, rows)
    params = pltpu.CompilerParams(vmem_limit_bytes=48 * 1024 * 1024)
    wanted = ref_index.reshape(1, refs)

    def block(*shape, dtype=jnp.float32):
        return jax.ShapeDtypeStruct(shape, dtype)

    def call(kernel, name, shapes, *operands):
        return pl.pallas_call(kernel, out_shape=shapes, compiler_params=params, name=name)(*operands)

    shapes = [block(kept + refs, samples)] * segments
    if peers == 4:
        records = call(load_kernel, "load", block(rows, samples), records_owned)
        first = paired(records, (1, 2))
        half = rows // 2
        send, keep, take = call(
            choose_four_kernel,
            "choose",
            [
                block(half + refs, 2 * rows, dtype=jnp.bfloat16),
                block(rows, 2 * rows, dtype=jnp.bfloat16),
                block(rows, half, dtype=jnp.bfloat16),
            ],
            lists,
            wanted,
        )
        sent, base = call(
            pick_kernel,
            "pick",
            [block(half + refs, samples), block(rows, samples)],
            records,
            first,
            send,
            keep,
        )
        placed = call(place_four_kernel, "place", shapes, base, take, sent, paired(sent, (2, 1)))
    else:
        packed, panel = call(
            pack_kernel,
            "pack",
            [block(rows, samples), block(refs, samples)],
            records_owned,
            lists,
            wanted,
        )
        blocks = packed.reshape(peers, share, samples)
        blocks = lax.all_to_all(blocks, "chan", split_axis=0, concat_axis=0, tiled=True)
        step = 1
        while step < peers:
            panel = panel + across(panel, step)
            step *= 2
        pick = call(
            functools.partial(choose_kernel, peers),
            "choose",
            block(rows, rows, dtype=jnp.bfloat16),
            lists,
        )
        placed = call(place_kernel, "place", shapes, pick, panel, blocks.reshape(rows, samples))
    held = {(0, 0): placed[0]}
    for lag_step in range(0, lags, 2):
        for segment_step in range(segments):
            if lag_step or segment_step:
                held[lag_step, segment_step] = swapped(placed[segment_step], lag_step, segment_step)
    for lag_step, segment_step in list(held):
        held[lag_step + 1, segment_step] = swapped(held[lag_step, segment_step], 1, 0)
    return pl.pallas_call(
        functools.partial(corr_kernel, refs, lag_width),
        out_shape=jax.ShapeDtypeStruct((kept, lag_width * refs), jnp.float32),
        scratch_shapes=[pltpu.VMEM((kept + refs, lags * segments * samples), jnp.float32)],
        compiler_params=params,
        name="correlate",
    )(*[held[step] for step in steps(lags, segments)])


def solution(mesh):
    return jax.shard_map(
        shards,
        mesh=mesh,
        in_specs=(P("chan", "seg", "lag"), P(), P()),
        out_specs=P(("chan", "seg"), "lag"),
        check_vma=False,
    )
```

```python
import functools
import math

import jax
import jax.numpy as jnp
from jax import lax
from jax.experimental import pallas as pl
from jax.experimental.pallas import tpu as pltpu
from jax.sharding import PartitionSpec as P

LAGS = 128
SAMPLES = 2048
PHASES = 4


def halves(value):
    high = value.astype(jnp.bfloat16)
    low = (value - high.astype(jnp.float32)).astype(jnp.bfloat16)
    return high, low


def product(left, right):
    return jnp.dot(left, right, preferred_element_type=jnp.float32)


def product_nt(left, right):
    return lax.dot_general(
        left, right, (((1,), (1,)), ((), ())), preferred_element_type=jnp.float32
    )


def steps(lags, segments):
    return [(lag, segment) for lag in range(lags) for segment in range(segments)]


def swapped(value, lag_step, segment_step):
    lags, segments = lax.axis_size("lag"), lax.axis_size("seg")
    pairs = [
        (lag * segments + segment, (lag ^ lag_step) * segments + (segment ^ segment_step))
        for lag, segment in steps(lags, segments)
    ]
    return lax.ppermute(value, ("lag", "seg"), pairs)


def across(value, step):
    return lax.ppermute(value, "chan", [(i, i ^ step) for i in range(lax.axis_size("chan"))])


def paired(value, order):
    lags = lax.axis_size("lag")
    pairs = [
        (chan * lags + lag, (chan ^ order[lag % 2]) * lags + lag)
        for chan in range(lax.axis_size("chan"))
        for lag in range(lags)
    ]
    return lax.ppermute(value, ("chan", "lag"), pairs)


def choice(pick, rows):
    high, low = halves(rows)
    return product(pick, high) + product(pick, low)


def counts_before(present):
    rows = present.shape[0]
    line = lax.broadcasted_iota(jnp.int32, (rows, rows), 0)
    lane = lax.broadcasted_iota(jnp.int32, (rows, rows), 1)
    return product((lane < line).astype(jnp.bfloat16), present.astype(jnp.bfloat16))


def columns(refs_ref, width):
    return jnp.broadcast_to(refs_ref[...], (width, refs_ref.shape[1])).T


def choose_four_kernel(lists_ref, refs_ref, send_ref, keep_ref, take_ref):
    rows = lists_ref.shape[1]
    kept = take_ref.shape[1]
    refs = refs_ref.shape[1]
    me = lax.axis_index("chan")
    odd = lax.rem(lax.axis_index("lag"), 2)
    near, far = 1 + odd, 2 - odd
    line = lax.broadcasted_iota(jnp.int32, (rows, 2 * rows), 0)

    def pool(owner):
        lists = [lists_ref[pl.ds(lax.bitwise_xor(owner, i), 1), :] for i in (0, near)]
        return jnp.concatenate(lists, axis=1)

    def where(owner, block):
        return pool(owner) == line + block * rows

    def ranks(found):
        present = jnp.max(found.astype(jnp.float32), axis=1, keepdims=True)
        return present, counts_before(jnp.broadcast_to(present, (rows, rows)))

    other = lax.bitwise_xor(me, far)
    found = where(me, other)
    _, rank = ranks(found)
    rank = jnp.concatenate([rank, rank], axis=1)
    slot = jnp.sum(jnp.where(found, rank + 1.0, 0.0), axis=0, keepdims=True).astype(jnp.int32)
    send_ref[:kept, :] = (line[:kept] + 1 == slot).astype(jnp.bfloat16)
    send_ref[kept:, :] = (columns(refs_ref, 2 * rows) == pool(me)).astype(jnp.bfloat16)
    keep_ref[...] = where(me, me).astype(jnp.bfloat16)
    present, rank = ranks(where(other, me))
    lane = lax.broadcasted_iota(jnp.int32, (rows, kept), 1)
    slot = jnp.where(present > 0.0, rank[:, :kept], -1.0).astype(jnp.int32)
    take_ref[...] = (lane == slot).astype(jnp.bfloat16)


def load_kernel(records_ref, out_ref, done):
    copy = pltpu.make_async_copy(records_ref, out_ref, done)
    copy.start()
    copy.wait()


def pick_kernel(records_ref, arrived_ref, send_ref, keep_ref, sent_ref, base_ref):
    rows = jnp.concatenate([records_ref[:, 0, :], arrived_ref[:, 0, :]], axis=0)
    high, low = halves(rows)
    sent_ref[...] = product(send_ref[...], high) + product(send_ref[...], low)
    base_ref[...] = product(keep_ref[...], high) + product(keep_ref[...], low)


def put(series, panel, out_refs):
    segments = len(out_refs)
    kept = series.shape[0] // segments
    own = lax.axis_index("seg")
    for part in range(segments):
        half = lax.bitwise_xor(own, part)
        chosen = series[:kept]
        for other in range(1, segments):
            chosen = jnp.where(half == other, series[other * kept : (other + 1) * kept], chosen)
        out_refs[part][:kept, :] = chosen
        out_refs[part][kept:, :] = panel


def place_four_kernel(base_ref, take_ref, sent_ref, arrived_ref, *out_refs):
    kept = take_ref.shape[1]
    series = base_ref[...] + choice(take_ref[...], arrived_ref[:kept, :])
    put(series, sent_ref[kept:, :] + arrived_ref[kept:, :], out_refs)


def pack_kernel(records_ref, lists_ref, refs_ref, out_ref, panel_ref):
    rows = records_ref.shape[0]
    refs = refs_ref.shape[1]
    own = jnp.broadcast_to(lists_ref[pl.ds(lax.axis_index("chan"), 1), :], (rows, rows))
    rank = jnp.sum((own.T < own).astype(jnp.int32), axis=0, keepdims=True)
    line = lax.broadcasted_iota(jnp.int32, (rows, rows), 0)
    records = records_ref[:, 0, :]
    panel_ref[...] = choice((columns(refs_ref, rows) == own[:refs]).astype(jnp.bfloat16), records)
    out_ref[...] = choice((line == rank).astype(jnp.bfloat16), records)


def choose_kernel(peers, lists_ref, pick_ref):
    rows = lists_ref.shape[1]
    share = rows // peers
    lane = lax.broadcasted_iota(jnp.int32, (rows, rows), 1)
    channel = lax.broadcasted_iota(jnp.int32, (rows, rows), 0) + lax.axis_index("chan") * rows
    owner = jnp.zeros((rows, 1), jnp.int32)
    for peer in range(peers):
        found = (lists_ref[pl.ds(peer, 1), :] == channel).astype(jnp.int32)
        owner = owner + jnp.sum(found, axis=1, keepdims=True) * peer
    same = lane == owner
    before = counts_before(same.astype(jnp.float32))
    rank = jnp.sum(jnp.where(same, before, 0.0), axis=1, keepdims=True).astype(jnp.int32)
    pick_ref[...] = (lane == owner * share + rank).astype(jnp.bfloat16)


def place_kernel(pick_ref, panel_ref, arrived_ref, *out_refs):
    put(choice(pick_ref[...], arrived_ref[...]), panel_ref[...], out_refs)


def corr_kernel(refs, lag_width, *rest):
    *chunk_refs, out_ref, joined_ref = rest
    kept = out_ref.shape[0]
    lags, segments = lax.axis_size("lag"), lax.axis_size("seg")
    width = chunk_refs[0].shape[1]
    for (lag_step, segment_step), chunk_ref in zip(steps(lags, segments), chunk_refs):
        lag = lax.bitwise_xor(lax.axis_index("lag"), lag_step)
        segment = lax.bitwise_xor(lax.axis_index("seg"), segment_step)
        start = pl.multiple_of((segment * lags + lag) * width, width)
        joined_ref[:, pl.ds(start, width)] = chunk_ref[...]
    series = joined_ref[:kept, :]
    panel = joined_ref[kept:, :]
    samples = panel.shape[1]
    terms = SAMPLES - LAGS
    times = lax.broadcasted_iota(jnp.int32, panel.shape, 1)
    panel = jnp.where(times < terms, panel, 0.0)
    series = pltpu.roll(series, samples - lax.axis_index("lag") * lag_width, 1)
    groups = lag_width // PHASES

    def shifted(value, count, step):
        parts = [value] + [pltpu.roll(value, (i * step) % samples, 1) for i in range(1, count)]
        return jnp.concatenate(parts, axis=0)

    panel_high, panel_low = (shifted(half, PHASES, 1) for half in halves(panel))
    series_high, series_low = (shifted(half, groups, -PHASES) for half in halves(series))
    lines = series_high.shape[0]
    total = product_nt(jnp.concatenate([series_high, series_low], axis=0), panel_high)
    total = total[:lines] + total[lines:] + product_nt(series_high, panel_low)
    total = total * (1.0 / math.sqrt(terms))
    columns = PHASES * refs
    for group in range(groups):
        out_ref[:, group * columns : (group + 1) * columns] = total[group * kept : (group + 1) * kept]


def shards(records_owned, section_list, ref_index):
    peers = lax.axis_size("chan")
    segments = lax.axis_size("seg")
    rows, _, samples = records_owned.shape
    refs = ref_index.shape[0]
    share = rows // peers
    kept = rows // segments
    lags = lax.axis_size("lag")
    lag_width = LAGS // lags
    lists = section_list.reshape(peers, rows)
    params = pltpu.CompilerParams(vmem_limit_bytes=48 * 1024 * 1024)
    wanted = ref_index.reshape(1, refs)

    def block(*shape, dtype=jnp.float32):
        return jax.ShapeDtypeStruct(shape, dtype)

    def call(kernel, name, shapes, *operands):
        return pl.pallas_call(kernel, out_shape=shapes, compiler_params=params, name=name)(*operands)

    shapes = [block(kept + refs, samples)] * segments
    if peers == 4:
        records = pl.pallas_call(
            load_kernel,
            out_shape=block(rows, 1, samples),
            in_specs=[pl.BlockSpec(memory_space=pl.ANY)],
            out_specs=pl.BlockSpec(memory_space=pl.ANY),
            scratch_shapes=[pltpu.SemaphoreType.DMA],
            compiler_params=params,
            name="load",
        )(pltpu.with_memory_space_constraint(records_owned, pltpu.HBM))
        first = paired(records, (1, 2))
        half = rows // 2
        send, keep, take = call(
            choose_four_kernel,
            "choose",
            [
                block(half + refs, 2 * rows, dtype=jnp.bfloat16),
                block(rows, 2 * rows, dtype=jnp.bfloat16),
                block(rows, half, dtype=jnp.bfloat16),
            ],
            lists,
            wanted,
        )
        sent, base = call(
            pick_kernel,
            "pick",
            [block(half + refs, samples), block(rows, samples)],
            records,
            first,
            send,
            keep,
        )
        placed = call(place_four_kernel, "place", shapes, base, take, sent, paired(sent, (2, 1)))
    else:
        packed, panel = call(
            pack_kernel,
            "pack",
            [block(rows, samples), block(refs, samples)],
            records_owned,
            lists,
            wanted,
        )
        blocks = packed.reshape(peers, share, samples)
        blocks = lax.all_to_all(blocks, "chan", split_axis=0, concat_axis=0, tiled=True)
        step = 1
        while step < peers:
            panel = panel + across(panel, step)
            step *= 2
        pick = call(
            functools.partial(choose_kernel, peers),
            "choose",
            block(rows, rows, dtype=jnp.bfloat16),
            lists,
        )
        placed = call(place_kernel, "place", shapes, pick, panel, blocks.reshape(rows, samples))
    held = {(0, 0): placed[0]}
    for lag_step in range(0, lags, 2):
        for segment_step in range(segments):
            if lag_step or segment_step:
                held[lag_step, segment_step] = swapped(placed[segment_step], lag_step, segment_step)
    for lag_step, segment_step in list(held):
        held[lag_step + 1, segment_step] = swapped(held[lag_step, segment_step], 1, 0)
    return pl.pallas_call(
        functools.partial(corr_kernel, refs, lag_width),
        out_shape=jax.ShapeDtypeStruct((kept, lag_width * refs), jnp.float32),
        scratch_shapes=[pltpu.VMEM((kept + refs, lags * segments * samples), jnp.float32)],
        compiler_params=params,
        name="correlate",
    )(*[held[step] for step in steps(lags, segments)])


def solution(mesh):
    return jax.shard_map(
        shards,
        mesh=mesh,
        in_specs=(P("chan", "seg", "lag"), P(), P()),
        out_specs=P(("chan", "seg"), "lag"),
        check_vma=False,
    )
```

```python
import functools
import math

import jax
import jax.numpy as jnp
from jax import lax
from jax.experimental import pallas as pl
from jax.experimental.pallas import tpu as pltpu
from jax.sharding import PartitionSpec as P

LAGS = 128
SAMPLES = 2048
PHASES = 4
GROUPS = 2


def halves(value):
    high = value.astype(jnp.bfloat16)
    low = (value - high.astype(jnp.float32)).astype(jnp.bfloat16)
    return high, low


def product(left, right):
    return jnp.dot(left, right, preferred_element_type=jnp.float32)


def product_nt(left, right):
    return lax.dot_general(
        left, right, (((1,), (1,)), ((), ())), preferred_element_type=jnp.float32
    )


def steps(lags, segments):
    return [(lag, segment) for lag in range(lags) for segment in range(segments)]


def swapped(value, lag_step, segment_step):
    lags, segments = lax.axis_size("lag"), lax.axis_size("seg")
    pairs = [
        (lag * segments + segment, (lag ^ lag_step) * segments + (segment ^ segment_step))
        for lag, segment in steps(lags, segments)
    ]
    return lax.ppermute(value, ("lag", "seg"), pairs)


def across(value, step):
    return lax.ppermute(value, "chan", [(i, i ^ step) for i in range(lax.axis_size("chan"))])


def paired(value, order):
    lags = lax.axis_size("lag")
    pairs = [
        (chan * lags + lag, (chan ^ order[lag % 2]) * lags + lag)
        for chan in range(lax.axis_size("chan"))
        for lag in range(lags)
    ]
    return lax.ppermute(value, ("chan", "lag"), pairs)


def choice(pick, rows):
    high, low = halves(rows)
    return product(pick, high) + product(pick, low)


def counts_before(present):
    rows = present.shape[0]
    line = lax.broadcasted_iota(jnp.int32, (rows, rows), 0)
    lane = lax.broadcasted_iota(jnp.int32, (rows, rows), 1)
    return product((lane < line).astype(jnp.bfloat16), present.astype(jnp.bfloat16))


def columns(refs_ref, width):
    return jnp.broadcast_to(refs_ref[...], (width, refs_ref.shape[1])).T


def choose_four_kernel(lists_ref, refs_ref, send_ref, keep_ref, take_ref):
    rows = lists_ref.shape[1]
    kept = take_ref.shape[1]
    refs = refs_ref.shape[1]
    me = lax.axis_index("chan")
    odd = lax.rem(lax.axis_index("lag"), 2)
    near, far = 1 + odd, 2 - odd
    line = lax.broadcasted_iota(jnp.int32, (rows, 2 * rows), 0)

    def pool(owner):
        lists = [lists_ref[pl.ds(lax.bitwise_xor(owner, i), 1), :] for i in (0, near)]
        return jnp.concatenate(lists, axis=1)

    def where(owner, block):
        return pool(owner) == line + block * rows

    def ranks(found):
        present = jnp.max(found.astype(jnp.float32), axis=1, keepdims=True)
        return present, counts_before(jnp.broadcast_to(present, (rows, rows)))

    other = lax.bitwise_xor(me, far)
    found = where(me, other)
    _, rank = ranks(found)
    rank = jnp.concatenate([rank, rank], axis=1)
    slot = jnp.sum(jnp.where(found, rank + 1.0, 0.0), axis=0, keepdims=True).astype(jnp.int32)
    send_ref[:kept, :] = (line[:kept] + 1 == slot).astype(jnp.bfloat16)
    send_ref[kept:, :] = (columns(refs_ref, 2 * rows) == pool(me)).astype(jnp.bfloat16)
    keep_ref[...] = where(me, me).astype(jnp.bfloat16)
    present, rank = ranks(where(other, me))
    lane = lax.broadcasted_iota(jnp.int32, (rows, kept), 1)
    slot = jnp.where(present > 0.0, rank[:, :kept], -1.0).astype(jnp.int32)
    take_ref[...] = (lane == slot).astype(jnp.bfloat16)


def load_kernel(records_ref, out_ref, done):
    pieces = done.shape[0]
    each = records_ref.shape[0] // pieces
    copies = [
        pltpu.make_async_copy(
            records_ref.at[pl.ds(i * each, each)], out_ref.at[pl.ds(i * each, each)], done.at[i]
        )
        for i in range(pieces)
    ]
    for copy in copies:
        copy.start()
    for copy in copies:
        copy.wait()


def pick_kernel(records_ref, arrived_ref, send_ref, keep_ref, sent_ref, base_ref):
    rows = jnp.concatenate([records_ref[:, 0, :], arrived_ref[:, 0, :]], axis=0)
    high, low = halves(rows)
    sent_ref[...] = product(send_ref[...], high) + product(send_ref[...], low)
    base_ref[...] = product(keep_ref[...], high) + product(keep_ref[...], low)


def put(series, panel, out_refs):
    segments = len(out_refs)
    kept = series.shape[0] // segments
    own = lax.axis_index("seg")
    for part in range(segments):
        half = lax.bitwise_xor(own, part)
        chosen = series[:kept]
        for other in range(1, segments):
            chosen = jnp.where(half == other, series[other * kept : (other + 1) * kept], chosen)
        out_refs[part][:kept, :] = chosen
        out_refs[part][kept:, :] = panel


def place_four_kernel(base_ref, take_ref, sent_ref, arrived_ref, *out_refs):
    kept = take_ref.shape[1]
    series = base_ref[...] + choice(take_ref[...], arrived_ref[:kept, :])
    put(series, sent_ref[kept:, :] + arrived_ref[kept:, :], out_refs)


def pack_kernel(records_ref, lists_ref, refs_ref, out_ref, panel_ref):
    rows = records_ref.shape[0]
    refs = refs_ref.shape[1]
    own = jnp.broadcast_to(lists_ref[pl.ds(lax.axis_index("chan"), 1), :], (rows, rows))
    rank = jnp.sum((own.T < own).astype(jnp.int32), axis=0, keepdims=True)
    line = lax.broadcasted_iota(jnp.int32, (rows, rows), 0)
    records = records_ref[:, 0, :]
    panel_ref[...] = choice((columns(refs_ref, rows) == own[:refs]).astype(jnp.bfloat16), records)
    out_ref[...] = choice((line == rank).astype(jnp.bfloat16), records)


def choose_kernel(peers, lists_ref, pick_ref):
    rows = lists_ref.shape[1]
    share = rows // peers
    lane = lax.broadcasted_iota(jnp.int32, (rows, rows), 1)
    channel = lax.broadcasted_iota(jnp.int32, (rows, rows), 0) + lax.axis_index("chan") * rows
    owner = jnp.zeros((rows, 1), jnp.int32)
    for peer in range(peers):
        found = (lists_ref[pl.ds(peer, 1), :] == channel).astype(jnp.int32)
        owner = owner + jnp.sum(found, axis=1, keepdims=True) * peer
    same = lane == owner
    before = counts_before(same.astype(jnp.float32))
    rank = jnp.sum(jnp.where(same, before, 0.0), axis=1, keepdims=True).astype(jnp.int32)
    pick_ref[...] = (lane == owner * share + rank).astype(jnp.bfloat16)


def place_kernel(pick_ref, panel_ref, arrived_ref, *out_refs):
    put(choice(pick_ref[...], arrived_ref[...]), panel_ref[...], out_refs)


def corr_kernel(refs, lag_width, *rest):
    *chunk_refs, out_ref, joined_ref, total_ref, done = rest
    kept = total_ref.shape[0]
    lags, segments = lax.axis_size("lag"), lax.axis_size("seg")
    width = chunk_refs[0].shape[1]
    for (lag_step, segment_step), chunk_ref in zip(steps(lags, segments), chunk_refs):
        lag = lax.bitwise_xor(lax.axis_index("lag"), lag_step)
        segment = lax.bitwise_xor(lax.axis_index("seg"), segment_step)
        start = pl.multiple_of((segment * lags + lag) * width, width)
        joined_ref[:, pl.ds(start, width)] = chunk_ref[...]
    series = joined_ref[:kept, :]
    panel = joined_ref[kept:, :]
    samples = panel.shape[1]
    terms = SAMPLES - LAGS
    times = lax.broadcasted_iota(jnp.int32, panel.shape, 1)
    panel = jnp.where(times < terms, panel, 0.0)
    series = pltpu.roll(series, samples - lax.axis_index("lag") * lag_width, 1)
    scale = 1.0 / math.sqrt(terms)
    columns = PHASES * refs
    each = lag_width // PHASES // GROUPS

    def shifted(value, shifts):
        parts = [pltpu.roll(value, shift % samples, 1) if shift else value for shift in shifts]
        return jnp.concatenate(parts, axis=0)

    panel_high, panel_low = (shifted(half, range(PHASES)) for half in halves(panel))
    series_high, series_low = halves(series)
    copies = []
    for group in range(GROUPS):
        shifts = [-PHASES * (group * each + i) for i in range(each)]
        high, low = shifted(series_high, shifts), shifted(series_low, shifts)
        lines = each * kept
        total = product_nt(jnp.concatenate([high, low], axis=0), panel_high)
        total = (total[:lines] + total[lines:] + product_nt(high, panel_low)) * scale
        for i in range(each):
            start = (group * each + i) * columns
            total_ref[:, start : start + columns] = total[i * kept : (i + 1) * kept]
        part = pl.ds(group * each * columns, each * columns)
        copies.append(pltpu.make_async_copy(total_ref.at[:, part], out_ref.at[:, part], done.at[group]))
        copies[-1].start()
    for copy in copies:
        copy.wait()


def shards(records_owned, section_list, ref_index):
    peers = lax.axis_size("chan")
    segments = lax.axis_size("seg")
    rows, _, samples = records_owned.shape
    refs = ref_index.shape[0]
    share = rows // peers
    kept = rows // segments
    lags = lax.axis_size("lag")
    lag_width = LAGS // lags
    lists = section_list.reshape(peers, rows)
    params = pltpu.CompilerParams(vmem_limit_bytes=48 * 1024 * 1024)
    wanted = ref_index.reshape(1, refs)

    def block(*shape, dtype=jnp.float32):
        return jax.ShapeDtypeStruct(shape, dtype)

    def call(kernel, name, shapes, *operands):
        return pl.pallas_call(kernel, out_shape=shapes, compiler_params=params, name=name)(*operands)

    shapes = [block(kept + refs, samples)] * segments
    if peers == 4:
        records = pl.pallas_call(
            load_kernel,
            out_shape=block(rows, 1, samples),
            in_specs=[pl.BlockSpec(memory_space=pl.ANY)],
            out_specs=pl.BlockSpec(memory_space=pl.ANY),
            scratch_shapes=[pltpu.SemaphoreType.DMA((8,))],
            compiler_params=params,
            name="load",
        )(pltpu.with_memory_space_constraint(records_owned, pltpu.HBM))
        first = paired(records, (1, 2))
        half = rows // 2
        send, keep, take = call(
            choose_four_kernel,
            "choose",
            [
                block(half + refs, 2 * rows, dtype=jnp.bfloat16),
                block(rows, 2 * rows, dtype=jnp.bfloat16),
                block(rows, half, dtype=jnp.bfloat16),
            ],
            lists,
            wanted,
        )
        sent, base = call(
            pick_kernel,
            "pick",
            [block(half + refs, samples), block(rows, samples)],
            records,
            first,
            send,
            keep,
        )
        placed = call(place_four_kernel, "place", shapes, base, take, sent, paired(sent, (2, 1)))
    else:
        packed, panel = call(
            pack_kernel,
            "pack",
            [block(rows, samples), block(refs, samples)],
            records_owned,
            lists,
            wanted,
        )
        blocks = packed.reshape(peers, share, samples)
        blocks = lax.all_to_all(blocks, "chan", split_axis=0, concat_axis=0, tiled=True)
        step = 1
        while step < peers:
            panel = panel + across(panel, step)
            step *= 2
        pick = call(
            functools.partial(choose_kernel, peers),
            "choose",
            block(rows, rows, dtype=jnp.bfloat16),
            lists,
        )
        placed = call(place_kernel, "place", shapes, pick, panel, blocks.reshape(rows, samples))
    held = {(0, 0): placed[0]}
    for lag_step in range(0, lags, 2):
        for segment_step in range(segments):
            if lag_step or segment_step:
                held[lag_step, segment_step] = swapped(placed[segment_step], lag_step, segment_step)
    for lag_step, segment_step in list(held):
        held[lag_step + 1, segment_step] = swapped(held[lag_step, segment_step], 1, 0)
    return pl.pallas_call(
        functools.partial(corr_kernel, refs, lag_width),
        out_shape=jax.ShapeDtypeStruct((kept, lag_width * refs), jnp.float32),
        out_specs=pl.BlockSpec(memory_space=pl.ANY),
        scratch_shapes=[
            pltpu.VMEM((kept + refs, lags * segments * samples), jnp.float32),
            pltpu.VMEM((kept, lag_width * refs), jnp.float32),
            pltpu.SemaphoreType.DMA((GROUPS,)),
        ],
        compiler_params=params,
        name="correlate",
    )(*[held[step] for step in steps(lags, segments)])


def solution(mesh):
    return jax.shard_map(
        shards,
        mesh=mesh,
        in_specs=(P("chan", "seg", "lag"), P(), P()),
        out_specs=P(("chan", "seg"), "lag"),
        check_vma=False,
    )
```

```python
import functools
import math

import jax
import jax.numpy as jnp
from jax import lax
from jax.experimental import pallas as pl
from jax.experimental.pallas import tpu as pltpu
from jax.sharding import PartitionSpec as P

LAGS = 128
SAMPLES = 2048
PHASES = 4
GROUPS = 2


def halves(value):
    high = value.astype(jnp.bfloat16)
    low = (value - high.astype(jnp.float32)).astype(jnp.bfloat16)
    return high, low


def product(left, right):
    return jnp.dot(left, right, preferred_element_type=jnp.float32)


def product_nt(left, right):
    return lax.dot_general(
        left, right, (((1,), (1,)), ((), ())), preferred_element_type=jnp.float32
    )


def steps(lags, segments):
    return [(lag, segment) for lag in range(lags) for segment in range(segments)]


def swapped(value, lag_step, segment_step):
    lags, segments = lax.axis_size("lag"), lax.axis_size("seg")
    pairs = [
        (lag * segments + segment, (lag ^ lag_step) * segments + (segment ^ segment_step))
        for lag, segment in steps(lags, segments)
    ]
    return lax.ppermute(value, ("lag", "seg"), pairs)


def across(value, step):
    return lax.ppermute(value, "chan", [(i, i ^ step) for i in range(lax.axis_size("chan"))])


def paired(value, order):
    lags = lax.axis_size("lag")
    pairs = [
        (chan * lags + lag, (chan ^ order[lag % 2]) * lags + lag)
        for chan in range(lax.axis_size("chan"))
        for lag in range(lags)
    ]
    return lax.ppermute(value, ("chan", "lag"), pairs)


def choice(pick, rows):
    high, low = halves(rows)
    return product(pick, high) + product(pick, low)


def counts_before(present):
    rows = present.shape[0]
    line = lax.broadcasted_iota(jnp.int32, (rows, rows), 0)
    lane = lax.broadcasted_iota(jnp.int32, (rows, rows), 1)
    return product((lane < line).astype(jnp.bfloat16), present.astype(jnp.bfloat16))


def columns(refs_ref, width):
    return jnp.broadcast_to(refs_ref[...], (width, refs_ref.shape[1])).T


def choose_four_kernel(
    records_ref,
    lists_ref,
    refs_ref,
    sent_ref,
    base_ref,
    send_ref,
    keep_ref,
    take_ref,
    held_ref,
    done,
):
    copy = pltpu.make_async_copy(records_ref, held_ref, done)
    copy.start()
    rows = lists_ref.shape[1]
    kept = take_ref.shape[1]
    refs = refs_ref.shape[1]
    me = lax.axis_index("chan")
    odd = lax.rem(lax.axis_index("lag"), 2)
    near, far = 1 + odd, 2 - odd
    line = lax.broadcasted_iota(jnp.int32, (rows, 2 * rows), 0)

    def pool(owner):
        lists = [lists_ref[pl.ds(lax.bitwise_xor(owner, i), 1), :] for i in (0, near)]
        return jnp.concatenate(lists, axis=1)

    def where(owner, block):
        return pool(owner) == line + block * rows

    def ranks(found):
        present = jnp.max(found.astype(jnp.float32), axis=1, keepdims=True)
        return present, counts_before(jnp.broadcast_to(present, (rows, rows)))

    other = lax.bitwise_xor(me, far)
    found = where(me, other)
    _, rank = ranks(found)
    rank = jnp.concatenate([rank, rank], axis=1)
    slot = jnp.sum(jnp.where(found, rank + 1.0, 0.0), axis=0, keepdims=True).astype(jnp.int32)
    send = jnp.concatenate([line[:kept] + 1 == slot, columns(refs_ref, 2 * rows) == pool(me)], axis=0)
    send = send.astype(jnp.bfloat16)
    keep = where(me, me).astype(jnp.bfloat16)
    send_ref[...] = send[:, rows:]
    keep_ref[...] = keep[:, rows:]
    present, rank = ranks(where(other, me))
    lane = lax.broadcasted_iota(jnp.int32, (rows, kept), 1)
    slot = jnp.where(present > 0.0, rank[:, :kept], -1.0).astype(jnp.int32)
    take_ref[...] = (lane == slot).astype(jnp.bfloat16)
    copy.wait()
    high, low = halves(held_ref[:, 0, :])
    sent_ref[...] = product(send[:, :rows], high) + product(send[:, :rows], low)
    base_ref[...] = product(keep[:, :rows], high) + product(keep[:, :rows], low)


def pick_kernel(arrived_ref, send_ref, keep_ref, own_sent_ref, own_base_ref, sent_ref, base_ref):
    high, low = halves(arrived_ref[:, 0, :])
    send, keep = send_ref[...], keep_ref[...]
    sent_ref[...] = own_sent_ref[...] + (product(send, high) + product(send, low))
    base_ref[...] = own_base_ref[...] + (product(keep, high) + product(keep, low))


def put(series, panel, out_refs):
    segments = len(out_refs)
    kept = series.shape[0] // segments
    own = lax.axis_index("seg")
    for part in range(segments):
        half = lax.bitwise_xor(own, part)
        chosen = series[:kept]
        for other in range(1, segments):
            chosen = jnp.where(half == other, series[other * kept : (other + 1) * kept], chosen)
        out_refs[part][:kept, :] = chosen
        out_refs[part][kept:, :] = panel


def place_four_kernel(base_ref, take_ref, sent_ref, arrived_ref, *out_refs):
    kept = take_ref.shape[1]
    series = base_ref[...] + choice(take_ref[...], arrived_ref[:kept, :])
    put(series, sent_ref[kept:, :] + arrived_ref[kept:, :], out_refs)


def pack_kernel(records_ref, lists_ref, refs_ref, out_ref, panel_ref):
    rows = records_ref.shape[0]
    refs = refs_ref.shape[1]
    own = jnp.broadcast_to(lists_ref[pl.ds(lax.axis_index("chan"), 1), :], (rows, rows))
    rank = jnp.sum((own.T < own).astype(jnp.int32), axis=0, keepdims=True)
    line = lax.broadcasted_iota(jnp.int32, (rows, rows), 0)
    records = records_ref[:, 0, :]
    panel_ref[...] = choice((columns(refs_ref, rows) == own[:refs]).astype(jnp.bfloat16), records)
    out_ref[...] = choice((line == rank).astype(jnp.bfloat16), records)


def choose_kernel(peers, lists_ref, pick_ref):
    rows = lists_ref.shape[1]
    share = rows // peers
    lane = lax.broadcasted_iota(jnp.int32, (rows, rows), 1)
    channel = lax.broadcasted_iota(jnp.int32, (rows, rows), 0) + lax.axis_index("chan") * rows
    owner = jnp.zeros((rows, 1), jnp.int32)
    for peer in range(peers):
        found = (lists_ref[pl.ds(peer, 1), :] == channel).astype(jnp.int32)
        owner = owner + jnp.sum(found, axis=1, keepdims=True) * peer
    same = lane == owner
    before = counts_before(same.astype(jnp.float32))
    rank = jnp.sum(jnp.where(same, before, 0.0), axis=1, keepdims=True).astype(jnp.int32)
    pick_ref[...] = (lane == owner * share + rank).astype(jnp.bfloat16)


def place_kernel(pick_ref, panel_ref, arrived_ref, *out_refs):
    put(choice(pick_ref[...], arrived_ref[...]), panel_ref[...], out_refs)


def corr_kernel(refs, lag_width, *rest):
    *chunk_refs, out_ref, joined_ref, total_ref, done = rest
    kept = total_ref.shape[0]
    lags, segments = lax.axis_size("lag"), lax.axis_size("seg")
    width = chunk_refs[0].shape[1]
    for (lag_step, segment_step), chunk_ref in zip(steps(lags, segments), chunk_refs):
        lag = lax.bitwise_xor(lax.axis_index("lag"), lag_step)
        segment = lax.bitwise_xor(lax.axis_index("seg"), segment_step)
        start = pl.multiple_of((segment * lags + lag) * width, width)
        joined_ref[:, pl.ds(start, width)] = chunk_ref[...]
    series = joined_ref[:kept, :]
    panel = joined_ref[kept:, :]
    samples = panel.shape[1]
    terms = SAMPLES - LAGS
    times = lax.broadcasted_iota(jnp.int32, panel.shape, 1)
    panel = jnp.where(times < terms, panel, 0.0)
    series = pltpu.roll(series, samples - lax.axis_index("lag") * lag_width, 1)
    scale = 1.0 / math.sqrt(terms)
    columns = PHASES * refs
    each = lag_width // PHASES // GROUPS

    def shifted(value, shifts):
        parts = [pltpu.roll(value, shift % samples, 1) if shift else value for shift in shifts]
        return jnp.concatenate(parts, axis=0)

    panel_high, panel_low = (shifted(half, range(PHASES)) for half in halves(panel))
    series_high, series_low = halves(series)
    copies = []
    for group in range(GROUPS):
        shifts = [-PHASES * (group * each + i) for i in range(each)]
        high, low = shifted(series_high, shifts), shifted(series_low, shifts)
        lines = each * kept
        total = product_nt(jnp.concatenate([high, low], axis=0), panel_high)
        total = (total[:lines] + total[lines:] + product_nt(high, panel_low)) * scale
        for i in range(each):
            start = (group * each + i) * columns
            total_ref[:, start : start + columns] = total[i * kept : (i + 1) * kept]
        part = pl.ds(group * each * columns, each * columns)
        copies.append(pltpu.make_async_copy(total_ref.at[:, part], out_ref.at[:, part], done.at[group]))
        copies[-1].start()
    for copy in copies:
        copy.wait()


def shards(records_owned, section_list, ref_index):
    peers = lax.axis_size("chan")
    segments = lax.axis_size("seg")
    rows, _, samples = records_owned.shape
    refs = ref_index.shape[0]
    share = rows // peers
    kept = rows // segments
    lags = lax.axis_size("lag")
    lag_width = LAGS // lags
    lists = section_list.reshape(peers, rows)
    params = pltpu.CompilerParams(vmem_limit_bytes=48 * 1024 * 1024)
    wanted = ref_index.reshape(1, refs)

    def block(*shape, dtype=jnp.float32):
        return jax.ShapeDtypeStruct(shape, dtype)

    def call(kernel, name, shapes, *operands):
        return pl.pallas_call(kernel, out_shape=shapes, compiler_params=params, name=name)(*operands)

    shapes = [block(kept + refs, samples)] * segments
    if peers == 4:
        first = paired(records_owned, (1, 2))
        half = rows // 2
        results = [block(half + refs, samples), block(rows, samples)]
        whole = pl.BlockSpec(memory_space=pltpu.VMEM)
        *own, send, keep, take = pl.pallas_call(
            choose_four_kernel,
            out_shape=[
                *results,
                block(half + refs, rows, dtype=jnp.bfloat16),
                block(rows, rows, dtype=jnp.bfloat16),
                block(rows, half, dtype=jnp.bfloat16),
            ],
            in_specs=[pl.BlockSpec(memory_space=pl.ANY), whole, whole],
            scratch_shapes=[pltpu.VMEM(records_owned.shape, jnp.float32), pltpu.SemaphoreType.DMA],
            compiler_params=params,
            name="choose",
        )(pltpu.with_memory_space_constraint(records_owned, pltpu.HBM), lists, wanted)
        sent, base = call(pick_kernel, "pick", results, first, send, keep, *own)
        placed = call(place_four_kernel, "place", shapes, base, take, sent, paired(sent, (2, 1)))
    else:
        packed, panel = call(
            pack_kernel,
            "pack",
            [block(rows, samples), block(refs, samples)],
            records_owned,
            lists,
            wanted,
        )
        blocks = packed.reshape(peers, share, samples)
        blocks = lax.all_to_all(blocks, "chan", split_axis=0, concat_axis=0, tiled=True)
        step = 1
        while step < peers:
            panel = panel + across(panel, step)
            step *= 2
        pick = call(
            functools.partial(choose_kernel, peers),
            "choose",
            block(rows, rows, dtype=jnp.bfloat16),
            lists,
        )
        placed = call(place_kernel, "place", shapes, pick, panel, blocks.reshape(rows, samples))
    held = {(0, 0): placed[0]}
    for lag_step in range(0, lags, 2):
        for segment_step in range(segments):
            if lag_step or segment_step:
                held[lag_step, segment_step] = swapped(placed[segment_step], lag_step, segment_step)
    for lag_step, segment_step in list(held):
        held[lag_step + 1, segment_step] = swapped(held[lag_step, segment_step], 1, 0)
    return pl.pallas_call(
        functools.partial(corr_kernel, refs, lag_width),
        out_shape=jax.ShapeDtypeStruct((kept, lag_width * refs), jnp.float32),
        out_specs=pl.BlockSpec(memory_space=pl.ANY),
        scratch_shapes=[
            pltpu.VMEM((kept + refs, lags * segments * samples), jnp.float32),
            pltpu.VMEM((kept, lag_width * refs), jnp.float32),
            pltpu.SemaphoreType.DMA((GROUPS,)),
        ],
        compiler_params=params,
        name="correlate",
    )(*[held[step] for step in steps(lags, segments)])


def solution(mesh):
    return jax.shard_map(
        shards,
        mesh=mesh,
        in_specs=(P("chan", "seg", "lag"), P(), P()),
        out_specs=P(("chan", "seg"), "lag"),
        check_vma=False,
    )
```

```python
import functools
import math

import jax
import jax.numpy as jnp
from jax import lax
from jax.experimental import pallas as pl
from jax.experimental.pallas import tpu as pltpu
from jax.sharding import PartitionSpec as P

LAGS = 128
SAMPLES = 2048
PHASES = 4


def halves(value):
    high = value.astype(jnp.bfloat16)
    low = (value - high.astype(jnp.float32)).astype(jnp.bfloat16)
    return high, low


def product(left, right):
    return jnp.dot(left, right, preferred_element_type=jnp.float32)


def product_nt(left, right):
    return lax.dot_general(
        left, right, (((1,), (1,)), ((), ())), preferred_element_type=jnp.float32
    )


def steps(lags, segments):
    return [(lag, segment) for lag in range(lags) for segment in range(segments)]


def swapped(value, lag_step, segment_step):
    lags, segments = lax.axis_size("lag"), lax.axis_size("seg")
    pairs = [
        (lag * segments + segment, (lag ^ lag_step) * segments + (segment ^ segment_step))
        for lag, segment in steps(lags, segments)
    ]
    return lax.ppermute(value, ("lag", "seg"), pairs)


def across(value, step):
    return lax.ppermute(value, "chan", [(i, i ^ step) for i in range(lax.axis_size("chan"))])


def paired(value, order):
    lags = lax.axis_size("lag")
    pairs = [
        (chan * lags + lag, (chan ^ order[lag % 2]) * lags + lag)
        for chan in range(lax.axis_size("chan"))
        for lag in range(lags)
    ]
    return lax.ppermute(value, ("chan", "lag"), pairs)


def choice(pick, rows):
    high, low = halves(rows)
    return product(
        jnp.concatenate([pick, pick], axis=1), jnp.concatenate([high, low], axis=0)
    )


def counts_before(present):
    rows = present.shape[0]
    line = lax.broadcasted_iota(jnp.int32, (rows, rows), 0)
    lane = lax.broadcasted_iota(jnp.int32, (rows, rows), 1)
    return product((lane < line).astype(jnp.bfloat16), present.astype(jnp.bfloat16))


def columns(refs_ref, width):
    return jnp.broadcast_to(refs_ref[...], (width, refs_ref.shape[1])).T


def choose_four_kernel(
    records_ref,
    lists_ref,
    refs_ref,
    own_ref,
    pick_ref,
    take_ref,
    held_ref,
    done,
):
    copy = pltpu.make_async_copy(records_ref, held_ref, done)
    copy.start()
    rows = lists_ref.shape[1]
    kept = take_ref.shape[1]
    refs = refs_ref.shape[1]
    me = lax.axis_index("chan")
    odd = lax.rem(lax.axis_index("lag"), 2)
    near, far = 1 + odd, 2 - odd
    line = lax.broadcasted_iota(jnp.int32, (rows, 2 * rows), 0)

    def pool(owner):
        lists = [lists_ref[pl.ds(lax.bitwise_xor(owner, i), 1), :] for i in (0, near)]
        return jnp.concatenate(lists, axis=1)

    def where(owner, block):
        return pool(owner) == line + block * rows

    def ranks(found):
        present = jnp.max(found.astype(jnp.float32), axis=1, keepdims=True)
        return present, counts_before(jnp.broadcast_to(present, (rows, rows)))

    other = lax.bitwise_xor(me, far)
    found = where(me, other)
    _, rank = ranks(found)
    rank = jnp.concatenate([rank, rank], axis=1)
    slot = jnp.sum(jnp.where(found, rank + 1.0, 0.0), axis=0, keepdims=True).astype(jnp.int32)
    send = jnp.concatenate([line[:kept] + 1 == slot, columns(refs_ref, 2 * rows) == pool(me)], axis=0)
    send = send.astype(jnp.bfloat16)
    keep = where(me, me).astype(jnp.bfloat16)
    pick_ref[...] = jnp.concatenate([send[:, rows:], keep[:, rows:]], axis=0)
    present, rank = ranks(where(other, me))
    lane = lax.broadcasted_iota(jnp.int32, (rows, kept), 1)
    slot = jnp.where(present > 0.0, rank[:, :kept], -1.0).astype(jnp.int32)
    take_ref[...] = (lane == slot).astype(jnp.bfloat16)
    copy.wait()
    own_ref[...] = choice(jnp.concatenate([send[:, :rows], keep[:, :rows]], axis=0), held_ref[:, 0, :])


def pick_kernel(arrived_ref, pick_ref, own_ref, sent_ref, base_ref):
    rows = own_ref[...] + choice(pick_ref[...], arrived_ref[:, 0, :])
    lines = sent_ref.shape[0]
    sent_ref[...] = rows[:lines]
    base_ref[...] = rows[lines:]


def put(series, panel, out_refs):
    width = series.shape[1]
    line = lax.broadcasted_iota(jnp.int32, (width, width), 0)
    lane = lax.broadcasted_iota(jnp.int32, (width, width), 1)
    source = 2 * lax.rem(lane, width // 2) + lax.div(lane, width // 2)
    order = (line == source).astype(jnp.bfloat16)
    high, low = halves(jnp.concatenate([series, panel], axis=0))
    rows = product(
        jnp.concatenate([high, low], axis=1), jnp.concatenate([order, order], axis=0)
    )
    series, panel = rows[: series.shape[0]], rows[series.shape[0] :]
    segments = len(out_refs)
    kept = series.shape[0] // segments
    own = lax.axis_index("seg")
    for part in range(segments):
        half = lax.bitwise_xor(own, part)
        chosen = series[:kept]
        for other in range(1, segments):
            chosen = jnp.where(half == other, series[other * kept : (other + 1) * kept], chosen)
        out_refs[part][:kept, :] = chosen
        out_refs[part][kept:, :] = panel


def place_four_kernel(base_ref, take_ref, sent_ref, arrived_ref, *out_refs):
    kept = take_ref.shape[1]
    series = base_ref[...] + choice(take_ref[...], arrived_ref[:kept, :])
    put(series, sent_ref[kept:, :] + arrived_ref[kept:, :], out_refs)


def pack_kernel(records_ref, lists_ref, refs_ref, out_ref, panel_ref):
    rows = records_ref.shape[0]
    refs = refs_ref.shape[1]
    own = jnp.broadcast_to(lists_ref[pl.ds(lax.axis_index("chan"), 1), :], (rows, rows))
    rank = jnp.sum((own.T < own).astype(jnp.int32), axis=0, keepdims=True)
    line = lax.broadcasted_iota(jnp.int32, (rows, rows), 0)
    records = records_ref[:, 0, :]
    panel_ref[...] = choice((columns(refs_ref, rows) == own[:refs]).astype(jnp.bfloat16), records)
    out_ref[...] = choice((line == rank).astype(jnp.bfloat16), records)


def choose_kernel(peers, lists_ref, pick_ref):
    rows = lists_ref.shape[1]
    share = rows // peers
    lane = lax.broadcasted_iota(jnp.int32, (rows, rows), 1)
    channel = lax.broadcasted_iota(jnp.int32, (rows, rows), 0) + lax.axis_index("chan") * rows
    owner = jnp.zeros((rows, 1), jnp.int32)
    for peer in range(peers):
        found = (lists_ref[pl.ds(peer, 1), :] == channel).astype(jnp.int32)
        owner = owner + jnp.sum(found, axis=1, keepdims=True) * peer
    same = lane == owner
    before = counts_before(same.astype(jnp.float32))
    rank = jnp.sum(jnp.where(same, before, 0.0), axis=1, keepdims=True).astype(jnp.int32)
    pick_ref[...] = (lane == owner * share + rank).astype(jnp.bfloat16)


def place_kernel(pick_ref, panel_ref, arrived_ref, *out_refs):
    put(choice(pick_ref[...], arrived_ref[...]), panel_ref[...], out_refs)


def corr_kernel(refs, lag_width, *rest):
    *chunk_refs, out_ref, joined_ref, products_ref = rest
    kept = out_ref.shape[0]
    lags, segments = lax.axis_size("lag"), lax.axis_size("seg")
    width = chunk_refs[0].shape[1] // 2
    for (lag_step, segment_step), chunk_ref in zip(steps(lags, segments), chunk_refs):
        lag = lax.bitwise_xor(lax.axis_index("lag"), lag_step)
        segment = lax.bitwise_xor(lax.axis_index("seg"), segment_step)
        start = pl.multiple_of((segment * lags + lag) * width, width)
        for phase in range(2):
            joined_ref[phase, :, pl.ds(start, width)] = chunk_ref[:, phase * width : (phase + 1) * width]
    length = joined_ref.shape[2]
    terms = SAMPLES - LAGS
    times = lax.broadcasted_iota(jnp.int32, (refs, length), 1)
    first = lax.axis_index("lag") * (lag_width // 2)
    even, odd = (pltpu.roll(joined_ref[phase, :kept, :], length - first, 1) for phase in range(2))
    panel_even, panel_odd = (
        jnp.where(times < terms // 2, joined_ref[phase, kept:, :], 0.0) for phase in range(2)
    )
    groups = lag_width // 2 // PHASES

    def shifted(value, count, step):
        parts = [value] + [pltpu.roll(value, (i * step) % length, 1) for i in range(1, count)]
        return jnp.concatenate(parts, axis=0)

    def correlated(series, panel):
        panel_high, panel_low = (shifted(half, PHASES, 1) for half in halves(panel))
        high, low = (shifted(half, groups, -PHASES) for half in halves(series))
        return product_nt(
            jnp.concatenate([high, low, high], axis=1),
            jnp.concatenate([panel_high, panel_high, panel_low], axis=1),
        )

    products_ref[0] = correlated(odd, panel_even + panel_odd)
    products_ref[1] = correlated(even - odd, panel_even)
    products_ref[2] = correlated(pltpu.roll(even, length - 1, 1) - odd, panel_odd)
    both = [products_ref[0] + products_ref[i] for i in (1, 2)]
    scale = 1.0 / math.sqrt(terms)
    for group in range(groups):
        lines = slice(group * kept, (group + 1) * kept)
        for phase in range(PHASES):
            lanes = slice(phase * refs, (phase + 1) * refs)
            start = (group * PHASES + phase) * 2 * refs
            out_ref[:, start : start + 2 * refs] = scale * jnp.concatenate(
                [total[lines, lanes] for total in both], axis=1
            )


def shards(records_owned, section_list, ref_index):
    peers = lax.axis_size("chan")
    segments = lax.axis_size("seg")
    rows, _, samples = records_owned.shape
    refs = ref_index.shape[0]
    share = rows // peers
    kept = rows // segments
    lags = lax.axis_size("lag")
    lag_width = LAGS // lags
    lists = section_list.reshape(peers, rows)
    params = pltpu.CompilerParams(vmem_limit_bytes=48 * 1024 * 1024)
    wanted = ref_index.reshape(1, refs)

    def block(*shape, dtype=jnp.float32):
        return jax.ShapeDtypeStruct(shape, dtype)

    def call(kernel, name, shapes, *operands):
        return pl.pallas_call(kernel, out_shape=shapes, compiler_params=params, name=name)(*operands)

    shapes = [block(kept + refs, samples)] * segments
    if peers == 4:
        first = paired(records_owned, (1, 2))
        half = rows // 2
        whole = pl.BlockSpec(memory_space=pltpu.VMEM)
        own, pick, take = pl.pallas_call(
            choose_four_kernel,
            out_shape=[
                block(half + refs + rows, samples),
                block(half + refs + rows, rows, dtype=jnp.bfloat16),
                block(rows, half, dtype=jnp.bfloat16),
            ],
            in_specs=[pl.BlockSpec(memory_space=pl.ANY), whole, whole],
            scratch_shapes=[pltpu.VMEM(records_owned.shape, jnp.float32), pltpu.SemaphoreType.DMA],
            compiler_params=params,
            name="choose",
        )(pltpu.with_memory_space_constraint(records_owned, pltpu.HBM), lists, wanted)
        results = [block(half + refs, samples), block(rows, samples)]
        sent, base = call(pick_kernel, "pick", results, first, pick, own)
        placed = call(place_four_kernel, "place", shapes, base, take, sent, paired(sent, (2, 1)))
    else:
        packed, panel = call(
            pack_kernel,
            "pack",
            [block(rows, samples), block(refs, samples)],
            records_owned,
            lists,
            wanted,
        )
        blocks = packed.reshape(peers, share, samples)
        blocks = lax.all_to_all(blocks, "chan", split_axis=0, concat_axis=0, tiled=True)
        step = 1
        while step < peers:
            panel = panel + across(panel, step)
            step *= 2
        pick = call(
            functools.partial(choose_kernel, peers),
            "choose",
            block(rows, rows, dtype=jnp.bfloat16),
            lists,
        )
        placed = call(place_kernel, "place", shapes, pick, panel, blocks.reshape(rows, samples))
    held = {(0, 0): placed[0]}
    for lag_step in range(0, lags, 2):
        for segment_step in range(segments):
            if lag_step or segment_step:
                held[lag_step, segment_step] = swapped(placed[segment_step], lag_step, segment_step)
    for lag_step, segment_step in list(held):
        held[lag_step + 1, segment_step] = swapped(held[lag_step, segment_step], 1, 0)
    return pl.pallas_call(
        functools.partial(corr_kernel, refs, lag_width),
        out_shape=jax.ShapeDtypeStruct((kept, lag_width * refs), jnp.float32),
        scratch_shapes=[
            pltpu.VMEM((2, kept + refs, lags * segments * samples // 2), jnp.float32),
            pltpu.VMEM((3, lag_width // 2 // PHASES * kept, PHASES * refs), jnp.float32),
        ],
        compiler_params=params,
        name="correlate",
    )(*[held[step] for step in steps(lags, segments)])


def solution(mesh):
    return jax.shard_map(
        shards,
        mesh=mesh,
        in_specs=(P("chan", "seg", "lag"), P(), P()),
        out_specs=P(("chan", "seg"), "lag"),
        check_vma=False,
    )
```

```python
import functools
import math

import jax
import jax.numpy as jnp
from jax import lax
from jax.experimental import pallas as pl
from jax.experimental.pallas import tpu as pltpu
from jax.sharding import PartitionSpec as P

LAGS = 128
SAMPLES = 2048
PHASES = 4
GROUPS = 4


def halves(value):
    high = value.astype(jnp.bfloat16)
    low = (value - high.astype(jnp.float32)).astype(jnp.bfloat16)
    return high, low


def product(left, right):
    return jnp.dot(left, right, preferred_element_type=jnp.float32)


def product_nt(left, right):
    return lax.dot_general(
        left, right, (((1,), (1,)), ((), ())), preferred_element_type=jnp.float32
    )


def steps(lags, segments):
    return [(lag, segment) for lag in range(lags) for segment in range(segments)]


def swapped(value, lag_step, segment_step):
    lags, segments = lax.axis_size("lag"), lax.axis_size("seg")
    pairs = [
        (lag * segments + segment, (lag ^ lag_step) * segments + (segment ^ segment_step))
        for lag, segment in steps(lags, segments)
    ]
    return lax.ppermute(value, ("lag", "seg"), pairs)


def across(value, step):
    return lax.ppermute(value, "chan", [(i, i ^ step) for i in range(lax.axis_size("chan"))])


def paired(value, order):
    lags = lax.axis_size("lag")
    pairs = [
        (chan * lags + lag, (chan ^ order[lag % 2]) * lags + lag)
        for chan in range(lax.axis_size("chan"))
        for lag in range(lags)
    ]
    return lax.ppermute(value, ("chan", "lag"), pairs)


def choice(pick, rows):
    high, low = halves(rows)
    return product(pick, high) + product(pick, low)


def counts_before(present):
    rows = present.shape[0]
    line = lax.broadcasted_iota(jnp.int32, (rows, rows), 0)
    lane = lax.broadcasted_iota(jnp.int32, (rows, rows), 1)
    return product((lane < line).astype(jnp.bfloat16), present.astype(jnp.bfloat16))


def columns(refs_ref, width):
    return jnp.broadcast_to(refs_ref[...], (width, refs_ref.shape[1])).T


def choose_four_kernel(
    records_ref,
    lists_ref,
    refs_ref,
    parts_ref,
    pick_ref,
    take_ref,
    held_ref,
    done,
):
    copy = pltpu.make_async_copy(records_ref, held_ref, done)
    copy.start()
    rows = lists_ref.shape[1]
    kept = take_ref.shape[1]
    refs = refs_ref.shape[1]
    me = lax.axis_index("chan")
    odd = lax.rem(lax.axis_index("lag"), 2)
    near, far = 1 + odd, 2 - odd
    line = lax.broadcasted_iota(jnp.int32, (rows, 2 * rows), 0)

    def pool(owner):
        lists = [lists_ref[pl.ds(lax.bitwise_xor(owner, i), 1), :] for i in (0, near)]
        return jnp.concatenate(lists, axis=1)

    def where(owner, block):
        return pool(owner) == line + block * rows

    def ranks(found):
        present = jnp.max(found.astype(jnp.float32), axis=1, keepdims=True)
        return present, counts_before(jnp.broadcast_to(present, (rows, rows)))

    other = lax.bitwise_xor(me, far)
    found = where(me, other)
    _, rank = ranks(found)
    rank = jnp.concatenate([rank, rank], axis=1)
    slot = jnp.sum(jnp.where(found, rank + 1.0, 0.0), axis=0, keepdims=True).astype(jnp.int32)
    send = jnp.concatenate([line[:kept] + 1 == slot, columns(refs_ref, 2 * rows) == pool(me)], axis=0)
    send = send.astype(jnp.bfloat16)
    keep = where(me, me).astype(jnp.bfloat16)
    picks = jnp.concatenate([send, keep], axis=0)
    own, arrived = picks[:, :rows], picks[:, rows:]
    pick_ref[...] = jnp.concatenate([own, own, arrived, arrived], axis=1)
    present, rank = ranks(where(other, me))
    lane = lax.broadcasted_iota(jnp.int32, (rows, kept), 1)
    slot = jnp.where(present > 0.0, rank[:, :kept], -1.0).astype(jnp.int32)
    take_ref[...] = (lane == slot).astype(jnp.bfloat16)
    copy.wait()
    parts_ref[...] = jnp.concatenate(halves(held_ref[:, 0, :]), axis=0)


def pick_kernel(arrived_ref, pick_ref, parts_ref, sent_ref, base_ref):
    parts = jnp.concatenate([parts_ref[...], *halves(arrived_ref[:, 0, :])], axis=0)
    rows = product(pick_ref[...], parts)
    lines = sent_ref.shape[0]
    sent_ref[...] = rows[:lines]
    base_ref[...] = rows[lines:]


def put(series, panel, out_refs):
    segments = len(out_refs)
    kept = series.shape[0] // segments
    own = lax.axis_index("seg")
    for part in range(segments):
        half = lax.bitwise_xor(own, part)
        chosen = series[:kept]
        for other in range(1, segments):
            chosen = jnp.where(half == other, series[other * kept : (other + 1) * kept], chosen)
        out_refs[part][:kept, :] = chosen
        out_refs[part][kept:, :] = panel


def place_four_kernel(base_ref, take_ref, sent_ref, arrived_ref, *out_refs):
    kept = take_ref.shape[1]
    series = base_ref[...] + choice(take_ref[...], arrived_ref[:kept, :])
    put(series, sent_ref[kept:, :] + arrived_ref[kept:, :], out_refs)


def pack_kernel(records_ref, lists_ref, refs_ref, out_ref, panel_ref):
    rows = records_ref.shape[0]
    refs = refs_ref.shape[1]
    own = jnp.broadcast_to(lists_ref[pl.ds(lax.axis_index("chan"), 1), :], (rows, rows))
    rank = jnp.sum((own.T < own).astype(jnp.int32), axis=0, keepdims=True)
    line = lax.broadcasted_iota(jnp.int32, (rows, rows), 0)
    records = records_ref[:, 0, :]
    panel_ref[...] = choice((columns(refs_ref, rows) == own[:refs]).astype(jnp.bfloat16), records)
    out_ref[...] = choice((line == rank).astype(jnp.bfloat16), records)


def choose_kernel(peers, lists_ref, pick_ref):
    rows = lists_ref.shape[1]
    share = rows // peers
    lane = lax.broadcasted_iota(jnp.int32, (rows, rows), 1)
    channel = lax.broadcasted_iota(jnp.int32, (rows, rows), 0) + lax.axis_index("chan") * rows
    owner = jnp.zeros((rows, 1), jnp.int32)
    for peer in range(peers):
        found = (lists_ref[pl.ds(peer, 1), :] == channel).astype(jnp.int32)
        owner = owner + jnp.sum(found, axis=1, keepdims=True) * peer
    same = lane == owner
    before = counts_before(same.astype(jnp.float32))
    rank = jnp.sum(jnp.where(same, before, 0.0), axis=1, keepdims=True).astype(jnp.int32)
    pick_ref[...] = (lane == owner * share + rank).astype(jnp.bfloat16)


def place_kernel(pick_ref, panel_ref, arrived_ref, *out_refs):
    put(choice(pick_ref[...], arrived_ref[...]), panel_ref[...], out_refs)


def corr_kernel(refs, lag_width, *rest):
    *chunk_refs, out_ref, joined_ref, total_ref, done = rest
    kept = total_ref.shape[0]
    lags, segments = lax.axis_size("lag"), lax.axis_size("seg")
    width = chunk_refs[0].shape[1]
    for (lag_step, segment_step), chunk_ref in zip(steps(lags, segments), chunk_refs):
        lag = lax.bitwise_xor(lax.axis_index("lag"), lag_step)
        segment = lax.bitwise_xor(lax.axis_index("seg"), segment_step)
        start = pl.multiple_of((segment * lags + lag) * width, width)
        joined_ref[:, pl.ds(start, width)] = chunk_ref[...]
    series = joined_ref[:kept, :]
    panel = joined_ref[kept:, :]
    samples = panel.shape[1]
    terms = SAMPLES - LAGS
    times = lax.broadcasted_iota(jnp.int32, panel.shape, 1)
    panel = jnp.where(times < terms, panel, 0.0)
    series = pltpu.roll(series, samples - lax.axis_index("lag") * lag_width, 1)
    scale = 1.0 / math.sqrt(terms)
    columns = PHASES * refs
    each = lag_width // PHASES // GROUPS

    def shifted(value, shifts):
        parts = [pltpu.roll(value, shift % samples, 1) if shift else value for shift in shifts]
        return jnp.concatenate(parts, axis=0)

    panel_high, panel_low = (shifted(half, range(PHASES)) for half in halves(panel))
    series_high, series_low = halves(series)
    copies = []
    for group in range(GROUPS):
        shifts = [-PHASES * (group * each + i) for i in range(each)]
        high, low = shifted(series_high, shifts), shifted(series_low, shifts)
        lines = each * kept
        total = product_nt(jnp.concatenate([high, low], axis=0), panel_high)
        total = (total[:lines] + total[lines:] + product_nt(high, panel_low)) * scale
        for i in range(each):
            start = (group * each + i) * columns
            total_ref[:, start : start + columns] = total[i * kept : (i + 1) * kept]
        part = pl.ds(group * each * columns, each * columns)
        copies.append(pltpu.make_async_copy(total_ref.at[:, part], out_ref.at[:, part], done.at[group]))
        copies[-1].start()
    for copy in copies:
        copy.wait()


def shards(records_owned, section_list, ref_index):
    peers = lax.axis_size("chan")
    segments = lax.axis_size("seg")
    rows, _, samples = records_owned.shape
    refs = ref_index.shape[0]
    share = rows // peers
    kept = rows // segments
    lags = lax.axis_size("lag")
    lag_width = LAGS // lags
    lists = section_list.reshape(peers, rows)
    params = pltpu.CompilerParams(vmem_limit_bytes=48 * 1024 * 1024)
    wanted = ref_index.reshape(1, refs)

    def block(*shape, dtype=jnp.float32):
        return jax.ShapeDtypeStruct(shape, dtype)

    def call(kernel, name, shapes, *operands):
        return pl.pallas_call(kernel, out_shape=shapes, compiler_params=params, name=name)(*operands)

    shapes = [block(kept + refs, samples)] * segments
    if peers == 4:
        first = paired(records_owned, (1, 2))
        half = rows // 2
        whole = pl.BlockSpec(memory_space=pltpu.VMEM)
        parts, pick, take = pl.pallas_call(
            choose_four_kernel,
            out_shape=[
                block(2 * rows, samples, dtype=jnp.bfloat16),
                block(half + refs + rows, 4 * rows, dtype=jnp.bfloat16),
                block(rows, half, dtype=jnp.bfloat16),
            ],
            in_specs=[pl.BlockSpec(memory_space=pl.ANY), whole, whole],
            scratch_shapes=[pltpu.VMEM(records_owned.shape, jnp.float32), pltpu.SemaphoreType.DMA],
            compiler_params=params,
            name="choose",
        )(pltpu.with_memory_space_constraint(records_owned, pltpu.HBM), lists, wanted)
        results = [block(half + refs, samples), block(rows, samples)]
        sent, base = call(pick_kernel, "pick", results, first, pick, parts)
        placed = call(place_four_kernel, "place", shapes, base, take, sent, paired(sent, (2, 1)))
    else:
        packed, panel = call(
            pack_kernel,
            "pack",
            [block(rows, samples), block(refs, samples)],
            records_owned,
            lists,
            wanted,
        )
        blocks = packed.reshape(peers, share, samples)
        blocks = lax.all_to_all(blocks, "chan", split_axis=0, concat_axis=0, tiled=True)
        step = 1
        while step < peers:
            panel = panel + across(panel, step)
            step *= 2
        pick = call(
            functools.partial(choose_kernel, peers),
            "choose",
            block(rows, rows, dtype=jnp.bfloat16),
            lists,
        )
        placed = call(place_kernel, "place", shapes, pick, panel, blocks.reshape(rows, samples))
    held = {(0, 0): placed[0]}
    for lag_step in range(0, lags, 2):
        for segment_step in range(segments):
            if lag_step or segment_step:
                held[lag_step, segment_step] = swapped(placed[segment_step], lag_step, segment_step)
    for lag_step, segment_step in list(held):
        held[lag_step + 1, segment_step] = swapped(held[lag_step, segment_step], 1, 0)
    return pl.pallas_call(
        functools.partial(corr_kernel, refs, lag_width),
        out_shape=jax.ShapeDtypeStruct((kept, lag_width * refs), jnp.float32),
        out_specs=pl.BlockSpec(memory_space=pl.ANY),
        scratch_shapes=[
            pltpu.VMEM((kept + refs, lags * segments * samples), jnp.float32),
            pltpu.VMEM((kept, lag_width * refs), jnp.float32),
            pltpu.SemaphoreType.DMA((GROUPS,)),
        ],
        compiler_params=params,
        name="correlate",
    )(*[held[step] for step in steps(lags, segments)])


def solution(mesh):
    return jax.shard_map(
        shards,
        mesh=mesh,
        in_specs=(P("chan", "seg", "lag"), P(), P()),
        out_specs=P(("chan", "seg"), "lag"),
        check_vma=False,
    )
```

```python
import functools
import math

import jax
import jax.numpy as jnp
from jax import lax
from jax.experimental import pallas as pl
from jax.experimental.pallas import tpu as pltpu
from jax.sharding import PartitionSpec as P

LAGS = 128
SAMPLES = 2048
PHASES = 4
GROUPS = 2


def halves(value):
    high = value.astype(jnp.bfloat16)
    low = (value - high.astype(jnp.float32)).astype(jnp.bfloat16)
    return high, low


def product(left, right):
    return jnp.dot(left, right, preferred_element_type=jnp.float32)


def product_nt(left, right):
    return lax.dot_general(
        left, right, (((1,), (1,)), ((), ())), preferred_element_type=jnp.float32
    )


def steps(lags, segments):
    return [(lag, segment) for lag in range(lags) for segment in range(segments)]


def swapped(value, lag_step, segment_step):
    lags, segments = lax.axis_size("lag"), lax.axis_size("seg")
    pairs = [
        (lag * segments + segment, (lag ^ lag_step) * segments + (segment ^ segment_step))
        for lag, segment in steps(lags, segments)
    ]
    return lax.ppermute(value, ("lag", "seg"), pairs)


def across(value, step):
    return lax.ppermute(value, "chan", [(i, i ^ step) for i in range(lax.axis_size("chan"))])


def paired(value, order):
    lags = lax.axis_size("lag")
    pairs = [
        (chan * lags + lag, (chan ^ order[lag % 2]) * lags + lag)
        for chan in range(lax.axis_size("chan"))
        for lag in range(lags)
    ]
    return lax.ppermute(value, ("chan", "lag"), pairs)


def choice(pick, rows):
    high, low = halves(rows)
    return product(pick, high) + product(pick, low)


def counts_before(present):
    rows = present.shape[0]
    line = lax.broadcasted_iota(jnp.int32, (rows, rows), 0)
    lane = lax.broadcasted_iota(jnp.int32, (rows, rows), 1)
    return product((lane < line).astype(jnp.bfloat16), present.astype(jnp.bfloat16))


def columns(refs_ref, width):
    return jnp.broadcast_to(refs_ref[...], (width, refs_ref.shape[1])).T


def choose_four_kernel(
    records_ref,
    lists_ref,
    refs_ref,
    parts_ref,
    pick_ref,
    take_ref,
    held_ref,
    done,
):
    copy = pltpu.make_async_copy(records_ref, held_ref, done)
    copy.start()
    rows = lists_ref.shape[1]
    kept = take_ref.shape[1]
    refs = refs_ref.shape[1]
    me = lax.axis_index("chan")
    odd = lax.rem(lax.axis_index("lag"), 2)
    near, far = 1 + odd, 2 - odd
    line = lax.broadcasted_iota(jnp.int32, (rows, 2 * rows), 0)

    def pool(owner):
        lists = [lists_ref[pl.ds(lax.bitwise_xor(owner, i), 1), :] for i in (0, near)]
        return jnp.concatenate(lists, axis=1)

    def where(owner, block):
        return pool(owner) == line + block * rows

    def ranks(found):
        present = jnp.max(found.astype(jnp.float32), axis=1, keepdims=True)
        return present, counts_before(jnp.broadcast_to(present, (rows, rows)))

    other = lax.bitwise_xor(me, far)
    found = where(me, other)
    _, rank = ranks(found)
    rank = jnp.concatenate([rank, rank], axis=1)
    slot = jnp.sum(jnp.where(found, rank + 1.0, 0.0), axis=0, keepdims=True).astype(jnp.int32)
    send = jnp.concatenate([line[:kept] + 1 == slot, columns(refs_ref, 2 * rows) == pool(me)], axis=0)
    send = send.astype(jnp.bfloat16)
    keep = where(me, me).astype(jnp.bfloat16)
    picks = jnp.concatenate([send, keep], axis=0)
    own, arrived = picks[:, :rows], picks[:, rows:]
    pick_ref[...] = jnp.concatenate([own, own, arrived, arrived], axis=1)
    present, rank = ranks(where(other, me))
    lane = lax.broadcasted_iota(jnp.int32, (rows, kept), 1)
    slot = jnp.where(present > 0.0, rank[:, :kept], -1.0).astype(jnp.int32)
    take_ref[...] = (lane == slot).astype(jnp.bfloat16)
    copy.wait()
    parts_ref[...] = jnp.concatenate(halves(held_ref[:, 0, :]), axis=0)


def pick_kernel(arrived_ref, pick_ref, parts_ref, sent_ref, panel_ref, base_ref):
    parts = jnp.concatenate([parts_ref[...], *halves(arrived_ref[:, 0, :])], axis=0)
    rows = product(pick_ref[...], parts)
    lines = sent_ref.shape[0]
    upto = lines + panel_ref.shape[0]
    sent_ref[...] = rows[:lines]
    panel_ref[...] = rows[lines:upto]
    base_ref[...] = rows[upto:]


def put(series, panel, out_refs):
    segments = len(out_refs)
    kept = series.shape[0] // segments
    own = lax.axis_index("seg")
    for part in range(segments):
        half = lax.bitwise_xor(own, part)
        chosen = series[:kept]
        for other in range(1, segments):
            chosen = jnp.where(half == other, series[other * kept : (other + 1) * kept], chosen)
        out_refs[part][:kept, :] = chosen
        out_refs[part][kept:, :] = panel


def place_four_kernel(base_ref, take_ref, arrived_ref, panel_ref, arrived_panel_ref, *out_refs):
    series = base_ref[...] + choice(take_ref[...], arrived_ref[...])
    put(series, panel_ref[...] + arrived_panel_ref[...], out_refs)


def pack_kernel(records_ref, lists_ref, refs_ref, out_ref, panel_ref):
    rows = records_ref.shape[0]
    refs = refs_ref.shape[1]
    own = jnp.broadcast_to(lists_ref[pl.ds(lax.axis_index("chan"), 1), :], (rows, rows))
    rank = jnp.sum((own.T < own).astype(jnp.int32), axis=0, keepdims=True)
    line = lax.broadcasted_iota(jnp.int32, (rows, rows), 0)
    records = records_ref[:, 0, :]
    panel_ref[...] = choice((columns(refs_ref, rows) == own[:refs]).astype(jnp.bfloat16), records)
    out_ref[...] = choice((line == rank).astype(jnp.bfloat16), records)


def choose_kernel(peers, lists_ref, pick_ref):
    rows = lists_ref.shape[1]
    share = rows // peers
    lane = lax.broadcasted_iota(jnp.int32, (rows, rows), 1)
    channel = lax.broadcasted_iota(jnp.int32, (rows, rows), 0) + lax.axis_index("chan") * rows
    owner = jnp.zeros((rows, 1), jnp.int32)
    for peer in range(peers):
        found = (lists_ref[pl.ds(peer, 1), :] == channel).astype(jnp.int32)
        owner = owner + jnp.sum(found, axis=1, keepdims=True) * peer
    same = lane == owner
    before = counts_before(same.astype(jnp.float32))
    rank = jnp.sum(jnp.where(same, before, 0.0), axis=1, keepdims=True).astype(jnp.int32)
    pick_ref[...] = (lane == owner * share + rank).astype(jnp.bfloat16)


def place_kernel(pick_ref, panel_ref, arrived_ref, *out_refs):
    put(choice(pick_ref[...], arrived_ref[...]), panel_ref[...], out_refs)


def corr_kernel(refs, lag_width, *rest):
    *chunk_refs, out_ref, joined_ref, total_ref, done = rest
    kept = total_ref.shape[0]
    lags, segments = lax.axis_size("lag"), lax.axis_size("seg")
    width = chunk_refs[0].shape[1]
    for (lag_step, segment_step), chunk_ref in zip(steps(lags, segments), chunk_refs):
        lag = lax.bitwise_xor(lax.axis_index("lag"), lag_step)
        segment = lax.bitwise_xor(lax.axis_index("seg"), segment_step)
        start = pl.multiple_of((segment * lags + lag) * width, width)
        joined_ref[:, pl.ds(start, width)] = chunk_ref[...]
    series = joined_ref[:kept, :]
    panel = joined_ref[kept:, :]
    samples = panel.shape[1]
    terms = SAMPLES - LAGS
    times = lax.broadcasted_iota(jnp.int32, panel.shape, 1)
    panel = jnp.where(times < terms, panel, 0.0)
    series = pltpu.roll(series, samples - lax.axis_index("lag") * lag_width, 1)
    scale = 1.0 / math.sqrt(terms)
    columns = PHASES * refs
    each = lag_width // PHASES // GROUPS

    def shifted(value, shifts):
        parts = [pltpu.roll(value, shift % samples, 1) if shift else value for shift in shifts]
        return jnp.concatenate(parts, axis=0)

    panel_high, panel_low = (shifted(half, range(PHASES)) for half in halves(panel))
    series_high, series_low = halves(series)
    copies = []
    for group in range(GROUPS):
        shifts = [-PHASES * (group * each + i) for i in range(each)]
        high, low = shifted(series_high, shifts), shifted(series_low, shifts)
        lines = each * kept
        total = product_nt(jnp.concatenate([high, low], axis=0), panel_high)
        total = (total[:lines] + total[lines:] + product_nt(high, panel_low)) * scale
        for i in range(each):
            start = (group * each + i) * columns
            total_ref[:, start : start + columns] = total[i * kept : (i + 1) * kept]
        part = pl.ds(group * each * columns, each * columns)
        copies.append(pltpu.make_async_copy(total_ref.at[:, part], out_ref.at[:, part], done.at[group]))
        copies[-1].start()
    for copy in copies:
        copy.wait()


def shards(records_owned, section_list, ref_index):
    peers = lax.axis_size("chan")
    segments = lax.axis_size("seg")
    rows, _, samples = records_owned.shape
    refs = ref_index.shape[0]
    share = rows // peers
    kept = rows // segments
    lags = lax.axis_size("lag")
    lag_width = LAGS // lags
    lists = section_list.reshape(peers, rows)
    params = pltpu.CompilerParams(vmem_limit_bytes=48 * 1024 * 1024)
    wanted = ref_index.reshape(1, refs)

    def block(*shape, dtype=jnp.float32):
        return jax.ShapeDtypeStruct(shape, dtype)

    def call(kernel, name, shapes, *operands):
        return pl.pallas_call(kernel, out_shape=shapes, compiler_params=params, name=name)(*operands)

    shapes = [block(kept + refs, samples)] * segments
    if peers == 4:
        first = paired(records_owned, (1, 2))
        half = rows // 2
        whole = pl.BlockSpec(memory_space=pltpu.VMEM)
        parts, pick, take = pl.pallas_call(
            choose_four_kernel,
            out_shape=[
                block(2 * rows, samples, dtype=jnp.bfloat16),
                block(half + refs + rows, 4 * rows, dtype=jnp.bfloat16),
                block(rows, half, dtype=jnp.bfloat16),
            ],
            in_specs=[pl.BlockSpec(memory_space=pl.ANY), whole, whole],
            scratch_shapes=[pltpu.VMEM(records_owned.shape, jnp.float32), pltpu.SemaphoreType.DMA],
            compiler_params=params,
            name="choose",
        )(pltpu.with_memory_space_constraint(records_owned, pltpu.HBM), lists, wanted)
        results = [block(half, samples), block(refs, samples), block(rows, samples)]
        sent, panel, base = call(pick_kernel, "pick", results, first, pick, parts)
        second, panel_second = paired(sent, (2, 1)), paired(panel, (2, 1))
        placed = call(
            place_four_kernel, "place", shapes, base, take, second, panel, panel_second
        )
    else:
        packed, panel = call(
            pack_kernel,
            "pack",
            [block(rows, samples), block(refs, samples)],
            records_owned,
            lists,
            wanted,
        )
        blocks = packed.reshape(peers, share, samples)
        blocks = lax.all_to_all(blocks, "chan", split_axis=0, concat_axis=0, tiled=True)
        step = 1
        while step < peers:
            panel = panel + across(panel, step)
            step *= 2
        pick = call(
            functools.partial(choose_kernel, peers),
            "choose",
            block(rows, rows, dtype=jnp.bfloat16),
            lists,
        )
        placed = call(place_kernel, "place", shapes, pick, panel, blocks.reshape(rows, samples))
    held = {(0, 0): placed[0]}
    for lag_step in range(0, lags, 2):
        for segment_step in range(segments):
            if lag_step or segment_step:
                held[lag_step, segment_step] = swapped(placed[segment_step], lag_step, segment_step)
    for lag_step, segment_step in list(held):
        held[lag_step + 1, segment_step] = swapped(held[lag_step, segment_step], 1, 0)
    return pl.pallas_call(
        functools.partial(corr_kernel, refs, lag_width),
        out_shape=jax.ShapeDtypeStruct((kept, lag_width * refs), jnp.float32),
        out_specs=pl.BlockSpec(memory_space=pl.ANY),
        scratch_shapes=[
            pltpu.VMEM((kept + refs, lags * segments * samples), jnp.float32),
            pltpu.VMEM((kept, lag_width * refs), jnp.float32),
            pltpu.SemaphoreType.DMA((GROUPS,)),
        ],
        compiler_params=params,
        name="correlate",
    )(*[held[step] for step in steps(lags, segments)])


def solution(mesh):
    return jax.shard_map(
        shards,
        mesh=mesh,
        in_specs=(P("chan", "seg", "lag"), P(), P()),
        out_specs=P(("chan", "seg"), "lag"),
        check_vma=False,
    )
```

```python
import functools
import math

import jax
import jax.numpy as jnp
from jax import lax
from jax.experimental import pallas as pl
from jax.experimental.pallas import tpu as pltpu
from jax.sharding import PartitionSpec as P

LAGS = 128
SAMPLES = 2048
PHASES = 4
PARTS = 2
MARGIN = 128


def halves(value):
    high = value.astype(jnp.bfloat16)
    low = (value - high.astype(jnp.float32)).astype(jnp.bfloat16)
    return high, low


def product(left, right):
    return jnp.dot(left, right, preferred_element_type=jnp.float32)


def product_nt(left, right):
    return lax.dot_general(
        left, right, (((1,), (1,)), ((), ())), preferred_element_type=jnp.float32
    )


def steps(lags, segments):
    return [(lag, segment) for lag in range(lags) for segment in range(segments)]


def swapped(value, lag_step, segment_step):
    lags, segments = lax.axis_size("lag"), lax.axis_size("seg")
    pairs = [
        (lag * segments + segment, (lag ^ lag_step) * segments + (segment ^ segment_step))
        for lag, segment in steps(lags, segments)
    ]
    return lax.ppermute(value, ("lag", "seg"), pairs)


def across(value, step):
    return lax.ppermute(value, "chan", [(i, i ^ step) for i in range(lax.axis_size("chan"))])


def paired(value, order):
    lags = lax.axis_size("lag")
    pairs = [
        (chan * lags + lag, (chan ^ order[lag % 2]) * lags + lag)
        for chan in range(lax.axis_size("chan"))
        for lag in range(lags)
    ]
    return lax.ppermute(value, ("chan", "lag"), pairs)


def choice(pick, rows):
    high, low = halves(rows)
    return product(pick, high) + product(pick, low)


def counts_before(present):
    rows = present.shape[0]
    line = lax.broadcasted_iota(jnp.int32, (rows, rows), 0)
    lane = lax.broadcasted_iota(jnp.int32, (rows, rows), 1)
    return product((lane < line).astype(jnp.bfloat16), present.astype(jnp.bfloat16))


def columns(refs_ref, width):
    return jnp.broadcast_to(refs_ref[...], (width, refs_ref.shape[1])).T


def choose_four_kernel(
    records_ref,
    lists_ref,
    refs_ref,
    own_ref,
    send_ref,
    keep_ref,
    take_ref,
    held_ref,
    done,
):
    copy = pltpu.make_async_copy(records_ref, held_ref, done)
    copy.start()
    rows = lists_ref.shape[1]
    kept = take_ref.shape[1]
    refs = refs_ref.shape[1]
    me = lax.axis_index("chan")
    odd = lax.rem(lax.axis_index("lag"), 2)
    near, far = 1 + odd, 2 - odd
    line = lax.broadcasted_iota(jnp.int32, (rows, 2 * rows), 0)

    def pool(owner):
        lists = [lists_ref[pl.ds(lax.bitwise_xor(owner, i), 1), :] for i in (0, near)]
        return jnp.concatenate(lists, axis=1)

    def where(owner, block):
        return pool(owner) == line + block * rows

    def ranks(found):
        present = jnp.max(found.astype(jnp.float32), axis=1, keepdims=True)
        return present, counts_before(jnp.broadcast_to(present, (rows, rows)))

    other = lax.bitwise_xor(me, far)
    found = where(me, other)
    _, rank = ranks(found)
    rank = jnp.concatenate([rank, rank], axis=1)
    slot = jnp.sum(jnp.where(found, rank + 1.0, 0.0), axis=0, keepdims=True).astype(jnp.int32)
    send = jnp.concatenate([line[:kept] + 1 == slot, columns(refs_ref, 2 * rows) == pool(me)], axis=0)
    send = send.astype(jnp.bfloat16)
    keep = where(me, me).astype(jnp.bfloat16)
    send_ref[...] = send
    keep_ref[...] = keep
    present, rank = ranks(where(other, me))
    lane = lax.broadcasted_iota(jnp.int32, (rows, kept), 1)
    slot = jnp.where(present > 0.0, rank[:, :kept], -1.0).astype(jnp.int32)
    take_ref[...] = (lane == slot).astype(jnp.bfloat16)
    copy.wait()
    own_ref[...] = held_ref[:, 0, :]


def pick_kernel(own_ref, arrived_ref, send_ref, keep_ref, sent_ref, base_ref):
    rows = jnp.concatenate([own_ref[...], arrived_ref[:, 0, :]], axis=0)
    high, low = halves(rows)
    sent_ref[...] = product(send_ref[...], high) + product(send_ref[...], low)
    base_ref[...] = product(keep_ref[...], high) + product(keep_ref[...], low)


def put(series, panel, out_refs):
    segments = len(out_refs)
    kept = series.shape[0] // segments
    own = lax.axis_index("seg")
    for part in range(segments):
        half = lax.bitwise_xor(own, part)
        chosen = series[:kept]
        for other in range(1, segments):
            chosen = jnp.where(half == other, series[other * kept : (other + 1) * kept], chosen)
        out_refs[part][:kept, :] = chosen
        out_refs[part][kept:, :] = panel


def place_four_kernel(base_ref, take_ref, sent_ref, arrived_ref, *out_refs):
    kept = take_ref.shape[1]
    series = base_ref[...] + choice(take_ref[...], arrived_ref[:kept, :])
    put(series, sent_ref[kept:, :] + arrived_ref[kept:, :], out_refs)


def pack_kernel(records_ref, lists_ref, refs_ref, out_ref, panel_ref):
    rows = records_ref.shape[0]
    refs = refs_ref.shape[1]
    own = jnp.broadcast_to(lists_ref[pl.ds(lax.axis_index("chan"), 1), :], (rows, rows))
    rank = jnp.sum((own.T < own).astype(jnp.int32), axis=0, keepdims=True)
    line = lax.broadcasted_iota(jnp.int32, (rows, rows), 0)
    records = records_ref[:, 0, :]
    panel_ref[...] = choice((columns(refs_ref, rows) == own[:refs]).astype(jnp.bfloat16), records)
    out_ref[...] = choice((line == rank).astype(jnp.bfloat16), records)


def choose_kernel(peers, lists_ref, pick_ref):
    rows = lists_ref.shape[1]
    share = rows // peers
    lane = lax.broadcasted_iota(jnp.int32, (rows, rows), 1)
    channel = lax.broadcasted_iota(jnp.int32, (rows, rows), 0) + lax.axis_index("chan") * rows
    owner = jnp.zeros((rows, 1), jnp.int32)
    for peer in range(peers):
        found = (lists_ref[pl.ds(peer, 1), :] == channel).astype(jnp.int32)
        owner = owner + jnp.sum(found, axis=1, keepdims=True) * peer
    same = lane == owner
    before = counts_before(same.astype(jnp.float32))
    rank = jnp.sum(jnp.where(same, before, 0.0), axis=1, keepdims=True).astype(jnp.int32)
    pick_ref[...] = (lane == owner * share + rank).astype(jnp.bfloat16)


def place_kernel(pick_ref, panel_ref, arrived_ref, *out_refs):
    put(choice(pick_ref[...], arrived_ref[...]), panel_ref[...], out_refs)


def corr_kernel(refs, lag_width, *rest):
    *chunk_refs, out_ref, joined_ref, total_ref = rest
    kept = out_ref.shape[0]
    lags, segments = lax.axis_size("lag"), lax.axis_size("seg")
    width = chunk_refs[0].shape[1]
    for (lag_step, segment_step), chunk_ref in zip(steps(lags, segments), chunk_refs):
        lag = lax.bitwise_xor(lax.axis_index("lag"), lag_step)
        segment = lax.bitwise_xor(lax.axis_index("seg"), segment_step)
        start = pl.multiple_of((segment * lags + lag) * width, width)
        joined_ref[:, pl.ds(start, width)] = chunk_ref[...]
    series = joined_ref[:kept, :]
    panel = joined_ref[kept:, :]
    samples = panel.shape[1]
    terms = SAMPLES - LAGS
    times = lax.broadcasted_iota(jnp.int32, panel.shape, 1)
    panel = jnp.where(times < terms, panel, 0.0)
    series = pltpu.roll(series, samples - lax.axis_index("lag") * lag_width, 1)
    groups = lag_width // PHASES
    length = samples // PARTS

    def shifted(value, shifts, first):
        size = value.shape[1]
        parts = [pltpu.roll(value, shift % size, 1) if shift else value for shift in shifts]
        return jnp.concatenate([part[:, first : first + length] for part in parts], axis=0)

    panel = jnp.concatenate([jnp.zeros((refs, MARGIN), jnp.float32), panel], axis=1)
    series = jnp.concatenate([series, series[:, :MARGIN]], axis=1)
    panel_parts, series_parts = halves(panel), halves(series)
    lines = groups * kept
    for part in range(PARTS):
        window = slice(part * length, (part + 1) * length + MARGIN)
        panel_high, panel_low = (
            shifted(half[:, window], range(PHASES), MARGIN) for half in panel_parts
        )
        high, low = (
            shifted(half[:, window], range(0, -lag_width, -PHASES), 0) for half in series_parts
        )
        total = product_nt(jnp.concatenate([high, low], axis=0), panel_high)
        total = total[:lines] + total[lines:] + product_nt(high, panel_low)
        total_ref[part] = total
    scale = 1.0 / math.sqrt(terms)
    columns = PHASES * refs
    for group in range(groups):
        place = slice(group * kept, (group + 1) * kept)
        total = total_ref[0, place, :]
        for part in range(1, PARTS):
            total = total + total_ref[part, place, :]
        out_ref[:, group * columns : (group + 1) * columns] = total * scale


def shards(records_owned, section_list, ref_index):
    peers = lax.axis_size("chan")
    segments = lax.axis_size("seg")
    rows, _, samples = records_owned.shape
    refs = ref_index.shape[0]
    share = rows // peers
    kept = rows // segments
    lags = lax.axis_size("lag")
    lag_width = LAGS // lags
    lists = section_list.reshape(peers, rows)
    params = pltpu.CompilerParams(vmem_limit_bytes=48 * 1024 * 1024)
    wanted = ref_index.reshape(1, refs)

    def block(*shape, dtype=jnp.float32):
        return jax.ShapeDtypeStruct(shape, dtype)

    def call(kernel, name, shapes, *operands):
        return pl.pallas_call(kernel, out_shape=shapes, compiler_params=params, name=name)(*operands)

    shapes = [block(kept + refs, samples)] * segments
    if peers == 4:
        first = paired(records_owned, (1, 2))
        half = rows // 2
        whole = pl.BlockSpec(memory_space=pltpu.VMEM)
        own, send, keep, take = pl.pallas_call(
            choose_four_kernel,
            out_shape=[
                block(rows, samples),
                block(half + refs, 2 * rows, dtype=jnp.bfloat16),
                block(rows, 2 * rows, dtype=jnp.bfloat16),
                block(rows, half, dtype=jnp.bfloat16),
            ],
            in_specs=[pl.BlockSpec(memory_space=pl.ANY), whole, whole],
            scratch_shapes=[pltpu.VMEM(records_owned.shape, jnp.float32), pltpu.SemaphoreType.DMA],
            compiler_params=params,
            name="choose",
        )(pltpu.with_memory_space_constraint(records_owned, pltpu.HBM), lists, wanted)
        results = [block(half + refs, samples), block(rows, samples)]
        sent, base = call(pick_kernel, "pick", results, own, first, send, keep)
        placed = call(place_four_kernel, "place", shapes, base, take, sent, paired(sent, (2, 1)))
    else:
        packed, panel = call(
            pack_kernel,
            "pack",
            [block(rows, samples), block(refs, samples)],
            records_owned,
            lists,
            wanted,
        )
        blocks = packed.reshape(peers, share, samples)
        blocks = lax.all_to_all(blocks, "chan", split_axis=0, concat_axis=0, tiled=True)
        step = 1
        while step < peers:
            panel = panel + across(panel, step)
            step *= 2
        pick = call(
            functools.partial(choose_kernel, peers),
            "choose",
            block(rows, rows, dtype=jnp.bfloat16),
            lists,
        )
        placed = call(place_kernel, "place", shapes, pick, panel, blocks.reshape(rows, samples))
    held = {(0, 0): placed[0]}
    for lag_step in range(0, lags, 2):
        for segment_step in range(segments):
            if lag_step or segment_step:
                held[lag_step, segment_step] = swapped(placed[segment_step], lag_step, segment_step)
    for lag_step, segment_step in list(held):
        held[lag_step + 1, segment_step] = swapped(held[lag_step, segment_step], 1, 0)
    return pl.pallas_call(
        functools.partial(corr_kernel, refs, lag_width),
        out_shape=jax.ShapeDtypeStruct((kept, lag_width * refs), jnp.float32),
        scratch_shapes=[
            pltpu.VMEM((kept + refs, lags * segments * samples), jnp.float32),
            pltpu.VMEM((PARTS, lag_width // PHASES * kept, PHASES * refs), jnp.float32),
        ],
        compiler_params=params,
        name="correlate",
    )(*[held[step] for step in steps(lags, segments)])


def solution(mesh):
    return jax.shard_map(
        shards,
        mesh=mesh,
        in_specs=(P("chan", "seg", "lag"), P(), P()),
        out_specs=P(("chan", "seg"), "lag"),
        check_vma=False,
    )
```

```python
import functools
import math

import jax
import jax.numpy as jnp
from jax import lax
from jax.experimental import pallas as pl
from jax.experimental.pallas import tpu as pltpu
from jax.sharding import PartitionSpec as P

LAGS = 128
SAMPLES = 2048
PHASES = 4
PARTS = 4
MARGIN = 128


def halves(value):
    high = value.astype(jnp.bfloat16)
    low = (value - high.astype(jnp.float32)).astype(jnp.bfloat16)
    return high, low


def product(left, right):
    return jnp.dot(left, right, preferred_element_type=jnp.float32)


def product_nt(left, right):
    return lax.dot_general(
        left, right, (((1,), (1,)), ((), ())), preferred_element_type=jnp.float32
    )


def steps(lags, segments):
    return [(lag, segment) for lag in range(lags) for segment in range(segments)]


def swapped(value, lag_step, segment_step):
    lags, segments = lax.axis_size("lag"), lax.axis_size("seg")
    pairs = [
        (lag * segments + segment, (lag ^ lag_step) * segments + (segment ^ segment_step))
        for lag, segment in steps(lags, segments)
    ]
    return lax.ppermute(value, ("lag", "seg"), pairs)


def across(value, step):
    return lax.ppermute(value, "chan", [(i, i ^ step) for i in range(lax.axis_size("chan"))])


def paired(value, order):
    lags = lax.axis_size("lag")
    pairs = [
        (chan * lags + lag, (chan ^ order[lag % 2]) * lags + lag)
        for chan in range(lax.axis_size("chan"))
        for lag in range(lags)
    ]
    return lax.ppermute(value, ("chan", "lag"), pairs)


def choice(pick, rows):
    high, low = halves(rows)
    return product(pick, high) + product(pick, low)


def counts_before(present):
    rows = present.shape[0]
    line = lax.broadcasted_iota(jnp.int32, (rows, rows), 0)
    lane = lax.broadcasted_iota(jnp.int32, (rows, rows), 1)
    return product((lane < line).astype(jnp.bfloat16), present.astype(jnp.bfloat16))


def columns(refs_ref, width):
    return jnp.broadcast_to(refs_ref[...], (width, refs_ref.shape[1])).T


def choose_four_kernel(
    records_ref,
    lists_ref,
    refs_ref,
    own_ref,
    send_ref,
    keep_ref,
    take_ref,
    held_ref,
    done,
):
    copy = pltpu.make_async_copy(records_ref, held_ref, done)
    copy.start()
    rows = lists_ref.shape[1]
    kept = take_ref.shape[1]
    refs = refs_ref.shape[1]
    me = lax.axis_index("chan")
    odd = lax.rem(lax.axis_index("lag"), 2)
    near, far = 1 + odd, 2 - odd
    line = lax.broadcasted_iota(jnp.int32, (rows, 2 * rows), 0)

    def pool(owner):
        lists = [lists_ref[pl.ds(lax.bitwise_xor(owner, i), 1), :] for i in (0, near)]
        return jnp.concatenate(lists, axis=1)

    def where(owner, block):
        return pool(owner) == line + block * rows

    def ranks(found):
        present = jnp.max(found.astype(jnp.float32), axis=1, keepdims=True)
        return present, counts_before(jnp.broadcast_to(present, (rows, rows)))

    other = lax.bitwise_xor(me, far)
    found = where(me, other)
    _, rank = ranks(found)
    rank = jnp.concatenate([rank, rank], axis=1)
    slot = jnp.sum(jnp.where(found, rank + 1.0, 0.0), axis=0, keepdims=True).astype(jnp.int32)
    send = jnp.concatenate([line[:kept] + 1 == slot, columns(refs_ref, 2 * rows) == pool(me)], axis=0)
    send = send.astype(jnp.bfloat16)
    keep = where(me, me).astype(jnp.bfloat16)
    send_ref[...] = send
    keep_ref[...] = keep
    present, rank = ranks(where(other, me))
    lane = lax.broadcasted_iota(jnp.int32, (rows, kept), 1)
    slot = jnp.where(present > 0.0, rank[:, :kept], -1.0).astype(jnp.int32)
    take_ref[...] = (lane == slot).astype(jnp.bfloat16)
    copy.wait()
    own_ref[...] = held_ref[:, 0, :]


def pick_kernel(own_ref, arrived_ref, send_ref, keep_ref, sent_ref, base_ref):
    rows = jnp.concatenate([own_ref[...], arrived_ref[:, 0, :]], axis=0)
    high, low = halves(rows)
    sent_ref[...] = product(send_ref[...], high) + product(send_ref[...], low)
    base_ref[...] = product(keep_ref[...], high) + product(keep_ref[...], low)


def put(series, panel, out_refs):
    segments = len(out_refs)
    kept = series.shape[0] // segments
    own = lax.axis_index("seg")
    for part in range(segments):
        half = lax.bitwise_xor(own, part)
        chosen = series[:kept]
        for other in range(1, segments):
            chosen = jnp.where(half == other, series[other * kept : (other + 1) * kept], chosen)
        out_refs[part][:kept, :] = chosen
        out_refs[part][kept:, :] = panel


def place_four_kernel(base_ref, take_ref, sent_ref, arrived_ref, *out_refs):
    kept = take_ref.shape[1]
    series = base_ref[...] + choice(take_ref[...], arrived_ref[:kept, :])
    put(series, sent_ref[kept:, :] + arrived_ref[kept:, :], out_refs)


def pack_kernel(records_ref, lists_ref, refs_ref, out_ref, panel_ref):
    rows = records_ref.shape[0]
    refs = refs_ref.shape[1]
    own = jnp.broadcast_to(lists_ref[pl.ds(lax.axis_index("chan"), 1), :], (rows, rows))
    rank = jnp.sum((own.T < own).astype(jnp.int32), axis=0, keepdims=True)
    line = lax.broadcasted_iota(jnp.int32, (rows, rows), 0)
    records = records_ref[:, 0, :]
    panel_ref[...] = choice((columns(refs_ref, rows) == own[:refs]).astype(jnp.bfloat16), records)
    out_ref[...] = choice((line == rank).astype(jnp.bfloat16), records)


def choose_kernel(peers, lists_ref, pick_ref):
    rows = lists_ref.shape[1]
    share = rows // peers
    lane = lax.broadcasted_iota(jnp.int32, (rows, rows), 1)
    channel = lax.broadcasted_iota(jnp.int32, (rows, rows), 0) + lax.axis_index("chan") * rows
    owner = jnp.zeros((rows, 1), jnp.int32)
    for peer in range(peers):
        found = (lists_ref[pl.ds(peer, 1), :] == channel).astype(jnp.int32)
        owner = owner + jnp.sum(found, axis=1, keepdims=True) * peer
    same = lane == owner
    before = counts_before(same.astype(jnp.float32))
    rank = jnp.sum(jnp.where(same, before, 0.0), axis=1, keepdims=True).astype(jnp.int32)
    pick_ref[...] = (lane == owner * share + rank).astype(jnp.bfloat16)


def place_kernel(pick_ref, panel_ref, arrived_ref, *out_refs):
    put(choice(pick_ref[...], arrived_ref[...]), panel_ref[...], out_refs)


def corr_kernel(refs, lag_width, *rest):
    *chunk_refs, out_ref, series_ref, panel_ref, total_ref = rest
    kept = out_ref.shape[0]
    lags, segments = lax.axis_size("lag"), lax.axis_size("seg")
    width = chunk_refs[0].shape[1]
    samples = lags * segments * width
    for (lag_step, segment_step), chunk_ref in zip(steps(lags, segments), chunk_refs):
        lag = lax.bitwise_xor(lax.axis_index("lag"), lag_step)
        segment = lax.bitwise_xor(lax.axis_index("seg"), segment_step)
        start = pl.multiple_of((segment * lags + lag) * width, width)
        series_ref[:, pl.ds(start, width)] = chunk_ref[:kept, :]
        panel_ref[:, pl.ds(start + MARGIN, width)] = chunk_ref[kept:, :]
    series_ref[:, samples:] = jnp.zeros((kept, MARGIN), jnp.float32)
    panel_ref[:, :MARGIN] = jnp.zeros((refs, MARGIN), jnp.float32)
    terms = SAMPLES - LAGS
    first = lax.axis_index("lag") * lag_width
    groups = lag_width // PHASES
    lines = groups * kept
    length = samples // PARTS
    span = length + MARGIN

    def shifted(value, shifts, start):
        parts = [pltpu.roll(value, shift % span, 1) if shift else value for shift in shifts]
        return jnp.concatenate([part[:, start : start + length] for part in parts], axis=0)

    total_ref[...] = jnp.zeros_like(total_ref)

    @pl.loop(0, PARTS)
    def _(part):
        window = pl.ds(pl.multiple_of(part * length, MARGIN), span)
        times = lax.broadcasted_iota(jnp.int32, (refs, span), 1) + (part * length - MARGIN)
        panel = jnp.where(times < terms, panel_ref[:, window], 0.0)
        series = pltpu.roll(series_ref[:, window], span - first, 1)
        panel_high, panel_low = (shifted(half, range(PHASES), MARGIN) for half in halves(panel))
        high, low = (shifted(half, range(0, -lag_width, -PHASES), 0) for half in halves(series))
        total = product_nt(jnp.concatenate([high, low], axis=0), panel_high)
        total_ref[...] += total[:lines] + total[lines:] + product_nt(high, panel_low)

    scale = 1.0 / math.sqrt(terms)
    columns = PHASES * refs
    for group in range(groups):
        total = total_ref[group * kept : (group + 1) * kept, :]
        out_ref[:, group * columns : (group + 1) * columns] = total * scale


def shards(records_owned, section_list, ref_index):
    peers = lax.axis_size("chan")
    segments = lax.axis_size("seg")
    rows, _, samples = records_owned.shape
    refs = ref_index.shape[0]
    share = rows // peers
    kept = rows // segments
    lags = lax.axis_size("lag")
    lag_width = LAGS // lags
    lists = section_list.reshape(peers, rows)
    params = pltpu.CompilerParams(vmem_limit_bytes=48 * 1024 * 1024)
    wanted = ref_index.reshape(1, refs)

    def block(*shape, dtype=jnp.float32):
        return jax.ShapeDtypeStruct(shape, dtype)

    def call(kernel, name, shapes, *operands):
        return pl.pallas_call(kernel, out_shape=shapes, compiler_params=params, name=name)(*operands)

    shapes = [block(kept + refs, samples)] * segments
    if peers == 4:
        first = paired(records_owned, (1, 2))
        half = rows // 2
        whole = pl.BlockSpec(memory_space=pltpu.VMEM)
        own, send, keep, take = pl.pallas_call(
            choose_four_kernel,
            out_shape=[
                block(rows, samples),
                block(half + refs, 2 * rows, dtype=jnp.bfloat16),
                block(rows, 2 * rows, dtype=jnp.bfloat16),
                block(rows, half, dtype=jnp.bfloat16),
            ],
            in_specs=[pl.BlockSpec(memory_space=pl.ANY), whole, whole],
            scratch_shapes=[pltpu.VMEM(records_owned.shape, jnp.float32), pltpu.SemaphoreType.DMA],
            compiler_params=params,
            name="choose",
        )(pltpu.with_memory_space_constraint(records_owned, pltpu.HBM), lists, wanted)
        results = [block(half + refs, samples), block(rows, samples)]
        sent, base = call(pick_kernel, "pick", results, own, first, send, keep)
        placed = call(place_four_kernel, "place", shapes, base, take, sent, paired(sent, (2, 1)))
    else:
        packed, panel = call(
            pack_kernel,
            "pack",
            [block(rows, samples), block(refs, samples)],
            records_owned,
            lists,
            wanted,
        )
        blocks = packed.reshape(peers, share, samples)
        blocks = lax.all_to_all(blocks, "chan", split_axis=0, concat_axis=0, tiled=True)
        step = 1
        while step < peers:
            panel = panel + across(panel, step)
            step *= 2
        pick = call(
            functools.partial(choose_kernel, peers),
            "choose",
            block(rows, rows, dtype=jnp.bfloat16),
            lists,
        )
        placed = call(place_kernel, "place", shapes, pick, panel, blocks.reshape(rows, samples))
    held = {(0, 0): placed[0]}
    for lag_step in range(0, lags, 2):
        for segment_step in range(segments):
            if lag_step or segment_step:
                held[lag_step, segment_step] = swapped(placed[segment_step], lag_step, segment_step)
    for lag_step, segment_step in list(held):
        held[lag_step + 1, segment_step] = swapped(held[lag_step, segment_step], 1, 0)
    return pl.pallas_call(
        functools.partial(corr_kernel, refs, lag_width),
        out_shape=jax.ShapeDtypeStruct((kept, lag_width * refs), jnp.float32),
        scratch_shapes=[
            pltpu.VMEM((kept, lags * segments * samples + MARGIN), jnp.float32),
            pltpu.VMEM((refs, lags * segments * samples + MARGIN), jnp.float32),
            pltpu.VMEM((lag_width // PHASES * kept, PHASES * refs), jnp.float32),
        ],
        compiler_params=params,
        name="correlate",
    )(*[held[step] for step in steps(lags, segments)])


def solution(mesh):
    return jax.shard_map(
        shards,
        mesh=mesh,
        in_specs=(P("chan", "seg", "lag"), P(), P()),
        out_specs=P(("chan", "seg"), "lag"),
        check_vma=False,
    )
```

```python
import functools
import math

import jax
import jax.numpy as jnp
from jax import lax
from jax.experimental import pallas as pl
from jax.experimental.pallas import tpu as pltpu
from jax.sharding import PartitionSpec as P

LAGS = 128
SAMPLES = 2048
PHASES = 4
PARTS = 2
MARGIN = 128


def halves(value):
    high = value.astype(jnp.bfloat16)
    low = (value - high.astype(jnp.float32)).astype(jnp.bfloat16)
    return high, low


def product(left, right):
    return jnp.dot(left, right, preferred_element_type=jnp.float32)


def product_nt(left, right):
    return lax.dot_general(
        left, right, (((1,), (1,)), ((), ())), preferred_element_type=jnp.float32
    )


def steps(lags, segments):
    return [(lag, segment) for lag in range(lags) for segment in range(segments)]


def swapped(value, lag_step, segment_step):
    lags, segments = lax.axis_size("lag"), lax.axis_size("seg")
    pairs = [
        (lag * segments + segment, (lag ^ lag_step) * segments + (segment ^ segment_step))
        for lag, segment in steps(lags, segments)
    ]
    return lax.ppermute(value, ("lag", "seg"), pairs)


def across(value, step):
    return lax.ppermute(value, "chan", [(i, i ^ step) for i in range(lax.axis_size("chan"))])


def paired(value, order):
    lags = lax.axis_size("lag")
    pairs = [
        (chan * lags + lag, (chan ^ order[lag % 2]) * lags + lag)
        for chan in range(lax.axis_size("chan"))
        for lag in range(lags)
        if order[lag % 2]
    ]
    return lax.ppermute(value, ("chan", "lag"), pairs)


def choice(pick, rows):
    high, low = halves(rows)
    return product(pick, high) + product(pick, low)


def counts_before(present):
    rows = present.shape[0]
    line = lax.broadcasted_iota(jnp.int32, (rows, rows), 0)
    lane = lax.broadcasted_iota(jnp.int32, (rows, rows), 1)
    return product((lane < line).astype(jnp.bfloat16), present.astype(jnp.bfloat16))


def columns(refs_ref, width):
    return jnp.broadcast_to(refs_ref[...], (width, refs_ref.shape[1])).T


def choose_four_kernel(
    records_ref,
    lists_ref,
    refs_ref,
    own_ref,
    send_ref,
    keep_ref,
    take_ref,
    held_ref,
    done,
):
    copy = pltpu.make_async_copy(records_ref, held_ref, done)
    copy.start()
    rows = lists_ref.shape[1]
    kept = take_ref.shape[1]
    refs = refs_ref.shape[1]
    me = lax.axis_index("chan")
    odd = lax.rem(lax.axis_index("lag"), 2)
    near, far = 1 + odd, 2 - odd
    line = lax.broadcasted_iota(jnp.int32, (rows, 2 * rows), 0)

    def pool(owner):
        lists = [lists_ref[pl.ds(lax.bitwise_xor(owner, i), 1), :] for i in (0, near)]
        return jnp.concatenate(lists, axis=1)

    def where(owner, block):
        return pool(owner) == line + block * rows

    def ranks(found):
        present = jnp.max(found.astype(jnp.float32), axis=1, keepdims=True)
        return present, counts_before(jnp.broadcast_to(present, (rows, rows)))

    other = lax.bitwise_xor(me, far)
    found = where(me, other)
    _, rank = ranks(found)
    rank = jnp.concatenate([rank, rank], axis=1)
    slot = jnp.sum(jnp.where(found, rank + 1.0, 0.0), axis=0, keepdims=True).astype(jnp.int32)
    send = jnp.concatenate([line[:kept] + 1 == slot, columns(refs_ref, 2 * rows) == pool(me)], axis=0)
    send = send.astype(jnp.bfloat16)
    keep = where(me, me).astype(jnp.bfloat16)
    send_ref[...] = send
    keep_ref[...] = keep
    present, rank = ranks(where(other, me))
    lane = lax.broadcasted_iota(jnp.int32, (rows, kept), 1)
    slot = jnp.where(present > 0.0, rank[:, :kept], -1.0).astype(jnp.int32)
    take_ref[...] = (lane == slot).astype(jnp.bfloat16)
    copy.wait()
    own_ref[...] = held_ref[:, 0, :]


def pick_kernel(own_ref, even_ref, odd_ref, send_ref, keep_ref, sent_ref, base_ref):
    arrived = jnp.where(lax.rem(lax.axis_index("lag"), 2) == 0, even_ref[:, 0, :], odd_ref[...])
    rows = jnp.concatenate([own_ref[...], arrived], axis=0)
    high, low = halves(rows)
    sent_ref[...] = product(send_ref[...], high) + product(send_ref[...], low)
    base_ref[...] = product(keep_ref[...], high) + product(keep_ref[...], low)


def put(series, panel, out_refs):
    segments = len(out_refs)
    kept = series.shape[0] // segments
    own = lax.axis_index("seg")
    for part in range(segments):
        half = lax.bitwise_xor(own, part)
        chosen = series[:kept]
        for other in range(1, segments):
            chosen = jnp.where(half == other, series[other * kept : (other + 1) * kept], chosen)
        out_refs[part][:kept, :] = chosen
        out_refs[part][kept:, :] = panel


def place_four_kernel(base_ref, take_ref, sent_ref, arrived_ref, *out_refs):
    kept = take_ref.shape[1]
    series = base_ref[...] + choice(take_ref[...], arrived_ref[:kept, :])
    put(series, sent_ref[kept:, :] + arrived_ref[kept:, :], out_refs)


def pack_kernel(records_ref, lists_ref, refs_ref, out_ref, panel_ref):
    rows = records_ref.shape[0]
    refs = refs_ref.shape[1]
    own = jnp.broadcast_to(lists_ref[pl.ds(lax.axis_index("chan"), 1), :], (rows, rows))
    rank = jnp.sum((own.T < own).astype(jnp.int32), axis=0, keepdims=True)
    line = lax.broadcasted_iota(jnp.int32, (rows, rows), 0)
    records = records_ref[:, 0, :]
    panel_ref[...] = choice((columns(refs_ref, rows) == own[:refs]).astype(jnp.bfloat16), records)
    out_ref[...] = choice((line == rank).astype(jnp.bfloat16), records)


def choose_kernel(peers, lists_ref, pick_ref):
    rows = lists_ref.shape[1]
    share = rows // peers
    lane = lax.broadcasted_iota(jnp.int32, (rows, rows), 1)
    channel = lax.broadcasted_iota(jnp.int32, (rows, rows), 0) + lax.axis_index("chan") * rows
    owner = jnp.zeros((rows, 1), jnp.int32)
    for peer in range(peers):
        found = (lists_ref[pl.ds(peer, 1), :] == channel).astype(jnp.int32)
        owner = owner + jnp.sum(found, axis=1, keepdims=True) * peer
    same = lane == owner
    before = counts_before(same.astype(jnp.float32))
    rank = jnp.sum(jnp.where(same, before, 0.0), axis=1, keepdims=True).astype(jnp.int32)
    pick_ref[...] = (lane == owner * share + rank).astype(jnp.bfloat16)


def place_kernel(pick_ref, panel_ref, arrived_ref, *out_refs):
    put(choice(pick_ref[...], arrived_ref[...]), panel_ref[...], out_refs)


def corr_kernel(refs, lag_width, *rest):
    *chunk_refs, out_ref, joined_ref, total_ref = rest
    kept = out_ref.shape[0]
    lags, segments = lax.axis_size("lag"), lax.axis_size("seg")
    width = chunk_refs[0].shape[1]
    for (lag_step, segment_step), chunk_ref in zip(steps(lags, segments), chunk_refs):
        lag = lax.bitwise_xor(lax.axis_index("lag"), lag_step)
        segment = lax.bitwise_xor(lax.axis_index("seg"), segment_step)
        start = pl.multiple_of((segment * lags + lag) * width, width)
        joined_ref[:, pl.ds(start, width)] = chunk_ref[...]
    series = joined_ref[:kept, :]
    panel = joined_ref[kept:, :]
    samples = panel.shape[1]
    terms = SAMPLES - LAGS
    times = lax.broadcasted_iota(jnp.int32, panel.shape, 1)
    panel = jnp.where(times < terms, panel, 0.0)
    series = pltpu.roll(series, samples - lax.axis_index("lag") * lag_width, 1)
    groups = lag_width // PHASES
    length = samples // PARTS

    def shifted(value, shifts, first):
        size = value.shape[1]
        parts = [pltpu.roll(value, shift % size, 1) if shift else value for shift in shifts]
        return jnp.concatenate([part[:, first : first + length] for part in parts], axis=0)

    panel = jnp.concatenate([jnp.zeros((refs, MARGIN), jnp.float32), panel], axis=1)
    series = jnp.concatenate([series, series[:, :MARGIN]], axis=1)
    panel_parts, series_parts = halves(panel), halves(series)
    lines = groups * kept
    for part in range(PARTS):
        window = slice(part * length, (part + 1) * length + MARGIN)
        panel_high, panel_low = (
            shifted(half[:, window], range(PHASES), MARGIN) for half in panel_parts
        )
        high, low = (
            shifted(half[:, window], range(0, -lag_width, -PHASES), 0) for half in series_parts
        )
        total = product_nt(jnp.concatenate([high, low], axis=0), panel_high)
        total = total[:lines] + total[lines:] + product_nt(high, panel_low)
        total_ref[part] = total
    scale = 1.0 / math.sqrt(terms)
    columns = PHASES * refs
    for group in range(groups):
        place = slice(group * kept, (group + 1) * kept)
        total = total_ref[0, place, :]
        for part in range(1, PARTS):
            total = total + total_ref[part, place, :]
        out_ref[:, group * columns : (group + 1) * columns] = total * scale


def shards(records_owned, section_list, ref_index):
    peers = lax.axis_size("chan")
    segments = lax.axis_size("seg")
    rows, _, samples = records_owned.shape
    refs = ref_index.shape[0]
    share = rows // peers
    kept = rows // segments
    lags = lax.axis_size("lag")
    lag_width = LAGS // lags
    lists = section_list.reshape(peers, rows)
    params = pltpu.CompilerParams(vmem_limit_bytes=48 * 1024 * 1024)
    wanted = ref_index.reshape(1, refs)

    def block(*shape, dtype=jnp.float32):
        return jax.ShapeDtypeStruct(shape, dtype)

    def call(kernel, name, shapes, *operands):
        return pl.pallas_call(kernel, out_shape=shapes, compiler_params=params, name=name)(*operands)

    shapes = [block(kept + refs, samples)] * segments
    if peers == 4:
        even = paired(records_owned, (1, 0))
        half = rows // 2
        whole = pl.BlockSpec(memory_space=pltpu.VMEM)
        own, send, keep, take = pl.pallas_call(
            choose_four_kernel,
            out_shape=[
                block(rows, samples),
                block(half + refs, 2 * rows, dtype=jnp.bfloat16),
                block(rows, 2 * rows, dtype=jnp.bfloat16),
                block(rows, half, dtype=jnp.bfloat16),
            ],
            in_specs=[pl.BlockSpec(memory_space=pl.ANY), whole, whole],
            scratch_shapes=[pltpu.VMEM(records_owned.shape, jnp.float32), pltpu.SemaphoreType.DMA],
            compiler_params=params,
            name="choose",
        )(pltpu.with_memory_space_constraint(records_owned, pltpu.HBM), lists, wanted)
        results = [block(half + refs, samples), block(rows, samples)]
        odd = paired(own, (0, 2))
        sent, base = call(pick_kernel, "pick", results, own, even, odd, send, keep)
        placed = call(place_four_kernel, "place", shapes, base, take, sent, paired(sent, (2, 1)))
    else:
        packed, panel = call(
            pack_kernel,
            "pack",
            [block(rows, samples), block(refs, samples)],
            records_owned,
            lists,
            wanted,
        )
        blocks = packed.reshape(peers, share, samples)
        blocks = lax.all_to_all(blocks, "chan", split_axis=0, concat_axis=0, tiled=True)
        step = 1
        while step < peers:
            panel = panel + across(panel, step)
            step *= 2
        pick = call(
            functools.partial(choose_kernel, peers),
            "choose",
            block(rows, rows, dtype=jnp.bfloat16),
            lists,
        )
        placed = call(place_kernel, "place", shapes, pick, panel, blocks.reshape(rows, samples))
    held = {(0, 0): placed[0]}
    for lag_step in range(0, lags, 2):
        for segment_step in range(segments):
            if lag_step or segment_step:
                held[lag_step, segment_step] = swapped(placed[segment_step], lag_step, segment_step)
    for lag_step, segment_step in list(held):
        held[lag_step + 1, segment_step] = swapped(held[lag_step, segment_step], 1, 0)
    return pl.pallas_call(
        functools.partial(corr_kernel, refs, lag_width),
        out_shape=jax.ShapeDtypeStruct((kept, lag_width * refs), jnp.float32),
        scratch_shapes=[
            pltpu.VMEM((kept + refs, lags * segments * samples), jnp.float32),
            pltpu.VMEM((PARTS, lag_width // PHASES * kept, PHASES * refs), jnp.float32),
        ],
        compiler_params=params,
        name="correlate",
    )(*[held[step] for step in steps(lags, segments)])


def solution(mesh):
    return jax.shard_map(
        shards,
        mesh=mesh,
        in_specs=(P("chan", "seg", "lag"), P(), P()),
        out_specs=P(("chan", "seg"), "lag"),
        check_vma=False,
    )
```

```python
import functools
import math

import jax
import jax.numpy as jnp
from jax import lax
from jax.experimental import pallas as pl
from jax.experimental.pallas import tpu as pltpu
from jax.sharding import PartitionSpec as P

LAGS = 128
SAMPLES = 2048
PHASES = 4
PARTS = 2
MARGIN = 128


def halves(value):
    high = value.astype(jnp.bfloat16)
    low = (value - high.astype(jnp.float32)).astype(jnp.bfloat16)
    return high, low


def product(left, right):
    return jnp.dot(left, right, preferred_element_type=jnp.float32)


def product_nt(left, right):
    return lax.dot_general(
        left, right, (((1,), (1,)), ((), ())), preferred_element_type=jnp.float32
    )


def steps(lags, segments):
    return [(lag, segment) for lag in range(lags) for segment in range(segments)]


def swapped(value, lag_step, segment_step):
    lags, segments = lax.axis_size("lag"), lax.axis_size("seg")
    pairs = [
        (lag * segments + segment, (lag ^ lag_step) * segments + (segment ^ segment_step))
        for lag, segment in steps(lags, segments)
    ]
    return lax.ppermute(value, ("lag", "seg"), pairs)


def across(value, step):
    return lax.ppermute(value, "chan", [(i, i ^ step) for i in range(lax.axis_size("chan"))])


def paired(value, order):
    lags = lax.axis_size("lag")
    pairs = [
        (chan * lags + lag, (chan ^ order[lag % 2]) * lags + lag)
        for chan in range(lax.axis_size("chan"))
        for lag in range(lags)
    ]
    return lax.ppermute(value, ("chan", "lag"), pairs)


def choice(pick, rows):
    high, low = halves(rows)
    return product(pick, high) + product(pick, low)


def counts_before(present):
    rows = present.shape[0]
    line = lax.broadcasted_iota(jnp.int32, (rows, rows), 0)
    lane = lax.broadcasted_iota(jnp.int32, (rows, rows), 1)
    return product((lane < line).astype(jnp.bfloat16), present.astype(jnp.bfloat16))


def columns(refs_ref, width):
    return jnp.broadcast_to(refs_ref[...], (width, refs_ref.shape[1])).T


def choose_four_kernel(
    records_ref,
    lists_ref,
    refs_ref,
    own_ref,
    send_ref,
    keep_ref,
    take_ref,
    held_ref,
    done,
):
    copy = pltpu.make_async_copy(records_ref, held_ref, done)
    copy.start()
    rows = lists_ref.shape[1]
    kept = take_ref.shape[1]
    refs = refs_ref.shape[1]
    me = lax.axis_index("chan")
    odd = lax.rem(lax.axis_index("lag"), 2)
    near, far = 1 + odd, 2 - odd
    line = lax.broadcasted_iota(jnp.int32, (rows, 2 * rows), 0)

    def pool(owner):
        lists = [lists_ref[pl.ds(lax.bitwise_xor(owner, i), 1), :] for i in (0, near)]
        return jnp.concatenate(lists, axis=1)

    def where(owner, block):
        return pool(owner) == line + block * rows

    def ranks(found):
        present = jnp.max(found.astype(jnp.float32), axis=1, keepdims=True)
        return present, counts_before(jnp.broadcast_to(present, (rows, rows)))

    other = lax.bitwise_xor(me, far)
    found = where(me, other)
    _, rank = ranks(found)
    rank = jnp.concatenate([rank, rank], axis=1)
    slot = jnp.sum(jnp.where(found, rank + 1.0, 0.0), axis=0, keepdims=True).astype(jnp.int32)
    send = jnp.concatenate([line[:kept] + 1 == slot, columns(refs_ref, 2 * rows) == pool(me)], axis=0)
    send = send.astype(jnp.bfloat16)
    keep = where(me, me).astype(jnp.bfloat16)
    send_ref[...] = send
    keep_ref[...] = keep
    present, rank = ranks(where(other, me))
    lane = lax.broadcasted_iota(jnp.int32, (rows, kept), 1)
    slot = jnp.where(present > 0.0, rank[:, :kept], -1.0).astype(jnp.int32)
    take_ref[...] = (lane == slot).astype(jnp.bfloat16)
    copy.wait()
    own_ref[...] = held_ref[:, 0, :]


def pick_kernel(own_ref, arrived_ref, send_ref, keep_ref, sent_ref, base_ref):
    rows = jnp.concatenate([own_ref[...], arrived_ref[:, 0, :]], axis=0)
    high, low = halves(rows)
    sent_ref[...] = product(send_ref[...], high) + product(send_ref[...], low)
    base_ref[...] = product(keep_ref[...], high) + product(keep_ref[...], low)


def put(series, panel, out_refs):
    segments = len(out_refs) - 1
    kept = series.shape[0] // segments
    own = lax.axis_index("seg")
    for part in range(segments):
        half = lax.bitwise_xor(own, part)
        chosen = series[:kept]
        for other in range(1, segments):
            chosen = jnp.where(half == other, series[other * kept : (other + 1) * kept], chosen)
        for out_ref in out_refs[:: segments] if part == 0 else [out_refs[part]]:
            out_ref[:kept, :] = chosen
            out_ref[kept:, :] = panel


def place_four_kernel(base_ref, take_ref, sent_ref, arrived_ref, *out_refs):
    kept = take_ref.shape[1]
    series = base_ref[...] + choice(take_ref[...], arrived_ref[:kept, :])
    put(series, sent_ref[kept:, :] + arrived_ref[kept:, :], out_refs)


def pack_kernel(records_ref, lists_ref, refs_ref, out_ref, panel_ref):
    rows = records_ref.shape[0]
    refs = refs_ref.shape[1]
    own = jnp.broadcast_to(lists_ref[pl.ds(lax.axis_index("chan"), 1), :], (rows, rows))
    rank = jnp.sum((own.T < own).astype(jnp.int32), axis=0, keepdims=True)
    line = lax.broadcasted_iota(jnp.int32, (rows, rows), 0)
    records = records_ref[:, 0, :]
    panel_ref[...] = choice((columns(refs_ref, rows) == own[:refs]).astype(jnp.bfloat16), records)
    out_ref[...] = choice((line == rank).astype(jnp.bfloat16), records)


def choose_kernel(peers, lists_ref, pick_ref):
    rows = lists_ref.shape[1]
    share = rows // peers
    lane = lax.broadcasted_iota(jnp.int32, (rows, rows), 1)
    channel = lax.broadcasted_iota(jnp.int32, (rows, rows), 0) + lax.axis_index("chan") * rows
    owner = jnp.zeros((rows, 1), jnp.int32)
    for peer in range(peers):
        found = (lists_ref[pl.ds(peer, 1), :] == channel).astype(jnp.int32)
        owner = owner + jnp.sum(found, axis=1, keepdims=True) * peer
    same = lane == owner
    before = counts_before(same.astype(jnp.float32))
    rank = jnp.sum(jnp.where(same, before, 0.0), axis=1, keepdims=True).astype(jnp.int32)
    pick_ref[...] = (lane == owner * share + rank).astype(jnp.bfloat16)


def place_kernel(pick_ref, panel_ref, arrived_ref, *out_refs):
    put(choice(pick_ref[...], arrived_ref[...]), panel_ref[...], out_refs)


def corr_kernel(refs, lag_width, *rest):
    *chunk_refs, out_ref, joined_ref, total_ref = rest
    kept = out_ref.shape[0]
    lags, segments = lax.axis_size("lag"), lax.axis_size("seg")
    width = chunk_refs[0].shape[1]
    for (lag_step, segment_step), chunk_ref in zip(steps(lags, segments), chunk_refs):
        lag = lax.bitwise_xor(lax.axis_index("lag"), lag_step)
        segment = lax.bitwise_xor(lax.axis_index("seg"), segment_step)
        start = pl.multiple_of((segment * lags + lag) * width, width)
        joined_ref[:, pl.ds(start, width)] = chunk_ref[...]
    series = joined_ref[:kept, :]
    panel = joined_ref[kept:, :]
    samples = panel.shape[1]
    terms = SAMPLES - LAGS
    times = lax.broadcasted_iota(jnp.int32, panel.shape, 1)
    panel = jnp.where(times < terms, panel, 0.0)
    series = pltpu.roll(series, samples - lax.axis_index("lag") * lag_width, 1)
    groups = lag_width // PHASES
    length = samples // PARTS

    def shifted(value, shifts, first):
        size = value.shape[1]
        parts = [pltpu.roll(value, shift % size, 1) if shift else value for shift in shifts]
        return jnp.concatenate([part[:, first : first + length] for part in parts], axis=0)

    panel = jnp.concatenate([jnp.zeros((refs, MARGIN), jnp.float32), panel], axis=1)
    series = jnp.concatenate([series, series[:, :MARGIN]], axis=1)
    panel_parts, series_parts = halves(panel), halves(series)
    lines = groups * kept
    for part in range(PARTS):
        window = slice(part * length, (part + 1) * length + MARGIN)
        panel_high, panel_low = (
            shifted(half[:, window], range(PHASES), MARGIN) for half in panel_parts
        )
        high, low = (
            shifted(half[:, window], range(0, -lag_width, -PHASES), 0) for half in series_parts
        )
        total = product_nt(jnp.concatenate([high, low], axis=0), panel_high)
        total = total[:lines] + total[lines:] + product_nt(high, panel_low)
        total_ref[part] = total
    scale = 1.0 / math.sqrt(terms)
    columns = PHASES * refs
    for group in range(groups):
        place = slice(group * kept, (group + 1) * kept)
        total = total_ref[0, place, :]
        for part in range(1, PARTS):
            total = total + total_ref[part, place, :]
        out_ref[:, group * columns : (group + 1) * columns] = total * scale


def shards(records_owned, section_list, ref_index):
    peers = lax.axis_size("chan")
    segments = lax.axis_size("seg")
    rows, _, samples = records_owned.shape
    refs = ref_index.shape[0]
    share = rows // peers
    kept = rows // segments
    lags = lax.axis_size("lag")
    lag_width = LAGS // lags
    lists = section_list.reshape(peers, rows)
    params = pltpu.CompilerParams(vmem_limit_bytes=48 * 1024 * 1024)
    wanted = ref_index.reshape(1, refs)

    def block(*shape, dtype=jnp.float32):
        return jax.ShapeDtypeStruct(shape, dtype)

    def call(kernel, name, shapes, *operands):
        return pl.pallas_call(kernel, out_shape=shapes, compiler_params=params, name=name)(*operands)

    shapes = [block(kept + refs, samples)] * (segments + 1)
    if peers == 4:
        first = paired(records_owned, (1, 2))
        half = rows // 2
        whole = pl.BlockSpec(memory_space=pltpu.VMEM)
        own, send, keep, take = pl.pallas_call(
            choose_four_kernel,
            out_shape=[
                block(rows, samples),
                block(half + refs, 2 * rows, dtype=jnp.bfloat16),
                block(rows, 2 * rows, dtype=jnp.bfloat16),
                block(rows, half, dtype=jnp.bfloat16),
            ],
            in_specs=[pl.BlockSpec(memory_space=pl.ANY), whole, whole],
            scratch_shapes=[pltpu.VMEM(records_owned.shape, jnp.float32), pltpu.SemaphoreType.DMA],
            compiler_params=params,
            name="choose",
        )(pltpu.with_memory_space_constraint(records_owned, pltpu.HBM), lists, wanted)
        results = [block(half + refs, samples), block(rows, samples)]
        sent, base = call(pick_kernel, "pick", results, own, first, send, keep)
        placed = call(place_four_kernel, "place", shapes, base, take, sent, paired(sent, (2, 1)))
    else:
        packed, panel = call(
            pack_kernel,
            "pack",
            [block(rows, samples), block(refs, samples)],
            records_owned,
            lists,
            wanted,
        )
        blocks = packed.reshape(peers, share, samples)
        blocks = lax.all_to_all(blocks, "chan", split_axis=0, concat_axis=0, tiled=True)
        step = 1
        while step < peers:
            panel = panel + across(panel, step)
            step *= 2
        pick = call(
            functools.partial(choose_kernel, peers),
            "choose",
            block(rows, rows, dtype=jnp.bfloat16),
            lists,
        )
        placed = call(place_kernel, "place", shapes, pick, panel, blocks.reshape(rows, samples))
    held = {(0, 0): placed[0]}
    for lag_step in range(0, lags, 2):
        for segment_step in range(segments):
            if lag_step or segment_step:
                part = placed[segment_step or segments]
                held[lag_step, segment_step] = swapped(part, lag_step, segment_step)
    for lag_step, segment_step in list(held):
        held[lag_step + 1, segment_step] = swapped(held[lag_step, segment_step], 1, 0)
    return pl.pallas_call(
        functools.partial(corr_kernel, refs, lag_width),
        out_shape=jax.ShapeDtypeStruct((kept, lag_width * refs), jnp.float32),
        scratch_shapes=[
            pltpu.VMEM((kept + refs, lags * segments * samples), jnp.float32),
            pltpu.VMEM((PARTS, lag_width // PHASES * kept, PHASES * refs), jnp.float32),
        ],
        compiler_params=params,
        name="correlate",
    )(*[held[step] for step in steps(lags, segments)])


def solution(mesh):
    return jax.shard_map(
        shards,
        mesh=mesh,
        in_specs=(P("chan", "seg", "lag"), P(), P()),
        out_specs=P(("chan", "seg"), "lag"),
        check_vma=False,
    )
```

```python
import functools
import math

import jax
import jax.numpy as jnp
from jax import lax
from jax.experimental import pallas as pl
from jax.experimental.pallas import tpu as pltpu
from jax.sharding import PartitionSpec as P

LAGS = 128
SAMPLES = 2048
PHASES = 4


def halves(value):
    high = value.astype(jnp.bfloat16)
    low = (value - high.astype(jnp.float32)).astype(jnp.bfloat16)
    return high, low


def product(left, right):
    return jnp.dot(left, right, preferred_element_type=jnp.float32)


def product_nt(left, right):
    return lax.dot_general(
        left, right, (((1,), (1,)), ((), ())), preferred_element_type=jnp.float32
    )


def steps(lags, segments):
    return [(lag, segment) for lag in range(lags) for segment in range(segments)]


def swapped(value, lag_step, segment_step):
    lags, segments = lax.axis_size("lag"), lax.axis_size("seg")
    pairs = [
        (lag * segments + segment, (lag ^ lag_step) * segments + (segment ^ segment_step))
        for lag, segment in steps(lags, segments)
    ]
    return lax.ppermute(value, ("lag", "seg"), pairs)


def across(value, step):
    return lax.ppermute(value, "chan", [(i, i ^ step) for i in range(lax.axis_size("chan"))])


def paired(value, order):
    lags = lax.axis_size("lag")
    pairs = [
        (chan * lags + lag, (chan ^ order[lag % 2]) * lags + lag)
        for chan in range(lax.axis_size("chan"))
        for lag in range(lags)
    ]
    return lax.ppermute(value, ("chan", "lag"), pairs)


def choice(pick, rows):
    high, low = halves(rows)
    return product(pick, high) + product(pick, low)


def counts_before(present):
    rows = present.shape[0]
    line = lax.broadcasted_iota(jnp.int32, (rows, rows), 0)
    lane = lax.broadcasted_iota(jnp.int32, (rows, rows), 1)
    return product((lane < line).astype(jnp.bfloat16), present.astype(jnp.bfloat16))


def columns(refs_ref, width):
    return jnp.broadcast_to(refs_ref[...], (width, refs_ref.shape[1])).T


def choose_four_kernel(
    records_ref,
    lists_ref,
    refs_ref,
    own_ref,
    send_ref,
    keep_ref,
    take_ref,
    held_ref,
    done,
):
    copy = pltpu.make_async_copy(records_ref, held_ref, done)
    copy.start()
    rows = lists_ref.shape[1]
    kept = take_ref.shape[1]
    refs = refs_ref.shape[1]
    me = lax.axis_index("chan")
    odd = lax.rem(lax.axis_index("lag"), 2)
    near, far = 1 + odd, 2 - odd
    line = lax.broadcasted_iota(jnp.int32, (rows, 2 * rows), 0)

    def pool(owner):
        lists = [lists_ref[pl.ds(lax.bitwise_xor(owner, i), 1), :] for i in (0, near)]
        return jnp.concatenate(lists, axis=1)

    def where(owner, block):
        return pool(owner) == line + block * rows

    def ranks(found):
        present = jnp.max(found.astype(jnp.float32), axis=1, keepdims=True)
        return present, counts_before(jnp.broadcast_to(present, (rows, rows)))

    other = lax.bitwise_xor(me, far)
    found = where(me, other)
    _, rank = ranks(found)
    rank = jnp.concatenate([rank, rank], axis=1)
    slot = jnp.sum(jnp.where(found, rank + 1.0, 0.0), axis=0, keepdims=True).astype(jnp.int32)
    send = jnp.concatenate([line[:kept] + 1 == slot, columns(refs_ref, 2 * rows) == pool(me)], axis=0)
    send = send.astype(jnp.bfloat16)
    keep = where(me, me).astype(jnp.bfloat16)
    send_ref[...] = send
    keep_ref[...] = keep
    present, rank = ranks(where(other, me))
    lane = lax.broadcasted_iota(jnp.int32, (rows, kept), 1)
    slot = jnp.where(present > 0.0, rank[:, :kept], -1.0).astype(jnp.int32)
    take_ref[...] = (lane == slot).astype(jnp.bfloat16)
    copy.wait()
    own_ref[...] = held_ref[:, 0, :]


def pick_kernel(own_ref, arrived_ref, send_ref, keep_ref, sent_ref, base_ref):
    rows = jnp.concatenate([own_ref[...], arrived_ref[:, 0, :]], axis=0)
    high, low = halves(rows)
    sent_ref[...] = product(send_ref[...], high) + product(send_ref[...], low)
    base_ref[...] = product(keep_ref[...], high) + product(keep_ref[...], low)


def put(series, panel, out_refs):
    segments = len(out_refs)
    kept = series.shape[0] // segments
    own = lax.axis_index("seg")
    for part in range(segments):
        half = lax.bitwise_xor(own, part)
        chosen = series[:kept]
        for other in range(1, segments):
            chosen = jnp.where(half == other, series[other * kept : (other + 1) * kept], chosen)
        out_refs[part][:kept, :] = chosen
        out_refs[part][kept:, :] = panel


def place_four_kernel(base_ref, take_ref, sent_ref, arrived_ref, *out_refs):
    kept = take_ref.shape[1]
    series = base_ref[...] + choice(take_ref[...], arrived_ref[:kept, :])
    put(series, sent_ref[kept:, :] + arrived_ref[kept:, :], out_refs)


def pack_kernel(records_ref, lists_ref, refs_ref, out_ref, panel_ref):
    rows = records_ref.shape[0]
    refs = refs_ref.shape[1]
    own = jnp.broadcast_to(lists_ref[pl.ds(lax.axis_index("chan"), 1), :], (rows, rows))
    rank = jnp.sum((own.T < own).astype(jnp.int32), axis=0, keepdims=True)
    line = lax.broadcasted_iota(jnp.int32, (rows, rows), 0)
    records = records_ref[:, 0, :]
    panel_ref[...] = choice((columns(refs_ref, rows) == own[:refs]).astype(jnp.bfloat16), records)
    out_ref[...] = choice((line == rank).astype(jnp.bfloat16), records)


def choose_kernel(peers, lists_ref, pick_ref):
    rows = lists_ref.shape[1]
    share = rows // peers
    lane = lax.broadcasted_iota(jnp.int32, (rows, rows), 1)
    channel = lax.broadcasted_iota(jnp.int32, (rows, rows), 0) + lax.axis_index("chan") * rows
    owner = jnp.zeros((rows, 1), jnp.int32)
    for peer in range(peers):
        found = (lists_ref[pl.ds(peer, 1), :] == channel).astype(jnp.int32)
        owner = owner + jnp.sum(found, axis=1, keepdims=True) * peer
    same = lane == owner
    before = counts_before(same.astype(jnp.float32))
    rank = jnp.sum(jnp.where(same, before, 0.0), axis=1, keepdims=True).astype(jnp.int32)
    pick_ref[...] = (lane == owner * share + rank).astype(jnp.bfloat16)


def place_kernel(pick_ref, panel_ref, arrived_ref, *out_refs):
    put(choice(pick_ref[...], arrived_ref[...]), panel_ref[...], out_refs)


def corr_kernel(refs, lag_width, *rest):
    *chunk_refs, out_ref, joined_ref, series_ref, panel_ref = rest
    kept = out_ref.shape[0]
    lags, segments = lax.axis_size("lag"), lax.axis_size("seg")
    width = chunk_refs[0].shape[1]
    for (lag_step, segment_step), chunk_ref in zip(steps(lags, segments), chunk_refs):
        lag = lax.bitwise_xor(lax.axis_index("lag"), lag_step)
        segment = lax.bitwise_xor(lax.axis_index("seg"), segment_step)
        start = pl.multiple_of((segment * lags + lag) * width, width)
        joined_ref[:, pl.ds(start, width)] = chunk_ref[...]
    series = joined_ref[:kept, :]
    panel = joined_ref[kept:, :]
    samples = panel.shape[1]
    terms = SAMPLES - LAGS
    times = lax.broadcasted_iota(jnp.int32, panel.shape, 1)
    panel = jnp.where(times < terms, panel, 0.0)
    series = pltpu.roll(series, samples - lax.axis_index("lag") * lag_width, 1)
    groups = lag_width // PHASES

    def spread(value, count, step, out_ref):
        lines = value.shape[0]
        for half, part in enumerate(halves(value)):
            for i in range(count):
                start = (half * count + i) * lines
                out_ref[start : start + lines, :] = (
                    pltpu.roll(part, (i * step) % samples, 1) if i else part
                )

    spread(panel, PHASES, 1, panel_ref)
    spread(series, groups, -PHASES, series_ref)
    lines, columns = groups * kept, PHASES * refs
    upper = product_nt(series_ref[...], panel_ref[:columns, :])
    lower = product_nt(series_ref[:lines, :], panel_ref[columns:, :])
    total = (upper[:lines] + upper[lines:] + lower) * (1.0 / math.sqrt(terms))
    for group in range(groups):
        out_ref[:, group * columns : (group + 1) * columns] = total[
            group * kept : (group + 1) * kept
        ]


def shards(records_owned, section_list, ref_index):
    peers = lax.axis_size("chan")
    segments = lax.axis_size("seg")
    rows, _, samples = records_owned.shape
    refs = ref_index.shape[0]
    share = rows // peers
    kept = rows // segments
    lags = lax.axis_size("lag")
    lag_width = LAGS // lags
    lists = section_list.reshape(peers, rows)
    params = pltpu.CompilerParams(vmem_limit_bytes=48 * 1024 * 1024)
    wanted = ref_index.reshape(1, refs)

    def block(*shape, dtype=jnp.float32):
        return jax.ShapeDtypeStruct(shape, dtype)

    def call(kernel, name, shapes, *operands):
        return pl.pallas_call(kernel, out_shape=shapes, compiler_params=params, name=name)(*operands)

    shapes = [block(kept + refs, samples)] * segments
    if peers == 4:
        first = paired(records_owned, (1, 2))
        half = rows // 2
        whole = pl.BlockSpec(memory_space=pltpu.VMEM)
        own, send, keep, take = pl.pallas_call(
            choose_four_kernel,
            out_shape=[
                block(rows, samples),
                block(half + refs, 2 * rows, dtype=jnp.bfloat16),
                block(rows, 2 * rows, dtype=jnp.bfloat16),
                block(rows, half, dtype=jnp.bfloat16),
            ],
            in_specs=[pl.BlockSpec(memory_space=pl.ANY), whole, whole],
            scratch_shapes=[pltpu.VMEM(records_owned.shape, jnp.float32), pltpu.SemaphoreType.DMA],
            compiler_params=params,
            name="choose",
        )(pltpu.with_memory_space_constraint(records_owned, pltpu.HBM), lists, wanted)
        results = [block(half + refs, samples), block(rows, samples)]
        sent, base = call(pick_kernel, "pick", results, own, first, send, keep)
        placed = call(place_four_kernel, "place", shapes, base, take, sent, paired(sent, (2, 1)))
    else:
        packed, panel = call(
            pack_kernel,
            "pack",
            [block(rows, samples), block(refs, samples)],
            records_owned,
            lists,
            wanted,
        )
        blocks = packed.reshape(peers, share, samples)
        blocks = lax.all_to_all(blocks, "chan", split_axis=0, concat_axis=0, tiled=True)
        step = 1
        while step < peers:
            panel = panel + across(panel, step)
            step *= 2
        pick = call(
            functools.partial(choose_kernel, peers),
            "choose",
            block(rows, rows, dtype=jnp.bfloat16),
            lists,
        )
        placed = call(place_kernel, "place", shapes, pick, panel, blocks.reshape(rows, samples))
    held = {(0, 0): placed[0]}
    for lag_step in range(0, lags, 2):
        for segment_step in range(segments):
            if lag_step or segment_step:
                held[lag_step, segment_step] = swapped(placed[segment_step], lag_step, segment_step)
    for lag_step, segment_step in list(held):
        held[lag_step + 1, segment_step] = swapped(held[lag_step, segment_step], 1, 0)
    return pl.pallas_call(
        functools.partial(corr_kernel, refs, lag_width),
        out_shape=jax.ShapeDtypeStruct((kept, lag_width * refs), jnp.float32),
        scratch_shapes=[
            pltpu.VMEM((kept + refs, lags * segments * samples), jnp.float32),
            pltpu.VMEM((2 * lag_width // PHASES * kept, lags * segments * samples), jnp.bfloat16),
            pltpu.VMEM((2 * PHASES * refs, lags * segments * samples), jnp.bfloat16),
        ],
        compiler_params=params,
        name="correlate",
    )(*[held[step] for step in steps(lags, segments)])


def solution(mesh):
    return jax.shard_map(
        shards,
        mesh=mesh,
        in_specs=(P("chan", "seg", "lag"), P(), P()),
        out_specs=P(("chan", "seg"), "lag"),
        check_vma=False,
    )
```

```python
import functools
import math

import jax
import jax.numpy as jnp
from jax import lax
from jax.experimental import pallas as pl
from jax.experimental.pallas import tpu as pltpu
from jax.sharding import PartitionSpec as P

LAGS = 128
SAMPLES = 2048
PHASES = 4
LAST = 2


def halves(value):
    high = value.astype(jnp.bfloat16)
    low = (value - high.astype(jnp.float32)).astype(jnp.bfloat16)
    return high, low


def product(left, right):
    return jnp.dot(left, right, preferred_element_type=jnp.float32)


def product_nt(left, right):
    return lax.dot_general(
        left, right, (((1,), (1,)), ((), ())), preferred_element_type=jnp.float32
    )


def steps(lags, segments):
    return [(lag, segment) for lag in range(lags) for segment in range(segments)]


def swapped(value, lag_step, segment_step):
    lags, segments = lax.axis_size("lag"), lax.axis_size("seg")
    pairs = [
        (lag * segments + segment, (lag ^ lag_step) * segments + (segment ^ segment_step))
        for lag, segment in steps(lags, segments)
    ]
    return lax.ppermute(value, ("lag", "seg"), pairs)


def across(value, step):
    return lax.ppermute(value, "chan", [(i, i ^ step) for i in range(lax.axis_size("chan"))])


def paired(value, order):
    lags = lax.axis_size("lag")
    pairs = [
        (chan * lags + lag, (chan ^ order[lag % 2]) * lags + lag)
        for chan in range(lax.axis_size("chan"))
        for lag in range(lags)
    ]
    return lax.ppermute(value, ("chan", "lag"), pairs)


def choice(pick, rows):
    high, low = halves(rows)
    return product(pick, high) + product(pick, low)


def counts_before(present):
    rows = present.shape[0]
    line = lax.broadcasted_iota(jnp.int32, (rows, rows), 0)
    lane = lax.broadcasted_iota(jnp.int32, (rows, rows), 1)
    return product((lane < line).astype(jnp.bfloat16), present.astype(jnp.bfloat16))


def columns(refs_ref, width):
    return jnp.broadcast_to(refs_ref[...], (width, refs_ref.shape[1])).T


def choose_four_kernel(
    records_ref,
    lists_ref,
    refs_ref,
    own_ref,
    send_ref,
    keep_ref,
    take_ref,
    held_ref,
    done,
):
    copy = pltpu.make_async_copy(records_ref, held_ref, done)
    copy.start()
    rows = lists_ref.shape[1]
    kept = take_ref.shape[1]
    refs = refs_ref.shape[1]
    me = lax.axis_index("chan")
    odd = lax.rem(lax.axis_index("lag"), 2)
    near, far = 1 + odd, 2 - odd
    line = lax.broadcasted_iota(jnp.int32, (rows, 2 * rows), 0)

    def pool(owner):
        lists = [lists_ref[pl.ds(lax.bitwise_xor(owner, i), 1), :] for i in (0, near)]
        return jnp.concatenate(lists, axis=1)

    def where(owner, block):
        return pool(owner) == line + block * rows

    def ranks(found):
        present = jnp.max(found.astype(jnp.float32), axis=1, keepdims=True)
        return present, counts_before(jnp.broadcast_to(present, (rows, rows)))

    other = lax.bitwise_xor(me, far)
    found = where(me, other)
    _, rank = ranks(found)
    rank = jnp.concatenate([rank, rank], axis=1)
    slot = jnp.sum(jnp.where(found, rank + 1.0, 0.0), axis=0, keepdims=True).astype(jnp.int32)
    send = jnp.concatenate([line[:kept] + 1 == slot, columns(refs_ref, 2 * rows) == pool(me)], axis=0)
    send = send.astype(jnp.bfloat16)
    keep = where(me, me).astype(jnp.bfloat16)
    send_ref[...] = send
    keep_ref[...] = keep
    present, rank = ranks(where(other, me))
    lane = lax.broadcasted_iota(jnp.int32, (rows, kept), 1)
    slot = jnp.where(present > 0.0, rank[:, :kept], -1.0).astype(jnp.int32)
    take_ref[...] = (lane == slot).astype(jnp.bfloat16)
    copy.wait()
    own_ref[...] = held_ref[:, 0, :]


def pick_kernel(own_ref, arrived_ref, send_ref, keep_ref, sent_ref, base_ref):
    rows = jnp.concatenate([own_ref[...], arrived_ref[:, 0, :]], axis=0)
    high, low = halves(rows)
    sent_ref[...] = product(send_ref[...], high) + product(send_ref[...], low)
    base_ref[...] = product(keep_ref[...], high) + product(keep_ref[...], low)


def put(series, panel, out_refs):
    segments = len(out_refs)
    kept = series.shape[0] // segments
    own = lax.axis_index("seg")
    for part in range(segments):
        half = lax.bitwise_xor(own, part)
        chosen = series[:kept]
        for other in range(1, segments):
            chosen = jnp.where(half == other, series[other * kept : (other + 1) * kept], chosen)
        out_refs[part][:kept, :] = chosen
        out_refs[part][kept:, :] = panel


def place_four_kernel(base_ref, take_ref, sent_ref, arrived_ref, *out_refs):
    kept = take_ref.shape[1]
    series = base_ref[...] + choice(take_ref[...], arrived_ref[:kept, :])
    put(series, sent_ref[kept:, :] + arrived_ref[kept:, :], out_refs)


def pack_kernel(records_ref, lists_ref, refs_ref, out_ref, panel_ref):
    rows = records_ref.shape[0]
    refs = refs_ref.shape[1]
    own = jnp.broadcast_to(lists_ref[pl.ds(lax.axis_index("chan"), 1), :], (rows, rows))
    rank = jnp.sum((own.T < own).astype(jnp.int32), axis=0, keepdims=True)
    line = lax.broadcasted_iota(jnp.int32, (rows, rows), 0)
    records = records_ref[:, 0, :]
    panel_ref[...] = choice((columns(refs_ref, rows) == own[:refs]).astype(jnp.bfloat16), records)
    out_ref[...] = choice((line == rank).astype(jnp.bfloat16), records)


def choose_kernel(peers, lists_ref, pick_ref):
    rows = lists_ref.shape[1]
    share = rows // peers
    lane = lax.broadcasted_iota(jnp.int32, (rows, rows), 1)
    channel = lax.broadcasted_iota(jnp.int32, (rows, rows), 0) + lax.axis_index("chan") * rows
    owner = jnp.zeros((rows, 1), jnp.int32)
    for peer in range(peers):
        found = (lists_ref[pl.ds(peer, 1), :] == channel).astype(jnp.int32)
        owner = owner + jnp.sum(found, axis=1, keepdims=True) * peer
    same = lane == owner
    before = counts_before(same.astype(jnp.float32))
    rank = jnp.sum(jnp.where(same, before, 0.0), axis=1, keepdims=True).astype(jnp.int32)
    pick_ref[...] = (lane == owner * share + rank).astype(jnp.bfloat16)


def place_kernel(pick_ref, panel_ref, arrived_ref, *out_refs):
    put(choice(pick_ref[...], arrived_ref[...]), panel_ref[...], out_refs)


def corr_kernel(refs, lag_width, *rest):
    *chunk_refs, out_ref, joined_ref, series_ref, panel_ref, total_ref, done = rest
    kept = total_ref.shape[0]
    lags, segments = lax.axis_size("lag"), lax.axis_size("seg")
    width = chunk_refs[0].shape[1]
    for (lag_step, segment_step), chunk_ref in zip(steps(lags, segments), chunk_refs):
        lag = lax.bitwise_xor(lax.axis_index("lag"), lag_step)
        segment = lax.bitwise_xor(lax.axis_index("seg"), segment_step)
        start = pl.multiple_of((segment * lags + lag) * width, width)
        joined_ref[:, pl.ds(start, width)] = chunk_ref[...]
    series = joined_ref[:kept, :]
    panel = joined_ref[kept:, :]
    samples = panel.shape[1]
    terms = SAMPLES - LAGS
    times = lax.broadcasted_iota(jnp.int32, panel.shape, 1)
    panel = jnp.where(times < terms, panel, 0.0)
    series = pltpu.roll(series, samples - lax.axis_index("lag") * lag_width, 1)
    groups = lag_width // PHASES

    def spread(value, shifts, out_ref, base):
        lines = value.shape[0]
        for half in halves(value):
            for shift in shifts:
                out_ref[base : base + lines, :] = (
                    pltpu.roll(half, shift % samples, 1) if shift else half
                )
                base += lines

    spread(panel, range(PHASES), panel_ref, 0)
    columns = PHASES * refs
    copies = []
    first = 0
    for count in (groups - LAST, LAST):
        base, lines = 2 * first * kept, count * kept
        spread(series, range(-PHASES * first, -PHASES * (first + count), -PHASES), series_ref, base)
        upper = product_nt(series_ref[base : base + 2 * lines, :], panel_ref[:columns, :])
        lower = product_nt(series_ref[base : base + lines, :], panel_ref[columns:, :])
        total = (upper[:lines] + upper[lines:] + lower) * (1.0 / math.sqrt(terms))
        for i in range(count):
            part = slice((first + i) * columns, (first + i + 1) * columns)
            total_ref[:, part] = total[i * kept : (i + 1) * kept]
            copy = pltpu.make_async_copy(
                total_ref.at[:, part], out_ref.at[:, part], done.at[first + i]
            )
            copy.start()
            copies.append(copy)
        first += count
    for copy in copies:
        copy.wait()


def shards(records_owned, section_list, ref_index):
    peers = lax.axis_size("chan")
    segments = lax.axis_size("seg")
    rows, _, samples = records_owned.shape
    refs = ref_index.shape[0]
    share = rows // peers
    kept = rows // segments
    lags = lax.axis_size("lag")
    lag_width = LAGS // lags
    lists = section_list.reshape(peers, rows)
    params = pltpu.CompilerParams(vmem_limit_bytes=48 * 1024 * 1024)
    wanted = ref_index.reshape(1, refs)

    def block(*shape, dtype=jnp.float32):
        return jax.ShapeDtypeStruct(shape, dtype)

    def call(kernel, name, shapes, *operands):
        return pl.pallas_call(kernel, out_shape=shapes, compiler_params=params, name=name)(*operands)

    shapes = [block(kept + refs, samples)] * segments
    if peers == 4:
        first = paired(records_owned, (1, 2))
        half = rows // 2
        whole = pl.BlockSpec(memory_space=pltpu.VMEM)
        own, send, keep, take = pl.pallas_call(
            choose_four_kernel,
            out_shape=[
                block(rows, samples),
                block(half + refs, 2 * rows, dtype=jnp.bfloat16),
                block(rows, 2 * rows, dtype=jnp.bfloat16),
                block(rows, half, dtype=jnp.bfloat16),
            ],
            in_specs=[pl.BlockSpec(memory_space=pl.ANY), whole, whole],
            scratch_shapes=[pltpu.VMEM(records_owned.shape, jnp.float32), pltpu.SemaphoreType.DMA],
            compiler_params=params,
            name="choose",
        )(pltpu.with_memory_space_constraint(records_owned, pltpu.HBM), lists, wanted)
        results = [block(half + refs, samples), block(rows, samples)]
        sent, base = call(pick_kernel, "pick", results, own, first, send, keep)
        placed = call(place_four_kernel, "place", shapes, base, take, sent, paired(sent, (2, 1)))
    else:
        packed, panel = call(
            pack_kernel,
            "pack",
            [block(rows, samples), block(refs, samples)],
            records_owned,
            lists,
            wanted,
        )
        blocks = packed.reshape(peers, share, samples)
        blocks = lax.all_to_all(blocks, "chan", split_axis=0, concat_axis=0, tiled=True)
        step = 1
        while step < peers:
            panel = panel + across(panel, step)
            step *= 2
        pick = call(
            functools.partial(choose_kernel, peers),
            "choose",
            block(rows, rows, dtype=jnp.bfloat16),
            lists,
        )
        placed = call(place_kernel, "place", shapes, pick, panel, blocks.reshape(rows, samples))
    held = {(0, 0): placed[0]}
    for lag_step in range(0, lags, 2):
        for segment_step in range(segments):
            if lag_step or segment_step:
                held[lag_step, segment_step] = swapped(placed[segment_step], lag_step, segment_step)
    for lag_step, segment_step in list(held):
        held[lag_step + 1, segment_step] = swapped(held[lag_step, segment_step], 1, 0)
    return pl.pallas_call(
        functools.partial(corr_kernel, refs, lag_width),
        out_shape=jax.ShapeDtypeStruct((kept, lag_width * refs), jnp.float32),
        out_specs=pl.BlockSpec(memory_space=pl.ANY),
        scratch_shapes=[
            pltpu.VMEM((kept + refs, lags * segments * samples), jnp.float32),
            pltpu.VMEM((2 * lag_width // PHASES * kept, lags * segments * samples), jnp.bfloat16),
            pltpu.VMEM((2 * PHASES * refs, lags * segments * samples), jnp.bfloat16),
            pltpu.VMEM((kept, lag_width * refs), jnp.float32),
            pltpu.SemaphoreType.DMA((lag_width // PHASES,)),
        ],
        compiler_params=params,
        name="correlate",
    )(*[held[step] for step in steps(lags, segments)])


def solution(mesh):
    return jax.shard_map(
        shards,
        mesh=mesh,
        in_specs=(P("chan", "seg", "lag"), P(), P()),
        out_specs=P(("chan", "seg"), "lag"),
        check_vma=False,
    )
```

```python
import functools
import math

import jax
import jax.numpy as jnp
from jax import lax
from jax.experimental import pallas as pl
from jax.experimental.pallas import tpu as pltpu
from jax.sharding import PartitionSpec as P

LAGS = 128
SAMPLES = 2048
PHASES = 4


def halves(value):
    high = value.astype(jnp.bfloat16)
    low = (value - high.astype(jnp.float32)).astype(jnp.bfloat16)
    return high, low


def product(left, right):
    return jnp.dot(left, right, preferred_element_type=jnp.float32)


def product_nt(left, right):
    return lax.dot_general(
        left, right, (((1,), (1,)), ((), ())), preferred_element_type=jnp.float32
    )


def steps(lags, segments):
    return [(lag, segment) for lag in range(lags) for segment in range(segments)]


def swapped(value, lag_step, segment_step):
    lags, segments = lax.axis_size("lag"), lax.axis_size("seg")
    pairs = [
        (lag * segments + segment, (lag ^ lag_step) * segments + (segment ^ segment_step))
        for lag, segment in steps(lags, segments)
    ]
    return lax.ppermute(value, ("lag", "seg"), pairs)


def across(value, step):
    return lax.ppermute(value, "chan", [(i, i ^ step) for i in range(lax.axis_size("chan"))])


def paired(value, order):
    lags = lax.axis_size("lag")
    pairs = [
        (chan * lags + lag, (chan ^ order[lag % 2]) * lags + lag)
        for chan in range(lax.axis_size("chan"))
        for lag in range(lags)
    ]
    return lax.ppermute(value, ("chan", "lag"), pairs)


def choice(pick, rows):
    high, low = halves(rows)
    return product(pick, high) + product(pick, low)


def counts_before(present):
    rows = present.shape[0]
    line = lax.broadcasted_iota(jnp.int32, (rows, rows), 0)
    lane = lax.broadcasted_iota(jnp.int32, (rows, rows), 1)
    return product((lane < line).astype(jnp.bfloat16), present.astype(jnp.bfloat16))


def columns(refs_ref, width):
    return jnp.broadcast_to(refs_ref[...], (width, refs_ref.shape[1])).T


def choose_four_kernel(
    records_ref,
    lists_ref,
    refs_ref,
    own_ref,
    send_ref,
    keep_ref,
    take_ref,
    held_ref,
    done,
):
    copy = pltpu.make_async_copy(records_ref, held_ref, done)
    copy.start()
    rows = lists_ref.shape[1]
    kept = take_ref.shape[1]
    refs = refs_ref.shape[1]
    me = lax.axis_index("chan")
    odd = lax.rem(lax.axis_index("lag"), 2)
    near, far = 1 + odd, 2 - odd
    line = lax.broadcasted_iota(jnp.int32, (rows, 2 * rows), 0)

    def pool(owner):
        lists = [lists_ref[pl.ds(lax.bitwise_xor(owner, i), 1), :] for i in (0, near)]
        return jnp.concatenate(lists, axis=1)

    def where(owner, block):
        return pool(owner) == line + block * rows

    def ranks(found):
        present = jnp.max(found.astype(jnp.float32), axis=1, keepdims=True)
        return present, counts_before(jnp.broadcast_to(present, (rows, rows)))

    other = lax.bitwise_xor(me, far)
    found = where(me, other)
    _, rank = ranks(found)
    rank = jnp.concatenate([rank, rank], axis=1)
    slot = jnp.sum(jnp.where(found, rank + 1.0, 0.0), axis=0, keepdims=True).astype(jnp.int32)
    send = jnp.concatenate([line[:kept] + 1 == slot, columns(refs_ref, 2 * rows) == pool(me)], axis=0)
    send = send.astype(jnp.bfloat16)
    keep = where(me, me).astype(jnp.bfloat16)
    send_ref[...] = send
    keep_ref[...] = keep
    present, rank = ranks(where(other, me))
    lane = lax.broadcasted_iota(jnp.int32, (rows, kept), 1)
    slot = jnp.where(present > 0.0, rank[:, :kept], -1.0).astype(jnp.int32)
    take_ref[...] = (lane == slot).astype(jnp.bfloat16)
    copy.wait()
    own_ref[...] = held_ref[:, 0, :]


def pick_kernel(own_ref, arrived_ref, send_ref, keep_ref, sent_ref, base_ref):
    rows = jnp.concatenate([own_ref[...], arrived_ref[:, 0, :]], axis=0)
    high, low = halves(rows)
    sent_ref[...] = product(send_ref[...], high) + product(send_ref[...], low)
    base_ref[...] = product(keep_ref[...], high) + product(keep_ref[...], low)


def put(series, panel, out_refs):
    segments = len(out_refs)
    kept = series.shape[0] // segments
    own = lax.axis_index("seg")
    for part in range(segments):
        half = lax.bitwise_xor(own, part)
        chosen = series[:kept]
        for other in range(1, segments):
            chosen = jnp.where(half == other, series[other * kept : (other + 1) * kept], chosen)
        out_refs[part][:kept, :] = chosen
        out_refs[part][kept:, :] = panel


def place_four_kernel(base_ref, take_ref, sent_ref, arrived_ref, *out_refs):
    kept = take_ref.shape[1]
    series = base_ref[...] + choice(take_ref[...], arrived_ref[:kept, :])
    put(series, sent_ref[kept:, :] + arrived_ref[kept:, :], out_refs)


def pack_kernel(records_ref, lists_ref, refs_ref, out_ref, panel_ref):
    rows = records_ref.shape[0]
    refs = refs_ref.shape[1]
    own = jnp.broadcast_to(lists_ref[pl.ds(lax.axis_index("chan"), 1), :], (rows, rows))
    rank = jnp.sum((own.T < own).astype(jnp.int32), axis=0, keepdims=True)
    line = lax.broadcasted_iota(jnp.int32, (rows, rows), 0)
    records = records_ref[:, 0, :]
    panel_ref[...] = choice((columns(refs_ref, rows) == own[:refs]).astype(jnp.bfloat16), records)
    out_ref[...] = choice((line == rank).astype(jnp.bfloat16), records)


def choose_kernel(peers, lists_ref, pick_ref):
    rows = lists_ref.shape[1]
    share = rows // peers
    lane = lax.broadcasted_iota(jnp.int32, (rows, rows), 1)
    channel = lax.broadcasted_iota(jnp.int32, (rows, rows), 0) + lax.axis_index("chan") * rows
    owner = jnp.zeros((rows, 1), jnp.int32)
    for peer in range(peers):
        found = (lists_ref[pl.ds(peer, 1), :] == channel).astype(jnp.int32)
        owner = owner + jnp.sum(found, axis=1, keepdims=True) * peer
    same = lane == owner
    before = counts_before(same.astype(jnp.float32))
    rank = jnp.sum(jnp.where(same, before, 0.0), axis=1, keepdims=True).astype(jnp.int32)
    pick_ref[...] = (lane == owner * share + rank).astype(jnp.bfloat16)


def place_kernel(pick_ref, panel_ref, arrived_ref, *out_refs):
    put(choice(pick_ref[...], arrived_ref[...]), panel_ref[...], out_refs)


def corr_kernel(refs, lag_width, *rest):
    *chunk_refs, out_ref, joined_ref, series_ref, panel_ref = rest
    kept = out_ref.shape[0]
    lags, segments = lax.axis_size("lag"), lax.axis_size("seg")
    width = chunk_refs[0].shape[1]
    for (lag_step, segment_step), chunk_ref in zip(reversed(steps(lags, segments)), chunk_refs):
        lag = lax.bitwise_xor(lax.axis_index("lag"), lag_step)
        segment = lax.bitwise_xor(lax.axis_index("seg"), segment_step)
        start = pl.multiple_of((segment * lags + lag) * width, width)
        joined_ref[:, pl.ds(start, width)] = chunk_ref[...]
    series = joined_ref[:kept, :]
    panel = joined_ref[kept:, :]
    samples = panel.shape[1]
    terms = SAMPLES - LAGS
    times = lax.broadcasted_iota(jnp.int32, panel.shape, 1)
    panel = jnp.where(times < terms, panel, 0.0)
    series = pltpu.roll(series, samples - lax.axis_index("lag") * lag_width, 1)
    groups = lag_width // PHASES

    def spread(value, count, step, out_ref):
        lines = value.shape[0]
        for half, part in enumerate(halves(value)):
            for i in range(count):
                start = (half * count + i) * lines
                out_ref[start : start + lines, :] = (
                    pltpu.roll(part, (i * step) % samples, 1) if i else part
                )

    spread(panel, PHASES, 1, panel_ref)
    spread(series, groups, -PHASES, series_ref)
    lines, columns = groups * kept, PHASES * refs
    upper = product_nt(series_ref[...], panel_ref[:columns, :])
    lower = product_nt(series_ref[:lines, :], panel_ref[columns:, :])
    total = (upper[:lines] + upper[lines:] + lower) * (1.0 / math.sqrt(terms))
    for group in range(groups):
        out_ref[:, group * columns : (group + 1) * columns] = total[
            group * kept : (group + 1) * kept
        ]


def shards(records_owned, section_list, ref_index):
    peers = lax.axis_size("chan")
    segments = lax.axis_size("seg")
    rows, _, samples = records_owned.shape
    refs = ref_index.shape[0]
    share = rows // peers
    kept = rows // segments
    lags = lax.axis_size("lag")
    lag_width = LAGS // lags
    lists = section_list.reshape(peers, rows)
    params = pltpu.CompilerParams(vmem_limit_bytes=48 * 1024 * 1024)
    wanted = ref_index.reshape(1, refs)

    def block(*shape, dtype=jnp.float32):
        return jax.ShapeDtypeStruct(shape, dtype)

    def call(kernel, name, shapes, *operands):
        return pl.pallas_call(kernel, out_shape=shapes, compiler_params=params, name=name)(*operands)

    shapes = [block(kept + refs, samples)] * segments
    if peers == 4:
        first = paired(records_owned, (1, 2))
        half = rows // 2
        whole = pl.BlockSpec(memory_space=pltpu.VMEM)
        own, send, keep, take = pl.pallas_call(
            choose_four_kernel,
            out_shape=[
                block(rows, samples),
                block(half + refs, 2 * rows, dtype=jnp.bfloat16),
                block(rows, 2 * rows, dtype=jnp.bfloat16),
                block(rows, half, dtype=jnp.bfloat16),
            ],
            in_specs=[pl.BlockSpec(memory_space=pl.ANY), whole, whole],
            scratch_shapes=[pltpu.VMEM(records_owned.shape, jnp.float32), pltpu.SemaphoreType.DMA],
            compiler_params=params,
            name="choose",
        )(pltpu.with_memory_space_constraint(records_owned, pltpu.HBM), lists, wanted)
        results = [block(half + refs, samples), block(rows, samples)]
        sent, base = call(pick_kernel, "pick", results, own, first, send, keep)
        placed = call(place_four_kernel, "place", shapes, base, take, sent, paired(sent, (2, 1)))
    else:
        packed, panel = call(
            pack_kernel,
            "pack",
            [block(rows, samples), block(refs, samples)],
            records_owned,
            lists,
            wanted,
        )
        blocks = packed.reshape(peers, share, samples)
        blocks = lax.all_to_all(blocks, "chan", split_axis=0, concat_axis=0, tiled=True)
        step = 1
        while step < peers:
            panel = panel + across(panel, step)
            step *= 2
        pick = call(
            functools.partial(choose_kernel, peers),
            "choose",
            block(rows, rows, dtype=jnp.bfloat16),
            lists,
        )
        placed = call(place_kernel, "place", shapes, pick, panel, blocks.reshape(rows, samples))
    held = {(0, 0): placed[0]}
    for lag_step in range(0, lags, 2):
        for segment_step in range(segments):
            if lag_step or segment_step:
                held[lag_step, segment_step] = swapped(placed[segment_step], lag_step, segment_step)
    for lag_step, segment_step in list(held):
        held[lag_step + 1, segment_step] = swapped(held[lag_step, segment_step], 1, 0)
    return pl.pallas_call(
        functools.partial(corr_kernel, refs, lag_width),
        out_shape=jax.ShapeDtypeStruct((kept, lag_width * refs), jnp.float32),
        scratch_shapes=[
            pltpu.VMEM((kept + refs, lags * segments * samples), jnp.float32),
            pltpu.VMEM((2 * lag_width // PHASES * kept, lags * segments * samples), jnp.bfloat16),
            pltpu.VMEM((2 * PHASES * refs, lags * segments * samples), jnp.bfloat16),
        ],
        compiler_params=params,
        name="correlate",
    )(*[held[step] for step in reversed(steps(lags, segments))])


def solution(mesh):
    return jax.shard_map(
        shards,
        mesh=mesh,
        in_specs=(P("chan", "seg", "lag"), P(), P()),
        out_specs=P(("chan", "seg"), "lag"),
        check_vma=False,
    )
```

```python
import functools
import math

import jax
import jax.numpy as jnp
from jax import lax
from jax.experimental import pallas as pl
from jax.experimental.pallas import tpu as pltpu
from jax.sharding import PartitionSpec as P

LAGS = 128
SAMPLES = 2048
PHASES = 4
MARGIN = 128


def halves(value):
    high = value.astype(jnp.bfloat16)
    low = (value - high.astype(jnp.float32)).astype(jnp.bfloat16)
    return high, low


def product(left, right):
    return jnp.dot(left, right, preferred_element_type=jnp.float32)


def product_nt(left, right):
    return lax.dot_general(
        left, right, (((1,), (1,)), ((), ())), preferred_element_type=jnp.float32
    )


def steps(lags, segments):
    return [(lag, segment) for lag in range(lags) for segment in range(segments)]


def swapped(value, lag_step, segment_step):
    lags, segments = lax.axis_size("lag"), lax.axis_size("seg")
    pairs = [
        (lag * segments + segment, (lag ^ lag_step) * segments + (segment ^ segment_step))
        for lag, segment in steps(lags, segments)
    ]
    return lax.ppermute(value, ("lag", "seg"), pairs)


def across(value, step):
    return lax.ppermute(value, "chan", [(i, i ^ step) for i in range(lax.axis_size("chan"))])


def paired(value, order):
    lags = lax.axis_size("lag")
    pairs = [
        (chan * lags + lag, (chan ^ order[lag % 2]) * lags + lag)
        for chan in range(lax.axis_size("chan"))
        for lag in range(lags)
    ]
    return lax.ppermute(value, ("chan", "lag"), pairs)


def choice(pick, rows):
    high, low = halves(rows)
    return product(pick, high) + product(pick, low)


def counts_before(present):
    rows = present.shape[0]
    line = lax.broadcasted_iota(jnp.int32, (rows, rows), 0)
    lane = lax.broadcasted_iota(jnp.int32, (rows, rows), 1)
    return product((lane < line).astype(jnp.bfloat16), present.astype(jnp.bfloat16))


def columns(refs_ref, width):
    return jnp.broadcast_to(refs_ref[...], (width, refs_ref.shape[1])).T


def choose_four_kernel(
    records_ref,
    lists_ref,
    refs_ref,
    own_ref,
    send_ref,
    keep_ref,
    take_ref,
    held_ref,
    done,
):
    copy = pltpu.make_async_copy(records_ref, held_ref, done)
    copy.start()
    rows = lists_ref.shape[1]
    kept = take_ref.shape[1]
    refs = refs_ref.shape[1]
    me = lax.axis_index("chan")
    odd = lax.rem(lax.axis_index("lag"), 2)
    near, far = 1 + odd, 2 - odd
    line = lax.broadcasted_iota(jnp.int32, (rows, 2 * rows), 0)

    def pool(owner):
        lists = [lists_ref[pl.ds(lax.bitwise_xor(owner, i), 1), :] for i in (0, near)]
        return jnp.concatenate(lists, axis=1)

    def where(owner, block):
        return pool(owner) == line + block * rows

    def ranks(found):
        present = jnp.max(found.astype(jnp.float32), axis=1, keepdims=True)
        return present, counts_before(jnp.broadcast_to(present, (rows, rows)))

    other = lax.bitwise_xor(me, far)
    found = where(me, other)
    _, rank = ranks(found)
    rank = jnp.concatenate([rank, rank], axis=1)
    slot = jnp.sum(jnp.where(found, rank + 1.0, 0.0), axis=0, keepdims=True).astype(jnp.int32)
    send = jnp.concatenate([line[:kept] + 1 == slot, columns(refs_ref, 2 * rows) == pool(me)], axis=0)
    send = send.astype(jnp.bfloat16)
    keep = where(me, me).astype(jnp.bfloat16)
    send_ref[...] = send
    keep_ref[...] = keep
    present, rank = ranks(where(other, me))
    lane = lax.broadcasted_iota(jnp.int32, (rows, kept), 1)
    slot = jnp.where(present > 0.0, rank[:, :kept], -1.0).astype(jnp.int32)
    take_ref[...] = (lane == slot).astype(jnp.bfloat16)
    copy.wait()
    own_ref[...] = held_ref[:, 0, :]


def pick_kernel(own_ref, arrived_ref, send_ref, keep_ref, sent_ref, base_ref):
    rows = jnp.concatenate([own_ref[...], arrived_ref[:, 0, :]], axis=0)
    high, low = halves(rows)
    sent_ref[...] = product(send_ref[...], high) + product(send_ref[...], low)
    base_ref[...] = product(keep_ref[...], high) + product(keep_ref[...], low)


def put(series, panel, out_refs):
    segments = len(out_refs)
    kept = series.shape[0] // segments
    own = lax.axis_index("seg")
    for part in range(segments):
        half = lax.bitwise_xor(own, part)
        chosen = series[:kept]
        for other in range(1, segments):
            chosen = jnp.where(half == other, series[other * kept : (other + 1) * kept], chosen)
        out_refs[part][:kept, :] = chosen
        out_refs[part][kept:, :] = panel


def place_four_kernel(base_ref, take_ref, sent_ref, arrived_ref, *out_refs):
    kept = take_ref.shape[1]
    series = base_ref[...] + choice(take_ref[...], arrived_ref[:kept, :])
    put(series, sent_ref[kept:, :] + arrived_ref[kept:, :], out_refs)


def pack_kernel(records_ref, lists_ref, refs_ref, out_ref, panel_ref):
    rows = records_ref.shape[0]
    refs = refs_ref.shape[1]
    own = jnp.broadcast_to(lists_ref[pl.ds(lax.axis_index("chan"), 1), :], (rows, rows))
    rank = jnp.sum((own.T < own).astype(jnp.int32), axis=0, keepdims=True)
    line = lax.broadcasted_iota(jnp.int32, (rows, rows), 0)
    records = records_ref[:, 0, :]
    panel_ref[...] = choice((columns(refs_ref, rows) == own[:refs]).astype(jnp.bfloat16), records)
    out_ref[...] = choice((line == rank).astype(jnp.bfloat16), records)


def choose_kernel(peers, lists_ref, pick_ref):
    rows = lists_ref.shape[1]
    share = rows // peers
    lane = lax.broadcasted_iota(jnp.int32, (rows, rows), 1)
    channel = lax.broadcasted_iota(jnp.int32, (rows, rows), 0) + lax.axis_index("chan") * rows
    owner = jnp.zeros((rows, 1), jnp.int32)
    for peer in range(peers):
        found = (lists_ref[pl.ds(peer, 1), :] == channel).astype(jnp.int32)
        owner = owner + jnp.sum(found, axis=1, keepdims=True) * peer
    same = lane == owner
    before = counts_before(same.astype(jnp.float32))
    rank = jnp.sum(jnp.where(same, before, 0.0), axis=1, keepdims=True).astype(jnp.int32)
    pick_ref[...] = (lane == owner * share + rank).astype(jnp.bfloat16)


def place_kernel(pick_ref, panel_ref, arrived_ref, *out_refs):
    put(choice(pick_ref[...], arrived_ref[...]), panel_ref[...], out_refs)


def join(chunk_refs, joined_ref):
    width = chunk_refs[0].shape[1]
    for lag_step, chunk_ref in enumerate(chunk_refs):
        lag = lax.bitwise_xor(lax.axis_index("lag"), lag_step)
        joined_ref[:, pl.ds(pl.multiple_of(lag * width, width), width)] = chunk_ref[...]


def within(panel, segment):
    samples = panel.shape[1]
    times = lax.broadcasted_iota(jnp.int32, panel.shape, 1) + segment * samples
    return jnp.where(times < SAMPLES - LAGS, panel, 0.0)


def spread(series, panel, lag_width, series_ref, panel_ref, start):
    span = series.shape[1]
    length = span - MARGIN
    series = pltpu.roll(series, span - lax.axis_index("lag") * lag_width, 1)
    for value, shifts, first, out_ref in (
        (panel, range(PHASES), MARGIN, panel_ref),
        (series, range(0, -lag_width, -PHASES), 0, series_ref),
    ):
        lines, base = value.shape[0], 0
        for half in halves(value):
            for shift in shifts:
                moved = pltpu.roll(half, shift % span, 1) if shift else half
                out_ref[base : base + lines, start : start + length] = moved[:, first : first + length]
                base += lines


def products(series_ref, panel_ref):
    lines, columns = series_ref.shape[0] // 2, panel_ref.shape[0] // 2
    upper = product_nt(series_ref[...], panel_ref[:columns, :])
    lower = product_nt(series_ref[:lines, :], panel_ref[columns:, :])
    return upper[:lines] + upper[lines:] + lower


def other_kernel(kept, lag_width, *rest):
    *chunk_refs, partial_ref, head_ref, tail_ref, joined_ref, series_ref, panel_ref = rest
    join(chunk_refs, joined_ref)
    series = joined_ref[:kept, :]
    panel = within(joined_ref[kept:, :], 1 - lax.axis_index("seg"))
    head_ref[...] = series[:, : 2 * MARGIN]
    tail_ref[...] = panel[:, -MARGIN:]
    nothing = jnp.zeros((kept, MARGIN), jnp.float32)
    spread(
        jnp.concatenate([series, nothing], axis=1),
        jnp.concatenate([nothing, panel], axis=1),
        lag_width,
        series_ref,
        panel_ref,
        0,
    )
    partial_ref[...] = products(series_ref, panel_ref)


def own_kernel(kept, lag_width, partial_ref, head_ref, tail_ref, *rest):
    *chunk_refs, out_ref, joined_ref, series_ref, panel_ref = rest
    join(chunk_refs, joined_ref)
    segment = lax.axis_index("seg")
    series = joined_ref[:kept, :]
    panel = within(joined_ref[kept:, :], segment)
    length = series.shape[1]
    nothing = jnp.zeros((kept, MARGIN), jnp.float32)
    head = jnp.where(segment == 0, head_ref[...], series[:, : 2 * MARGIN])
    tail = jnp.where(segment == 0, panel[:, -MARGIN:], tail_ref[...])
    spread(
        jnp.concatenate([series, nothing], axis=1),
        jnp.concatenate([nothing, panel], axis=1),
        lag_width,
        series_ref,
        panel_ref,
        0,
    )
    spread(
        jnp.concatenate([nothing, head], axis=1),
        jnp.concatenate([nothing, tail, nothing], axis=1),
        lag_width,
        series_ref,
        panel_ref,
        length,
    )
    total = products(series_ref, panel_ref) + partial_ref[...]
    total = total * (1.0 / math.sqrt(SAMPLES - LAGS))
    columns = total.shape[1]
    for group in range(total.shape[0] // kept):
        out_ref[:, group * columns : (group + 1) * columns] = total[
            group * kept : (group + 1) * kept
        ]


def shards(records_owned, section_list, ref_index):
    peers = lax.axis_size("chan")
    segments = lax.axis_size("seg")
    rows, _, samples = records_owned.shape
    refs = ref_index.shape[0]
    share = rows // peers
    kept = rows // segments
    lags = lax.axis_size("lag")
    lag_width = LAGS // lags
    lists = section_list.reshape(peers, rows)
    params = pltpu.CompilerParams(vmem_limit_bytes=48 * 1024 * 1024)
    wanted = ref_index.reshape(1, refs)

    def block(*shape, dtype=jnp.float32):
        return jax.ShapeDtypeStruct(shape, dtype)

    def call(kernel, name, shapes, *operands):
        return pl.pallas_call(kernel, out_shape=shapes, compiler_params=params, name=name)(*operands)

    shapes = [block(kept + refs, samples)] * segments
    if peers == 4:
        first = paired(records_owned, (1, 2))
        half = rows // 2
        whole = pl.BlockSpec(memory_space=pltpu.VMEM)
        own, send, keep, take = pl.pallas_call(
            choose_four_kernel,
            out_shape=[
                block(rows, samples),
                block(half + refs, 2 * rows, dtype=jnp.bfloat16),
                block(rows, 2 * rows, dtype=jnp.bfloat16),
                block(rows, half, dtype=jnp.bfloat16),
            ],
            in_specs=[pl.BlockSpec(memory_space=pl.ANY), whole, whole],
            scratch_shapes=[pltpu.VMEM(records_owned.shape, jnp.float32), pltpu.SemaphoreType.DMA],
            compiler_params=params,
            name="choose",
        )(pltpu.with_memory_space_constraint(records_owned, pltpu.HBM), lists, wanted)
        results = [block(half + refs, samples), block(rows, samples)]
        sent, base = call(pick_kernel, "pick", results, own, first, send, keep)
        placed = call(place_four_kernel, "place", shapes, base, take, sent, paired(sent, (2, 1)))
    else:
        packed, panel = call(
            pack_kernel,
            "pack",
            [block(rows, samples), block(refs, samples)],
            records_owned,
            lists,
            wanted,
        )
        blocks = packed.reshape(peers, share, samples)
        blocks = lax.all_to_all(blocks, "chan", split_axis=0, concat_axis=0, tiled=True)
        step = 1
        while step < peers:
            panel = panel + across(panel, step)
            step *= 2
        pick = call(
            functools.partial(choose_kernel, peers),
            "choose",
            block(rows, rows, dtype=jnp.bfloat16),
            lists,
        )
        placed = call(place_kernel, "place", shapes, pick, panel, blocks.reshape(rows, samples))
    held = {(0, 0): placed[0]}
    for lag_step in range(0, lags, 2):
        for segment_step in range(segments):
            if lag_step or segment_step:
                held[lag_step, segment_step] = swapped(placed[segment_step], lag_step, segment_step)
    for lag_step, segment_step in list(held):
        held[lag_step + 1, segment_step] = swapped(held[lag_step, segment_step], 1, 0)
    length = lags * samples
    lines, columns = lag_width // PHASES * kept, PHASES * refs

    def scratch(width):
        return [
            pltpu.VMEM((kept + refs, length), jnp.float32),
            pltpu.VMEM((2 * lines, width), jnp.bfloat16),
            pltpu.VMEM((2 * columns, width), jnp.bfloat16),
        ]

    other = pl.pallas_call(
        functools.partial(other_kernel, kept, lag_width),
        out_shape=[block(lines, columns), block(kept, 2 * MARGIN), block(refs, MARGIN)],
        scratch_shapes=scratch(length),
        compiler_params=params,
        name="other",
    )(*[held[lag_step, 1] for lag_step in range(lags)])
    return pl.pallas_call(
        functools.partial(own_kernel, kept, lag_width),
        out_shape=block(kept, lag_width * refs),
        scratch_shapes=scratch(length + 2 * MARGIN),
        compiler_params=params,
        name="own",
    )(*other, *[held[lag_step, 0] for lag_step in range(lags)])


def solution(mesh):
    return jax.shard_map(
        shards,
        mesh=mesh,
        in_specs=(P("chan", "seg", "lag"), P(), P()),
        out_specs=P(("chan", "seg"), "lag"),
        check_vma=False,
    )
```

```python
import functools
import math

import jax
import jax.numpy as jnp
from jax import lax
from jax.experimental import pallas as pl
from jax.experimental.pallas import tpu as pltpu
from jax.sharding import PartitionSpec as P

LAGS = 128
SAMPLES = 2048
PHASES = 4


def halves(value):
    high = value.astype(jnp.bfloat16)
    low = (value - high.astype(jnp.float32)).astype(jnp.bfloat16)
    return high, low


def product(left, right):
    return jnp.dot(left, right, preferred_element_type=jnp.float32)


def product_nt(left, right):
    return lax.dot_general(
        left, right, (((1,), (1,)), ((), ())), preferred_element_type=jnp.float32
    )


def steps(lags, segments):
    return [(lag, segment) for lag in range(lags) for segment in range(segments)]


def swapped(value, lag_step, segment_step):
    lags, segments = lax.axis_size("lag"), lax.axis_size("seg")
    pairs = [
        (lag * segments + segment, (lag ^ lag_step) * segments + (segment ^ segment_step))
        for lag, segment in steps(lags, segments)
    ]
    return lax.ppermute(value, ("lag", "seg"), pairs)


def across(value, step):
    return lax.ppermute(value, "chan", [(i, i ^ step) for i in range(lax.axis_size("chan"))])


def paired(value, order):
    lags = lax.axis_size("lag")
    pairs = [
        (chan * lags + lag, (chan ^ order[lag % 2]) * lags + lag)
        for chan in range(lax.axis_size("chan"))
        for lag in range(lags)
    ]
    return lax.ppermute(value, ("chan", "lag"), pairs)


def choice(pick, rows):
    high, low = halves(rows)
    return product(pick, high) + product(pick, low)


def counts_before(present):
    rows = present.shape[0]
    line = lax.broadcasted_iota(jnp.int32, (rows, rows), 0)
    lane = lax.broadcasted_iota(jnp.int32, (rows, rows), 1)
    return product((lane < line).astype(jnp.bfloat16), present.astype(jnp.bfloat16))


def columns(refs_ref, width):
    return jnp.broadcast_to(refs_ref[...], (width, refs_ref.shape[1])).T


def choose_four_kernel(
    records_ref,
    lists_ref,
    refs_ref,
    own_ref,
    send_ref,
    keep_ref,
    take_ref,
    held_ref,
    done,
):
    copy = pltpu.make_async_copy(records_ref, held_ref, done)
    copy.start()
    rows = lists_ref.shape[1]
    kept = take_ref.shape[1]
    refs = refs_ref.shape[1]
    me = lax.axis_index("chan")
    odd = lax.rem(lax.axis_index("lag"), 2)
    near, far = 1 + odd, 2 - odd
    line = lax.broadcasted_iota(jnp.int32, (rows, 2 * rows), 0)

    def pool(owner):
        lists = [lists_ref[pl.ds(lax.bitwise_xor(owner, i), 1), :] for i in (0, near)]
        return jnp.concatenate(lists, axis=1)

    def where(owner, block):
        return pool(owner) == line + block * rows

    def ranks(found):
        present = jnp.max(found.astype(jnp.float32), axis=1, keepdims=True)
        return present, counts_before(jnp.broadcast_to(present, (rows, rows)))

    other = lax.bitwise_xor(me, far)
    found = where(me, other)
    _, rank = ranks(found)
    rank = jnp.concatenate([rank, rank], axis=1)
    slot = jnp.sum(jnp.where(found, rank + 1.0, 0.0), axis=0, keepdims=True).astype(jnp.int32)
    send = jnp.concatenate([line[:kept] + 1 == slot, columns(refs_ref, 2 * rows) == pool(me)], axis=0)
    send = send.astype(jnp.bfloat16)
    keep = where(me, me).astype(jnp.bfloat16)
    send_ref[...] = send
    keep_ref[...] = keep
    present, rank = ranks(where(other, me))
    lane = lax.broadcasted_iota(jnp.int32, (rows, kept), 1)
    slot = jnp.where(present > 0.0, rank[:, :kept], -1.0).astype(jnp.int32)
    take_ref[...] = (lane == slot).astype(jnp.bfloat16)
    copy.wait()
    own_ref[...] = held_ref[:, 0, :]


def pick_kernel(own_ref, arrived_ref, send_ref, keep_ref, sent_ref, base_ref):
    rows = jnp.concatenate([own_ref[...], arrived_ref[:, 0, :]], axis=0)
    high, low = halves(rows)
    sent_ref[...] = product(send_ref[...], high) + product(send_ref[...], low)
    base_ref[...] = product(keep_ref[...], high) + product(keep_ref[...], low)


def put(series, panel, out_refs):
    segments = len(out_refs) - 1
    kept = series.shape[0] // segments
    own = lax.axis_index("seg")
    for part in range(segments):
        half = lax.bitwise_xor(own, part)
        chosen = series[:kept]
        for other in range(1, segments):
            chosen = jnp.where(half == other, series[other * kept : (other + 1) * kept], chosen)
        for out_ref in out_refs[::segments] if part == 0 else [out_refs[part]]:
            out_ref[:kept, :] = chosen
            out_ref[kept:, :] = panel


def place_four_kernel(base_ref, take_ref, sent_ref, arrived_ref, *out_refs):
    kept = take_ref.shape[1]
    series = base_ref[...] + choice(take_ref[...], arrived_ref[:kept, :])
    put(series, sent_ref[kept:, :] + arrived_ref[kept:, :], out_refs)


def pack_kernel(records_ref, lists_ref, refs_ref, out_ref, panel_ref):
    rows = records_ref.shape[0]
    refs = refs_ref.shape[1]
    own = jnp.broadcast_to(lists_ref[pl.ds(lax.axis_index("chan"), 1), :], (rows, rows))
    rank = jnp.sum((own.T < own).astype(jnp.int32), axis=0, keepdims=True)
    line = lax.broadcasted_iota(jnp.int32, (rows, rows), 0)
    records = records_ref[:, 0, :]
    panel_ref[...] = choice((columns(refs_ref, rows) == own[:refs]).astype(jnp.bfloat16), records)
    out_ref[...] = choice((line == rank).astype(jnp.bfloat16), records)


def choose_kernel(peers, lists_ref, pick_ref):
    rows = lists_ref.shape[1]
    share = rows // peers
    lane = lax.broadcasted_iota(jnp.int32, (rows, rows), 1)
    channel = lax.broadcasted_iota(jnp.int32, (rows, rows), 0) + lax.axis_index("chan") * rows
    owner = jnp.zeros((rows, 1), jnp.int32)
    for peer in range(peers):
        found = (lists_ref[pl.ds(peer, 1), :] == channel).astype(jnp.int32)
        owner = owner + jnp.sum(found, axis=1, keepdims=True) * peer
    same = lane == owner
    before = counts_before(same.astype(jnp.float32))
    rank = jnp.sum(jnp.where(same, before, 0.0), axis=1, keepdims=True).astype(jnp.int32)
    pick_ref[...] = (lane == owner * share + rank).astype(jnp.bfloat16)


def place_kernel(pick_ref, panel_ref, arrived_ref, *out_refs):
    put(choice(pick_ref[...], arrived_ref[...]), panel_ref[...], out_refs)


def corr_kernel(refs, lag_width, *rest):
    *chunk_refs, out_ref, joined_ref, series_ref, panel_ref = rest
    kept = out_ref.shape[0]
    lags, segments = lax.axis_size("lag"), lax.axis_size("seg")
    width = chunk_refs[0].shape[1]
    for (lag_step, segment_step), chunk_ref in zip(reversed(steps(lags, segments)), chunk_refs):
        lag = lax.bitwise_xor(lax.axis_index("lag"), lag_step)
        segment = lax.bitwise_xor(lax.axis_index("seg"), segment_step)
        start = pl.multiple_of((segment * lags + lag) * width, width)
        joined_ref[:, pl.ds(start, width)] = chunk_ref[...]
    series = joined_ref[:kept, :]
    panel = joined_ref[kept:, :]
    samples = panel.shape[1]
    terms = SAMPLES - LAGS
    times = lax.broadcasted_iota(jnp.int32, panel.shape, 1)
    panel = jnp.where(times < terms, panel, 0.0)
    series = pltpu.roll(series, samples - lax.axis_index("lag") * lag_width, 1)
    groups = lag_width // PHASES

    def spread(value, count, step, out_ref):
        lines = value.shape[0]
        for half, part in enumerate(halves(value)):
            for i in range(count):
                start = (half * count + i) * lines
                out_ref[start : start + lines, :] = (
                    pltpu.roll(part, (i * step) % samples, 1) if i else part
                )

    spread(panel, PHASES, 1, panel_ref)
    spread(series, groups, -PHASES, series_ref)
    lines, columns = groups * kept, PHASES * refs
    upper = product_nt(series_ref[...], panel_ref[:columns, :])
    lower = product_nt(series_ref[:lines, :], panel_ref[columns:, :])
    total = (upper[:lines] + upper[lines:] + lower) * (1.0 / math.sqrt(terms))
    for group in range(groups):
        out_ref[:, group * columns : (group + 1) * columns] = total[
            group * kept : (group + 1) * kept
        ]


def shards(records_owned, section_list, ref_index):
    peers = lax.axis_size("chan")
    segments = lax.axis_size("seg")
    rows, _, samples = records_owned.shape
    refs = ref_index.shape[0]
    share = rows // peers
    kept = rows // segments
    lags = lax.axis_size("lag")
    lag_width = LAGS // lags
    lists = section_list.reshape(peers, rows)
    params = pltpu.CompilerParams(vmem_limit_bytes=48 * 1024 * 1024)
    wanted = ref_index.reshape(1, refs)

    def block(*shape, dtype=jnp.float32):
        return jax.ShapeDtypeStruct(shape, dtype)

    def call(kernel, name, shapes, *operands):
        return pl.pallas_call(kernel, out_shape=shapes, compiler_params=params, name=name)(*operands)

    shapes = [block(kept + refs, samples)] * (segments + 1)
    if peers == 4:
        first = paired(records_owned, (1, 2))
        half = rows // 2
        whole = pl.BlockSpec(memory_space=pltpu.VMEM)
        own, send, keep, take = pl.pallas_call(
            choose_four_kernel,
            out_shape=[
                block(rows, samples),
                block(half + refs, 2 * rows, dtype=jnp.bfloat16),
                block(rows, 2 * rows, dtype=jnp.bfloat16),
                block(rows, half, dtype=jnp.bfloat16),
            ],
            in_specs=[pl.BlockSpec(memory_space=pl.ANY), whole, whole],
            scratch_shapes=[pltpu.VMEM(records_owned.shape, jnp.float32), pltpu.SemaphoreType.DMA],
            compiler_params=params,
            name="choose",
        )(pltpu.with_memory_space_constraint(records_owned, pltpu.HBM), lists, wanted)
        results = [block(half + refs, samples), block(rows, samples)]
        sent, base = call(pick_kernel, "pick", results, own, first, send, keep)
        placed = call(place_four_kernel, "place", shapes, base, take, sent, paired(sent, (2, 1)))
    else:
        packed, panel = call(
            pack_kernel,
            "pack",
            [block(rows, samples), block(refs, samples)],
            records_owned,
            lists,
            wanted,
        )
        blocks = packed.reshape(peers, share, samples)
        blocks = lax.all_to_all(blocks, "chan", split_axis=0, concat_axis=0, tiled=True)
        step = 1
        while step < peers:
            panel = panel + across(panel, step)
            step *= 2
        pick = call(
            functools.partial(choose_kernel, peers),
            "choose",
            block(rows, rows, dtype=jnp.bfloat16),
            lists,
        )
        placed = call(place_kernel, "place", shapes, pick, panel, blocks.reshape(rows, samples))
    held = {(0, 0): placed[0]}
    for lag_step in range(0, lags, 2):
        for segment_step in range(segments):
            if lag_step or segment_step:
                part = placed[segment_step or segments]
                held[lag_step, segment_step] = swapped(part, lag_step, segment_step)
    for lag_step, segment_step in list(held):
        held[lag_step + 1, segment_step] = swapped(held[lag_step, segment_step], 1, 0)
    return pl.pallas_call(
        functools.partial(corr_kernel, refs, lag_width),
        out_shape=jax.ShapeDtypeStruct((kept, lag_width * refs), jnp.float32),
        scratch_shapes=[
            pltpu.VMEM((kept + refs, lags * segments * samples), jnp.float32),
            pltpu.VMEM((2 * lag_width // PHASES * kept, lags * segments * samples), jnp.bfloat16),
            pltpu.VMEM((2 * PHASES * refs, lags * segments * samples), jnp.bfloat16),
        ],
        compiler_params=params,
        name="correlate",
    )(*[held[step] for step in reversed(steps(lags, segments))])


def solution(mesh):
    return jax.shard_map(
        shards,
        mesh=mesh,
        in_specs=(P("chan", "seg", "lag"), P(), P()),
        out_specs=P(("chan", "seg"), "lag"),
        check_vma=False,
    )
```

```python
import functools
import math

import jax
import jax.numpy as jnp
from jax import lax
from jax.experimental import pallas as pl
from jax.experimental.pallas import tpu as pltpu
from jax.sharding import PartitionSpec as P

LAGS = 128
SAMPLES = 2048
PHASES = 8


def halves(value):
    high = value.astype(jnp.bfloat16)
    low = (value - high.astype(jnp.float32)).astype(jnp.bfloat16)
    return high, low


def product(left, right):
    return jnp.dot(left, right, preferred_element_type=jnp.float32)


def product_nt(left, right):
    return lax.dot_general(
        left, right, (((1,), (1,)), ((), ())), preferred_element_type=jnp.float32
    )


def steps(lags, segments):
    return [(lag, segment) for lag in range(lags) for segment in range(segments)]


def swapped(value, lag_step, segment_step):
    lags, segments = lax.axis_size("lag"), lax.axis_size("seg")
    pairs = [
        (lag * segments + segment, (lag ^ lag_step) * segments + (segment ^ segment_step))
        for lag, segment in steps(lags, segments)
    ]
    return lax.ppermute(value, ("lag", "seg"), pairs)


def across(value, step):
    return lax.ppermute(value, "chan", [(i, i ^ step) for i in range(lax.axis_size("chan"))])


def paired(value, order):
    lags = lax.axis_size("lag")
    pairs = [
        (chan * lags + lag, (chan ^ order[lag % 2]) * lags + lag)
        for chan in range(lax.axis_size("chan"))
        for lag in range(lags)
    ]
    return lax.ppermute(value, ("chan", "lag"), pairs)


def choice(pick, rows):
    high, low = halves(rows)
    return product(pick, high) + product(pick, low)


def counts_before(present):
    rows = present.shape[0]
    line = lax.broadcasted_iota(jnp.int32, (rows, rows), 0)
    lane = lax.broadcasted_iota(jnp.int32, (rows, rows), 1)
    return product((lane < line).astype(jnp.bfloat16), present.astype(jnp.bfloat16))


def columns(refs_ref, width):
    return jnp.broadcast_to(refs_ref[...], (width, refs_ref.shape[1])).T


def choose_four_kernel(
    records_ref,
    lists_ref,
    refs_ref,
    own_ref,
    send_ref,
    keep_ref,
    take_ref,
    held_ref,
    done,
):
    copy = pltpu.make_async_copy(records_ref, held_ref, done)
    copy.start()
    rows = lists_ref.shape[1]
    kept = take_ref.shape[1]
    refs = refs_ref.shape[1]
    me = lax.axis_index("chan")
    odd = lax.rem(lax.axis_index("lag"), 2)
    near, far = 1 + odd, 2 - odd
    line = lax.broadcasted_iota(jnp.int32, (rows, 2 * rows), 0)

    def pool(owner):
        lists = [lists_ref[pl.ds(lax.bitwise_xor(owner, i), 1), :] for i in (0, near)]
        return jnp.concatenate(lists, axis=1)

    def where(owner, block):
        return pool(owner) == line + block * rows

    def ranks(found):
        present = jnp.max(found.astype(jnp.float32), axis=1, keepdims=True)
        return present, counts_before(jnp.broadcast_to(present, (rows, rows)))

    other = lax.bitwise_xor(me, far)
    found = where(me, other)
    _, rank = ranks(found)
    rank = jnp.concatenate([rank, rank], axis=1)
    slot = jnp.sum(jnp.where(found, rank + 1.0, 0.0), axis=0, keepdims=True).astype(jnp.int32)
    send = jnp.concatenate([line[:kept] + 1 == slot, columns(refs_ref, 2 * rows) == pool(me)], axis=0)
    send = send.astype(jnp.bfloat16)
    keep = where(me, me).astype(jnp.bfloat16)
    send_ref[...] = send
    keep_ref[...] = keep
    present, rank = ranks(where(other, me))
    lane = lax.broadcasted_iota(jnp.int32, (rows, kept), 1)
    slot = jnp.where(present > 0.0, rank[:, :kept], -1.0).astype(jnp.int32)
    take_ref[...] = (lane == slot).astype(jnp.bfloat16)
    copy.wait()
    own_ref[...] = held_ref[:, 0, :]


def pick_kernel(own_ref, arrived_ref, send_ref, keep_ref, sent_ref, base_ref):
    rows = jnp.concatenate([own_ref[...], arrived_ref[:, 0, :]], axis=0)
    high, low = halves(rows)
    sent_ref[...] = product(send_ref[...], high) + product(send_ref[...], low)
    base_ref[...] = product(keep_ref[...], high) + product(keep_ref[...], low)


def put(series, panel, out_refs):
    segments = len(out_refs)
    kept = series.shape[0] // segments
    own = lax.axis_index("seg")
    for part in range(segments):
        half = lax.bitwise_xor(own, part)
        chosen = series[:kept]
        for other in range(1, segments):
            chosen = jnp.where(half == other, series[other * kept : (other + 1) * kept], chosen)
        out_refs[part][:kept, :] = chosen
        out_refs[part][kept:, :] = panel


def place_four_kernel(base_ref, take_ref, sent_ref, arrived_ref, *out_refs):
    kept = take_ref.shape[1]
    series = base_ref[...] + choice(take_ref[...], arrived_ref[:kept, :])
    put(series, sent_ref[kept:, :] + arrived_ref[kept:, :], out_refs)


def pack_kernel(records_ref, lists_ref, refs_ref, out_ref, panel_ref):
    rows = records_ref.shape[0]
    refs = refs_ref.shape[1]
    own = jnp.broadcast_to(lists_ref[pl.ds(lax.axis_index("chan"), 1), :], (rows, rows))
    rank = jnp.sum((own.T < own).astype(jnp.int32), axis=0, keepdims=True)
    line = lax.broadcasted_iota(jnp.int32, (rows, rows), 0)
    records = records_ref[:, 0, :]
    panel_ref[...] = choice((columns(refs_ref, rows) == own[:refs]).astype(jnp.bfloat16), records)
    out_ref[...] = choice((line == rank).astype(jnp.bfloat16), records)


def choose_kernel(peers, lists_ref, pick_ref):
    rows = lists_ref.shape[1]
    share = rows // peers
    lane = lax.broadcasted_iota(jnp.int32, (rows, rows), 1)
    channel = lax.broadcasted_iota(jnp.int32, (rows, rows), 0) + lax.axis_index("chan") * rows
    owner = jnp.zeros((rows, 1), jnp.int32)
    for peer in range(peers):
        found = (lists_ref[pl.ds(peer, 1), :] == channel).astype(jnp.int32)
        owner = owner + jnp.sum(found, axis=1, keepdims=True) * peer
    same = lane == owner
    before = counts_before(same.astype(jnp.float32))
    rank = jnp.sum(jnp.where(same, before, 0.0), axis=1, keepdims=True).astype(jnp.int32)
    pick_ref[...] = (lane == owner * share + rank).astype(jnp.bfloat16)


def place_kernel(pick_ref, panel_ref, arrived_ref, *out_refs):
    put(choice(pick_ref[...], arrived_ref[...]), panel_ref[...], out_refs)


def corr_kernel(refs, lag_width, *rest):
    *chunk_refs, out_ref, joined_ref, series_ref, panel_ref = rest
    kept = out_ref.shape[0]
    lags, segments = lax.axis_size("lag"), lax.axis_size("seg")
    width = chunk_refs[0].shape[1]
    for (lag_step, segment_step), chunk_ref in zip(steps(lags, segments), chunk_refs):
        lag = lax.bitwise_xor(lax.axis_index("lag"), lag_step)
        segment = lax.bitwise_xor(lax.axis_index("seg"), segment_step)
        start = pl.multiple_of((segment * lags + lag) * width, width)
        joined_ref[:, pl.ds(start, width)] = chunk_ref[...]
    series = joined_ref[:kept, :]
    panel = joined_ref[kept:, :]
    samples = panel.shape[1]
    terms = SAMPLES - LAGS
    times = lax.broadcasted_iota(jnp.int32, panel.shape, 1)
    panel = jnp.where(times < terms, panel, 0.0)
    series = pltpu.roll(series, samples - lax.axis_index("lag") * lag_width, 1)
    groups = lag_width // PHASES

    def spread(value, count, step, out_ref):
        lines = value.shape[0]
        for half, part in enumerate(halves(value)):
            for i in range(count):
                start = (half * count + i) * lines
                out_ref[start : start + lines, :] = (
                    pltpu.roll(part, (i * step) % samples, 1) if i else part
                )

    spread(panel, PHASES, 1, panel_ref)
    spread(series, groups, -PHASES, series_ref)
    lines, columns = groups * kept, PHASES * refs
    upper = product_nt(series_ref[...], panel_ref[:columns, :])
    lower = product_nt(series_ref[:lines, :], panel_ref[columns:, :])
    total = (upper[:lines] + upper[lines:] + lower) * (1.0 / math.sqrt(terms))
    for group in range(groups):
        out_ref[:, group * columns : (group + 1) * columns] = total[
            group * kept : (group + 1) * kept
        ]


def shards(records_owned, section_list, ref_index):
    peers = lax.axis_size("chan")
    segments = lax.axis_size("seg")
    rows, _, samples = records_owned.shape
    refs = ref_index.shape[0]
    share = rows // peers
    kept = rows // segments
    lags = lax.axis_size("lag")
    lag_width = LAGS // lags
    lists = section_list.reshape(peers, rows)
    params = pltpu.CompilerParams(vmem_limit_bytes=48 * 1024 * 1024)
    wanted = ref_index.reshape(1, refs)

    def block(*shape, dtype=jnp.float32):
        return jax.ShapeDtypeStruct(shape, dtype)

    def call(kernel, name, shapes, *operands):
        return pl.pallas_call(kernel, out_shape=shapes, compiler_params=params, name=name)(*operands)

    shapes = [block(kept + refs, samples)] * segments
    if peers == 4:
        first = paired(records_owned, (1, 2))
        half = rows // 2
        whole = pl.BlockSpec(memory_space=pltpu.VMEM)
        own, send, keep, take = pl.pallas_call(
            choose_four_kernel,
            out_shape=[
                block(rows, samples),
                block(half + refs, 2 * rows, dtype=jnp.bfloat16),
                block(rows, 2 * rows, dtype=jnp.bfloat16),
                block(rows, half, dtype=jnp.bfloat16),
            ],
            in_specs=[pl.BlockSpec(memory_space=pl.ANY), whole, whole],
            scratch_shapes=[pltpu.VMEM(records_owned.shape, jnp.float32), pltpu.SemaphoreType.DMA],
            compiler_params=params,
            name="choose",
        )(pltpu.with_memory_space_constraint(records_owned, pltpu.HBM), lists, wanted)
        results = [block(half + refs, samples), block(rows, samples)]
        sent, base = call(pick_kernel, "pick", results, own, first, send, keep)
        placed = call(place_four_kernel, "place", shapes, base, take, sent, paired(sent, (2, 1)))
    else:
        packed, panel = call(
            pack_kernel,
            "pack",
            [block(rows, samples), block(refs, samples)],
            records_owned,
            lists,
            wanted,
        )
        blocks = packed.reshape(peers, share, samples)
        blocks = lax.all_to_all(blocks, "chan", split_axis=0, concat_axis=0, tiled=True)
        step = 1
        while step < peers:
            panel = panel + across(panel, step)
            step *= 2
        pick = call(
            functools.partial(choose_kernel, peers),
            "choose",
            block(rows, rows, dtype=jnp.bfloat16),
            lists,
        )
        placed = call(place_kernel, "place", shapes, pick, panel, blocks.reshape(rows, samples))
    held = {(0, 0): placed[0]}
    for lag_step in range(0, lags, 2):
        for segment_step in range(segments):
            if lag_step or segment_step:
                held[lag_step, segment_step] = swapped(placed[segment_step], lag_step, segment_step)
    for lag_step, segment_step in list(held):
        held[lag_step + 1, segment_step] = swapped(held[lag_step, segment_step], 1, 0)
    return pl.pallas_call(
        functools.partial(corr_kernel, refs, lag_width),
        out_shape=jax.ShapeDtypeStruct((kept, lag_width * refs), jnp.float32),
        scratch_shapes=[
            pltpu.VMEM((kept + refs, lags * segments * samples), jnp.float32),
            pltpu.VMEM((2 * lag_width // PHASES * kept, lags * segments * samples), jnp.bfloat16),
            pltpu.VMEM((2 * PHASES * refs, lags * segments * samples), jnp.bfloat16),
        ],
        compiler_params=params,
        name="correlate",
    )(*[held[step] for step in steps(lags, segments)])


def solution(mesh):
    return jax.shard_map(
        shards,
        mesh=mesh,
        in_specs=(P("chan", "seg", "lag"), P(), P()),
        out_specs=P(("chan", "seg"), "lag"),
        check_vma=False,
    )
```

```python
import functools
import math

import jax
import jax.numpy as jnp
from jax import lax
from jax.experimental import pallas as pl
from jax.experimental.pallas import tpu as pltpu
from jax.sharding import PartitionSpec as P

LAGS = 128
SAMPLES = 2048
PHASES = 8
PARTS = 2


def halves(value):
    high = value.astype(jnp.bfloat16)
    low = (value - high.astype(jnp.float32)).astype(jnp.bfloat16)
    return high, low


def product(left, right):
    return jnp.dot(left, right, preferred_element_type=jnp.float32)


def product_nt(left, right):
    return lax.dot_general(
        left, right, (((1,), (1,)), ((), ())), preferred_element_type=jnp.float32
    )


def steps(lags, segments):
    return [(lag, segment) for lag in range(lags) for segment in range(segments)]


def swapped(value, lag_step, segment_step):
    lags, segments = lax.axis_size("lag"), lax.axis_size("seg")
    pairs = [
        (lag * segments + segment, (lag ^ lag_step) * segments + (segment ^ segment_step))
        for lag, segment in steps(lags, segments)
    ]
    return lax.ppermute(value, ("lag", "seg"), pairs)


def across(value, step):
    return lax.ppermute(value, "chan", [(i, i ^ step) for i in range(lax.axis_size("chan"))])


def paired(value, order):
    lags = lax.axis_size("lag")
    pairs = [
        (chan * lags + lag, (chan ^ order[lag % 2]) * lags + lag)
        for chan in range(lax.axis_size("chan"))
        for lag in range(lags)
    ]
    return lax.ppermute(value, ("chan", "lag"), pairs)


def choice(pick, rows):
    high, low = halves(rows)
    return product(pick, high) + product(pick, low)


def counts_before(present):
    rows = present.shape[0]
    line = lax.broadcasted_iota(jnp.int32, (rows, rows), 0)
    lane = lax.broadcasted_iota(jnp.int32, (rows, rows), 1)
    return product((lane < line).astype(jnp.bfloat16), present.astype(jnp.bfloat16))


def columns(refs_ref, width):
    return jnp.broadcast_to(refs_ref[...], (width, refs_ref.shape[1])).T


def choose_four_kernel(
    records_ref,
    lists_ref,
    refs_ref,
    own_ref,
    send_ref,
    keep_ref,
    take_ref,
    held_ref,
    done,
):
    copy = pltpu.make_async_copy(records_ref, held_ref, done)
    copy.start()
    rows = lists_ref.shape[1]
    kept = take_ref.shape[1]
    refs = refs_ref.shape[1]
    me = lax.axis_index("chan")
    odd = lax.rem(lax.axis_index("lag"), 2)
    near, far = 1 + odd, 2 - odd
    line = lax.broadcasted_iota(jnp.int32, (rows, 2 * rows), 0)

    def pool(owner):
        lists = [lists_ref[pl.ds(lax.bitwise_xor(owner, i), 1), :] for i in (0, near)]
        return jnp.concatenate(lists, axis=1)

    def where(owner, block):
        return pool(owner) == line + block * rows

    def ranks(found):
        present = jnp.max(found.astype(jnp.float32), axis=1, keepdims=True)
        return present, counts_before(jnp.broadcast_to(present, (rows, rows)))

    other = lax.bitwise_xor(me, far)
    found = where(me, other)
    _, rank = ranks(found)
    rank = jnp.concatenate([rank, rank], axis=1)
    slot = jnp.sum(jnp.where(found, rank + 1.0, 0.0), axis=0, keepdims=True).astype(jnp.int32)
    send = jnp.concatenate([line[:kept] + 1 == slot, columns(refs_ref, 2 * rows) == pool(me)], axis=0)
    send = send.astype(jnp.bfloat16)
    keep = where(me, me).astype(jnp.bfloat16)
    send_ref[...] = send
    keep_ref[...] = keep
    present, rank = ranks(where(other, me))
    lane = lax.broadcasted_iota(jnp.int32, (rows, kept), 1)
    slot = jnp.where(present > 0.0, rank[:, :kept], -1.0).astype(jnp.int32)
    take_ref[...] = (lane == slot).astype(jnp.bfloat16)
    copy.wait()
    own_ref[...] = held_ref[:, 0, :]


def pick_kernel(own_ref, arrived_ref, send_ref, keep_ref, sent_ref, base_ref):
    rows = jnp.concatenate([own_ref[...], arrived_ref[:, 0, :]], axis=0)
    high, low = halves(rows)
    sent_ref[...] = product(send_ref[...], high) + product(send_ref[...], low)
    base_ref[...] = product(keep_ref[...], high) + product(keep_ref[...], low)


def put(series, panel, out_refs):
    segments = len(out_refs)
    kept = series.shape[0] // segments
    own = lax.axis_index("seg")
    for part in range(segments):
        half = lax.bitwise_xor(own, part)
        chosen = series[:kept]
        for other in range(1, segments):
            chosen = jnp.where(half == other, series[other * kept : (other + 1) * kept], chosen)
        out_refs[part][:kept, :] = chosen
        out_refs[part][kept:, :] = panel


def place_four_kernel(base_ref, take_ref, sent_ref, arrived_ref, *out_refs):
    kept = take_ref.shape[1]
    series = base_ref[...] + choice(take_ref[...], arrived_ref[:kept, :])
    put(series, sent_ref[kept:, :] + arrived_ref[kept:, :], out_refs)


def pack_kernel(records_ref, lists_ref, refs_ref, out_ref, panel_ref):
    rows = records_ref.shape[0]
    refs = refs_ref.shape[1]
    own = jnp.broadcast_to(lists_ref[pl.ds(lax.axis_index("chan"), 1), :], (rows, rows))
    rank = jnp.sum((own.T < own).astype(jnp.int32), axis=0, keepdims=True)
    line = lax.broadcasted_iota(jnp.int32, (rows, rows), 0)
    records = records_ref[:, 0, :]
    panel_ref[...] = choice((columns(refs_ref, rows) == own[:refs]).astype(jnp.bfloat16), records)
    out_ref[...] = choice((line == rank).astype(jnp.bfloat16), records)


def choose_kernel(peers, lists_ref, pick_ref):
    rows = lists_ref.shape[1]
    share = rows // peers
    lane = lax.broadcasted_iota(jnp.int32, (rows, rows), 1)
    channel = lax.broadcasted_iota(jnp.int32, (rows, rows), 0) + lax.axis_index("chan") * rows
    owner = jnp.zeros((rows, 1), jnp.int32)
    for peer in range(peers):
        found = (lists_ref[pl.ds(peer, 1), :] == channel).astype(jnp.int32)
        owner = owner + jnp.sum(found, axis=1, keepdims=True) * peer
    same = lane == owner
    before = counts_before(same.astype(jnp.float32))
    rank = jnp.sum(jnp.where(same, before, 0.0), axis=1, keepdims=True).astype(jnp.int32)
    pick_ref[...] = (lane == owner * share + rank).astype(jnp.bfloat16)


def place_kernel(pick_ref, panel_ref, arrived_ref, *out_refs):
    put(choice(pick_ref[...], arrived_ref[...]), panel_ref[...], out_refs)


def corr_kernel(refs, lag_width, *rest):
    *chunk_refs, out_ref, joined_ref, series_ref, panel_ref, total_ref, done = rest
    kept = total_ref.shape[0]
    lags, segments = lax.axis_size("lag"), lax.axis_size("seg")
    width = chunk_refs[0].shape[1]
    for (lag_step, segment_step), chunk_ref in zip(steps(lags, segments), chunk_refs):
        lag = lax.bitwise_xor(lax.axis_index("lag"), lag_step)
        segment = lax.bitwise_xor(lax.axis_index("seg"), segment_step)
        start = pl.multiple_of((segment * lags + lag) * width, width)
        joined_ref[:, pl.ds(start, width)] = chunk_ref[...]
    series = joined_ref[:kept, :]
    panel = joined_ref[kept:, :]
    samples = panel.shape[1]
    terms = SAMPLES - LAGS
    times = lax.broadcasted_iota(jnp.int32, panel.shape, 1)
    panel = jnp.where(times < terms, panel, 0.0)
    series = pltpu.roll(series, samples - lax.axis_index("lag") * lag_width, 1)
    groups = lag_width // PHASES

    def spread(value, shifts, out_ref, base):
        lines = value.shape[0]
        for half in halves(value):
            for shift in shifts:
                out_ref[base : base + lines, :] = (
                    pltpu.roll(half, shift % samples, 1) if shift else half
                )
                base += lines

    spread(series, range(0, -lag_width, -PHASES), series_ref, 0)
    lines, each = groups * kept, PHASES // PARTS
    columns = each * refs
    copies = []
    for part in range(PARTS):
        base = part * 2 * columns
        spread(panel, range(part * each, (part + 1) * each), panel_ref, base)
        upper = product_nt(series_ref[...], panel_ref[base : base + columns, :])
        lower = product_nt(series_ref[:lines, :], panel_ref[base + columns : base + 2 * columns, :])
        total = (upper[:lines] + upper[lines:] + lower) * (1.0 / math.sqrt(terms))
        for group in range(groups):
            start = (group * PARTS + part) * columns
            place = slice(start, start + columns)
            total_ref[:, place] = total[group * kept : (group + 1) * kept]
            copy = pltpu.make_async_copy(
                total_ref.at[:, place], out_ref.at[:, place], done.at[part * groups + group]
            )
            copy.start()
            copies.append(copy)
    for copy in copies:
        copy.wait()


def shards(records_owned, section_list, ref_index):
    peers = lax.axis_size("chan")
    segments = lax.axis_size("seg")
    rows, _, samples = records_owned.shape
    refs = ref_index.shape[0]
    share = rows // peers
    kept = rows // segments
    lags = lax.axis_size("lag")
    lag_width = LAGS // lags
    lists = section_list.reshape(peers, rows)
    params = pltpu.CompilerParams(vmem_limit_bytes=48 * 1024 * 1024)
    wanted = ref_index.reshape(1, refs)

    def block(*shape, dtype=jnp.float32):
        return jax.ShapeDtypeStruct(shape, dtype)

    def call(kernel, name, shapes, *operands):
        return pl.pallas_call(kernel, out_shape=shapes, compiler_params=params, name=name)(*operands)

    shapes = [block(kept + refs, samples)] * segments
    if peers == 4:
        first = paired(records_owned, (1, 2))
        half = rows // 2
        whole = pl.BlockSpec(memory_space=pltpu.VMEM)
        own, send, keep, take = pl.pallas_call(
            choose_four_kernel,
            out_shape=[
                block(rows, samples),
                block(half + refs, 2 * rows, dtype=jnp.bfloat16),
                block(rows, 2 * rows, dtype=jnp.bfloat16),
                block(rows, half, dtype=jnp.bfloat16),
            ],
            in_specs=[pl.BlockSpec(memory_space=pl.ANY), whole, whole],
            scratch_shapes=[pltpu.VMEM(records_owned.shape, jnp.float32), pltpu.SemaphoreType.DMA],
            compiler_params=params,
            name="choose",
        )(pltpu.with_memory_space_constraint(records_owned, pltpu.HBM), lists, wanted)
        results = [block(half + refs, samples), block(rows, samples)]
        sent, base = call(pick_kernel, "pick", results, own, first, send, keep)
        placed = call(place_four_kernel, "place", shapes, base, take, sent, paired(sent, (2, 1)))
    else:
        packed, panel = call(
            pack_kernel,
            "pack",
            [block(rows, samples), block(refs, samples)],
            records_owned,
            lists,
            wanted,
        )
        blocks = packed.reshape(peers, share, samples)
        blocks = lax.all_to_all(blocks, "chan", split_axis=0, concat_axis=0, tiled=True)
        step = 1
        while step < peers:
            panel = panel + across(panel, step)
            step *= 2
        pick = call(
            functools.partial(choose_kernel, peers),
            "choose",
            block(rows, rows, dtype=jnp.bfloat16),
            lists,
        )
        placed = call(place_kernel, "place", shapes, pick, panel, blocks.reshape(rows, samples))
    held = {(0, 0): placed[0]}
    for lag_step in range(0, lags, 2):
        for segment_step in range(segments):
            if lag_step or segment_step:
                held[lag_step, segment_step] = swapped(placed[segment_step], lag_step, segment_step)
    for lag_step, segment_step in list(held):
        held[lag_step + 1, segment_step] = swapped(held[lag_step, segment_step], 1, 0)
    return pl.pallas_call(
        functools.partial(corr_kernel, refs, lag_width),
        out_shape=jax.ShapeDtypeStruct((kept, lag_width * refs), jnp.float32),
        out_specs=pl.BlockSpec(memory_space=pl.ANY),
        scratch_shapes=[
            pltpu.VMEM((kept + refs, lags * segments * samples), jnp.float32),
            pltpu.VMEM((2 * lag_width // PHASES * kept, lags * segments * samples), jnp.bfloat16),
            pltpu.VMEM((2 * PHASES * refs, lags * segments * samples), jnp.bfloat16),
            pltpu.VMEM((kept, lag_width * refs), jnp.float32),
            pltpu.SemaphoreType.DMA((lag_width // PHASES * PARTS,)),
        ],
        compiler_params=params,
        name="correlate",
    )(*[held[step] for step in steps(lags, segments)])


def solution(mesh):
    return jax.shard_map(
        shards,
        mesh=mesh,
        in_specs=(P("chan", "seg", "lag"), P(), P()),
        out_specs=P(("chan", "seg"), "lag"),
        check_vma=False,
    )
```

```python
import functools
import math

import jax
import jax.numpy as jnp
from jax import lax
from jax.experimental import pallas as pl
from jax.experimental.pallas import tpu as pltpu
from jax.sharding import PartitionSpec as P

LAGS = 128
SAMPLES = 2048
PHASES = 16


def halves(value):
    high = value.astype(jnp.bfloat16)
    low = (value - high.astype(jnp.float32)).astype(jnp.bfloat16)
    return high, low


def product(left, right):
    return jnp.dot(left, right, preferred_element_type=jnp.float32)


def product_nt(left, right):
    return lax.dot_general(
        left, right, (((1,), (1,)), ((), ())), preferred_element_type=jnp.float32
    )


def steps(lags, segments):
    return [(lag, segment) for lag in range(lags) for segment in range(segments)]


def swapped(value, lag_step, segment_step):
    lags, segments = lax.axis_size("lag"), lax.axis_size("seg")
    pairs = [
        (lag * segments + segment, (lag ^ lag_step) * segments + (segment ^ segment_step))
        for lag, segment in steps(lags, segments)
    ]
    return lax.ppermute(value, ("lag", "seg"), pairs)


def across(value, step):
    return lax.ppermute(value, "chan", [(i, i ^ step) for i in range(lax.axis_size("chan"))])


def paired(value, order):
    lags = lax.axis_size("lag")
    pairs = [
        (chan * lags + lag, (chan ^ order[lag % 2]) * lags + lag)
        for chan in range(lax.axis_size("chan"))
        for lag in range(lags)
    ]
    return lax.ppermute(value, ("chan", "lag"), pairs)


def choice(pick, rows):
    high, low = halves(rows)
    return product(pick, high) + product(pick, low)


def counts_before(present):
    rows = present.shape[0]
    line = lax.broadcasted_iota(jnp.int32, (rows, rows), 0)
    lane = lax.broadcasted_iota(jnp.int32, (rows, rows), 1)
    return product((lane < line).astype(jnp.bfloat16), present.astype(jnp.bfloat16))


def columns(refs_ref, width):
    return jnp.broadcast_to(refs_ref[...], (width, refs_ref.shape[1])).T


def choose_four_kernel(
    records_ref,
    lists_ref,
    refs_ref,
    own_ref,
    send_ref,
    keep_ref,
    take_ref,
    held_ref,
    done,
):
    copy = pltpu.make_async_copy(records_ref, held_ref, done)
    copy.start()
    rows = lists_ref.shape[1]
    kept = take_ref.shape[1]
    refs = refs_ref.shape[1]
    me = lax.axis_index("chan")
    odd = lax.rem(lax.axis_index("lag"), 2)
    near, far = 1 + odd, 2 - odd
    line = lax.broadcasted_iota(jnp.int32, (rows, 2 * rows), 0)

    def pool(owner):
        lists = [lists_ref[pl.ds(lax.bitwise_xor(owner, i), 1), :] for i in (0, near)]
        return jnp.concatenate(lists, axis=1)

    def where(owner, block):
        return pool(owner) == line + block * rows

    def ranks(found):
        present = jnp.max(found.astype(jnp.float32), axis=1, keepdims=True)
        return present, counts_before(jnp.broadcast_to(present, (rows, rows)))

    other = lax.bitwise_xor(me, far)
    found = where(me, other)
    _, rank = ranks(found)
    rank = jnp.concatenate([rank, rank], axis=1)
    slot = jnp.sum(jnp.where(found, rank + 1.0, 0.0), axis=0, keepdims=True).astype(jnp.int32)
    send = jnp.concatenate([line[:kept] + 1 == slot, columns(refs_ref, 2 * rows) == pool(me)], axis=0)
    send = send.astype(jnp.bfloat16)
    keep = where(me, me).astype(jnp.bfloat16)
    send_ref[...] = send
    keep_ref[...] = keep
    present, rank = ranks(where(other, me))
    lane = lax.broadcasted_iota(jnp.int32, (rows, kept), 1)
    slot = jnp.where(present > 0.0, rank[:, :kept], -1.0).astype(jnp.int32)
    take_ref[...] = (lane == slot).astype(jnp.bfloat16)
    copy.wait()
    own_ref[...] = held_ref[:, 0, :]


def pick_kernel(own_ref, arrived_ref, send_ref, keep_ref, sent_ref, base_ref):
    rows = jnp.concatenate([own_ref[...], arrived_ref[:, 0, :]], axis=0)
    high, low = halves(rows)
    sent_ref[...] = product(send_ref[...], high) + product(send_ref[...], low)
    base_ref[...] = product(keep_ref[...], high) + product(keep_ref[...], low)


def put(series, panel, out_refs):
    segments = len(out_refs)
    kept = series.shape[0] // segments
    own = lax.axis_index("seg")
    for part in range(segments):
        half = lax.bitwise_xor(own, part)
        chosen = series[:kept]
        for other in range(1, segments):
            chosen = jnp.where(half == other, series[other * kept : (other + 1) * kept], chosen)
        out_refs[part][:kept, :] = chosen
        out_refs[part][kept:, :] = panel


def place_four_kernel(base_ref, take_ref, sent_ref, arrived_ref, *out_refs):
    kept = take_ref.shape[1]
    series = base_ref[...] + choice(take_ref[...], arrived_ref[:kept, :])
    put(series, sent_ref[kept:, :] + arrived_ref[kept:, :], out_refs)


def pack_kernel(records_ref, lists_ref, refs_ref, out_ref, panel_ref):
    rows = records_ref.shape[0]
    refs = refs_ref.shape[1]
    own = jnp.broadcast_to(lists_ref[pl.ds(lax.axis_index("chan"), 1), :], (rows, rows))
    rank = jnp.sum((own.T < own).astype(jnp.int32), axis=0, keepdims=True)
    line = lax.broadcasted_iota(jnp.int32, (rows, rows), 0)
    records = records_ref[:, 0, :]
    panel_ref[...] = choice((columns(refs_ref, rows) == own[:refs]).astype(jnp.bfloat16), records)
    out_ref[...] = choice((line == rank).astype(jnp.bfloat16), records)


def choose_kernel(peers, lists_ref, pick_ref):
    rows = lists_ref.shape[1]
    share = rows // peers
    lane = lax.broadcasted_iota(jnp.int32, (rows, rows), 1)
    channel = lax.broadcasted_iota(jnp.int32, (rows, rows), 0) + lax.axis_index("chan") * rows
    owner = jnp.zeros((rows, 1), jnp.int32)
    for peer in range(peers):
        found = (lists_ref[pl.ds(peer, 1), :] == channel).astype(jnp.int32)
        owner = owner + jnp.sum(found, axis=1, keepdims=True) * peer
    same = lane == owner
    before = counts_before(same.astype(jnp.float32))
    rank = jnp.sum(jnp.where(same, before, 0.0), axis=1, keepdims=True).astype(jnp.int32)
    pick_ref[...] = (lane == owner * share + rank).astype(jnp.bfloat16)


def place_kernel(pick_ref, panel_ref, arrived_ref, *out_refs):
    put(choice(pick_ref[...], arrived_ref[...]), panel_ref[...], out_refs)


def corr_kernel(refs, lag_width, *rest):
    *chunk_refs, out_ref, joined_ref, series_ref, panel_ref = rest
    kept = out_ref.shape[0]
    lags, segments = lax.axis_size("lag"), lax.axis_size("seg")
    width = chunk_refs[0].shape[1]
    for (lag_step, segment_step), chunk_ref in zip(steps(lags, segments), chunk_refs):
        lag = lax.bitwise_xor(lax.axis_index("lag"), lag_step)
        segment = lax.bitwise_xor(lax.axis_index("seg"), segment_step)
        start = pl.multiple_of((segment * lags + lag) * width, width)
        joined_ref[:, pl.ds(start, width)] = chunk_ref[...]
    series = joined_ref[:kept, :]
    panel = joined_ref[kept:, :]
    samples = panel.shape[1]
    terms = SAMPLES - LAGS
    times = lax.broadcasted_iota(jnp.int32, panel.shape, 1)
    panel = jnp.where(times < terms, panel, 0.0)
    series = pltpu.roll(series, samples - lax.axis_index("lag") * lag_width, 1)
    groups = lag_width // PHASES

    def spread(value, count, step, out_ref):
        lines = value.shape[0]
        for half, part in enumerate(halves(value)):
            for i in range(count):
                start = (half * count + i) * lines
                out_ref[start : start + lines, :] = (
                    pltpu.roll(part, (i * step) % samples, 1) if i else part
                )

    spread(panel, PHASES, 1, panel_ref)
    spread(series, groups, -PHASES, series_ref)
    lines, columns = groups * kept, PHASES * refs
    upper = product_nt(series_ref[...], panel_ref[:columns, :])
    lower = product_nt(series_ref[:lines, :], panel_ref[columns:, :])
    total = (upper[:lines] + upper[lines:] + lower) * (1.0 / math.sqrt(terms))
    for group in range(groups):
        out_ref[:, group * columns : (group + 1) * columns] = total[
            group * kept : (group + 1) * kept
        ]


def shards(records_owned, section_list, ref_index):
    peers = lax.axis_size("chan")
    segments = lax.axis_size("seg")
    rows, _, samples = records_owned.shape
    refs = ref_index.shape[0]
    share = rows // peers
    kept = rows // segments
    lags = lax.axis_size("lag")
    lag_width = LAGS // lags
    lists = section_list.reshape(peers, rows)
    params = pltpu.CompilerParams(vmem_limit_bytes=48 * 1024 * 1024)
    wanted = ref_index.reshape(1, refs)

    def block(*shape, dtype=jnp.float32):
        return jax.ShapeDtypeStruct(shape, dtype)

    def call(kernel, name, shapes, *operands):
        return pl.pallas_call(kernel, out_shape=shapes, compiler_params=params, name=name)(*operands)

    shapes = [block(kept + refs, samples)] * segments
    if peers == 4:
        first = paired(records_owned, (1, 2))
        half = rows // 2
        whole = pl.BlockSpec(memory_space=pltpu.VMEM)
        own, send, keep, take = pl.pallas_call(
            choose_four_kernel,
            out_shape=[
                block(rows, samples),
                block(half + refs, 2 * rows, dtype=jnp.bfloat16),
                block(rows, 2 * rows, dtype=jnp.bfloat16),
                block(rows, half, dtype=jnp.bfloat16),
            ],
            in_specs=[pl.BlockSpec(memory_space=pl.ANY), whole, whole],
            scratch_shapes=[pltpu.VMEM(records_owned.shape, jnp.float32), pltpu.SemaphoreType.DMA],
            compiler_params=params,
            name="choose",
        )(pltpu.with_memory_space_constraint(records_owned, pltpu.HBM), lists, wanted)
        results = [block(half + refs, samples), block(rows, samples)]
        sent, base = call(pick_kernel, "pick", results, own, first, send, keep)
        placed = call(place_four_kernel, "place", shapes, base, take, sent, paired(sent, (2, 1)))
    else:
        packed, panel = call(
            pack_kernel,
            "pack",
            [block(rows, samples), block(refs, samples)],
            records_owned,
            lists,
            wanted,
        )
        blocks = packed.reshape(peers, share, samples)
        blocks = lax.all_to_all(blocks, "chan", split_axis=0, concat_axis=0, tiled=True)
        step = 1
        while step < peers:
            panel = panel + across(panel, step)
            step *= 2
        pick = call(
            functools.partial(choose_kernel, peers),
            "choose",
            block(rows, rows, dtype=jnp.bfloat16),
            lists,
        )
        placed = call(place_kernel, "place", shapes, pick, panel, blocks.reshape(rows, samples))
    held = {(0, 0): placed[0]}
    for lag_step in range(0, lags, 2):
        for segment_step in range(segments):
            if lag_step or segment_step:
                held[lag_step, segment_step] = swapped(placed[segment_step], lag_step, segment_step)
    for lag_step, segment_step in list(held):
        held[lag_step + 1, segment_step] = swapped(held[lag_step, segment_step], 1, 0)
    return pl.pallas_call(
        functools.partial(corr_kernel, refs, lag_width),
        out_shape=jax.ShapeDtypeStruct((kept, lag_width * refs), jnp.float32),
        scratch_shapes=[
            pltpu.VMEM((kept + refs, lags * segments * samples), jnp.float32),
            pltpu.VMEM((2 * lag_width // PHASES * kept, lags * segments * samples), jnp.bfloat16),
            pltpu.VMEM((2 * PHASES * refs, lags * segments * samples), jnp.bfloat16),
        ],
        compiler_params=params,
        name="correlate",
    )(*[held[step] for step in steps(lags, segments)])


def solution(mesh):
    return jax.shard_map(
        shards,
        mesh=mesh,
        in_specs=(P("chan", "seg", "lag"), P(), P()),
        out_specs=P(("chan", "seg"), "lag"),
        check_vma=False,
    )
```

```python
import functools
import math

import jax
import jax.numpy as jnp
from jax import lax
from jax.experimental import pallas as pl
from jax.experimental.pallas import tpu as pltpu
from jax.sharding import PartitionSpec as P

LAGS = 128
SAMPLES = 2048
PHASES = 8


def halves(value):
    high = value.astype(jnp.bfloat16)
    low = (value - high.astype(jnp.float32)).astype(jnp.bfloat16)
    return high, low


def product(left, right):
    return jnp.dot(left, right, preferred_element_type=jnp.float32)


def product_nt(left, right):
    return lax.dot_general(
        left, right, (((1,), (1,)), ((), ())), preferred_element_type=jnp.float32
    )


def steps(lags, segments):
    return [(lag, segment) for lag in range(lags) for segment in range(segments)]


def swapped(value, lag_step, segment_step):
    lags, segments = lax.axis_size("lag"), lax.axis_size("seg")
    pairs = [
        (lag * segments + segment, (lag ^ lag_step) * segments + (segment ^ segment_step))
        for lag, segment in steps(lags, segments)
    ]
    return lax.ppermute(value, ("lag", "seg"), pairs)


def across(value, step):
    return lax.ppermute(value, "chan", [(i, i ^ step) for i in range(lax.axis_size("chan"))])


def paired(value, order):
    lags = lax.axis_size("lag")
    pairs = [
        (chan * lags + lag, (chan ^ order[lag % 2]) * lags + lag)
        for chan in range(lax.axis_size("chan"))
        for lag in range(lags)
    ]
    return lax.ppermute(value, ("chan", "lag"), pairs)


def choice(pick, rows):
    high, low = halves(rows)
    return product(pick, high) + product(pick, low)


def counts_before(present):
    rows = present.shape[0]
    line = lax.broadcasted_iota(jnp.int32, (rows, rows), 0)
    lane = lax.broadcasted_iota(jnp.int32, (rows, rows), 1)
    return product((lane < line).astype(jnp.bfloat16), present.astype(jnp.bfloat16))


def columns(refs_ref, width):
    return jnp.broadcast_to(refs_ref[...], (width, refs_ref.shape[1])).T


def choose_four_kernel(
    records_ref,
    lists_ref,
    refs_ref,
    own_ref,
    send_ref,
    keep_ref,
    take_ref,
    held_ref,
    done,
):
    copy = pltpu.make_async_copy(records_ref, held_ref, done)
    copy.start()
    rows = lists_ref.shape[1]
    kept = take_ref.shape[1]
    refs = refs_ref.shape[1]
    me = lax.axis_index("chan")
    odd = lax.rem(lax.axis_index("lag"), 2)
    near, far = 2 - odd, 1 + odd
    line = lax.broadcasted_iota(jnp.int32, (rows, 2 * rows), 0)

    def pool(owner):
        lists = [lists_ref[pl.ds(lax.bitwise_xor(owner, i), 1), :] for i in (0, near)]
        return jnp.concatenate(lists, axis=1)

    def where(owner, block):
        return pool(owner) == line + block * rows

    def ranks(found):
        present = jnp.max(found.astype(jnp.float32), axis=1, keepdims=True)
        return present, counts_before(jnp.broadcast_to(present, (rows, rows)))

    other = lax.bitwise_xor(me, far)
    found = where(me, other)
    _, rank = ranks(found)
    rank = jnp.concatenate([rank, rank], axis=1)
    slot = jnp.sum(jnp.where(found, rank + 1.0, 0.0), axis=0, keepdims=True).astype(jnp.int32)
    send = jnp.concatenate([line[:kept] + 1 == slot, columns(refs_ref, 2 * rows) == pool(me)], axis=0)
    send = send.astype(jnp.bfloat16)
    keep = where(me, me).astype(jnp.bfloat16)
    send_ref[...] = send
    keep_ref[...] = keep
    present, rank = ranks(where(other, me))
    lane = lax.broadcasted_iota(jnp.int32, (rows, kept), 1)
    slot = jnp.where(present > 0.0, rank[:, :kept], -1.0).astype(jnp.int32)
    take_ref[...] = (lane == slot).astype(jnp.bfloat16)
    copy.wait()
    own_ref[...] = held_ref[:, 0, :]


def pick_kernel(own_ref, arrived_ref, send_ref, keep_ref, sent_ref, base_ref):
    rows = jnp.concatenate([own_ref[...], arrived_ref[:, 0, :]], axis=0)
    high, low = halves(rows)
    sent_ref[...] = product(send_ref[...], high) + product(send_ref[...], low)
    base_ref[...] = product(keep_ref[...], high) + product(keep_ref[...], low)


def put(series, panel, out_refs):
    segments = len(out_refs)
    kept = series.shape[0] // segments
    own = lax.axis_index("seg")
    for part in range(segments):
        half = lax.bitwise_xor(own, part)
        chosen = series[:kept]
        for other in range(1, segments):
            chosen = jnp.where(half == other, series[other * kept : (other + 1) * kept], chosen)
        out_refs[part][:kept, :] = chosen
        out_refs[part][kept:, :] = panel


def place_four_kernel(base_ref, take_ref, sent_ref, arrived_ref, *out_refs):
    kept = take_ref.shape[1]
    series = base_ref[...] + choice(take_ref[...], arrived_ref[:kept, :])
    put(series, sent_ref[kept:, :] + arrived_ref[kept:, :], out_refs)


def pack_kernel(records_ref, lists_ref, refs_ref, out_ref, panel_ref):
    rows = records_ref.shape[0]
    refs = refs_ref.shape[1]
    own = jnp.broadcast_to(lists_ref[pl.ds(lax.axis_index("chan"), 1), :], (rows, rows))
    rank = jnp.sum((own.T < own).astype(jnp.int32), axis=0, keepdims=True)
    line = lax.broadcasted_iota(jnp.int32, (rows, rows), 0)
    records = records_ref[:, 0, :]
    panel_ref[...] = choice((columns(refs_ref, rows) == own[:refs]).astype(jnp.bfloat16), records)
    out_ref[...] = choice((line == rank).astype(jnp.bfloat16), records)


def choose_kernel(peers, lists_ref, pick_ref):
    rows = lists_ref.shape[1]
    share = rows // peers
    lane = lax.broadcasted_iota(jnp.int32, (rows, rows), 1)
    channel = lax.broadcasted_iota(jnp.int32, (rows, rows), 0) + lax.axis_index("chan") * rows
    owner = jnp.zeros((rows, 1), jnp.int32)
    for peer in range(peers):
        found = (lists_ref[pl.ds(peer, 1), :] == channel).astype(jnp.int32)
        owner = owner + jnp.sum(found, axis=1, keepdims=True) * peer
    same = lane == owner
    before = counts_before(same.astype(jnp.float32))
    rank = jnp.sum(jnp.where(same, before, 0.0), axis=1, keepdims=True).astype(jnp.int32)
    pick_ref[...] = (lane == owner * share + rank).astype(jnp.bfloat16)


def place_kernel(pick_ref, panel_ref, arrived_ref, *out_refs):
    put(choice(pick_ref[...], arrived_ref[...]), panel_ref[...], out_refs)


def corr_kernel(refs, lag_width, *rest):
    *chunk_refs, out_ref, joined_ref, series_ref, panel_ref = rest
    kept = out_ref.shape[0]
    lags, segments = lax.axis_size("lag"), lax.axis_size("seg")
    width = chunk_refs[0].shape[1]
    for (lag_step, segment_step), chunk_ref in zip(steps(lags, segments), chunk_refs):
        lag = lax.bitwise_xor(lax.axis_index("lag"), lag_step)
        segment = lax.bitwise_xor(lax.axis_index("seg"), segment_step)
        start = pl.multiple_of((segment * lags + lag) * width, width)
        joined_ref[:, pl.ds(start, width)] = chunk_ref[...]
    series = joined_ref[:kept, :]
    panel = joined_ref[kept:, :]
    samples = panel.shape[1]
    terms = SAMPLES - LAGS
    times = lax.broadcasted_iota(jnp.int32, panel.shape, 1)
    panel = jnp.where(times < terms, panel, 0.0)
    series = pltpu.roll(series, samples - lax.axis_index("lag") * lag_width, 1)
    groups = lag_width // PHASES

    def spread(value, count, step, out_ref):
        lines = value.shape[0]
        for half, part in enumerate(halves(value)):
            for i in range(count):
                start = (half * count + i) * lines
                out_ref[start : start + lines, :] = (
                    pltpu.roll(part, (i * step) % samples, 1) if i else part
                )

    spread(panel, PHASES, 1, panel_ref)
    spread(series, groups, -PHASES, series_ref)
    lines, columns = groups * kept, PHASES * refs
    upper = product_nt(series_ref[...], panel_ref[:columns, :])
    lower = product_nt(series_ref[:lines, :], panel_ref[columns:, :])
    total = (upper[:lines] + upper[lines:] + lower) * (1.0 / math.sqrt(terms))
    for group in range(groups):
        out_ref[:, group * columns : (group + 1) * columns] = total[
            group * kept : (group + 1) * kept
        ]


def shards(records_owned, section_list, ref_index):
    peers = lax.axis_size("chan")
    segments = lax.axis_size("seg")
    rows, _, samples = records_owned.shape
    refs = ref_index.shape[0]
    share = rows // peers
    kept = rows // segments
    lags = lax.axis_size("lag")
    lag_width = LAGS // lags
    lists = section_list.reshape(peers, rows)
    params = pltpu.CompilerParams(vmem_limit_bytes=48 * 1024 * 1024)
    wanted = ref_index.reshape(1, refs)

    def block(*shape, dtype=jnp.float32):
        return jax.ShapeDtypeStruct(shape, dtype)

    def call(kernel, name, shapes, *operands):
        return pl.pallas_call(kernel, out_shape=shapes, compiler_params=params, name=name)(*operands)

    shapes = [block(kept + refs, samples)] * segments
    if peers == 4:
        first = paired(records_owned, (2, 1))
        half = rows // 2
        whole = pl.BlockSpec(memory_space=pltpu.VMEM)
        own, send, keep, take = pl.pallas_call(
            choose_four_kernel,
            out_shape=[
                block(rows, samples),
                block(half + refs, 2 * rows, dtype=jnp.bfloat16),
                block(rows, 2 * rows, dtype=jnp.bfloat16),
                block(rows, half, dtype=jnp.bfloat16),
            ],
            in_specs=[pl.BlockSpec(memory_space=pl.ANY), whole, whole],
            scratch_shapes=[pltpu.VMEM(records_owned.shape, jnp.float32), pltpu.SemaphoreType.DMA],
            compiler_params=params,
            name="choose",
        )(pltpu.with_memory_space_constraint(records_owned, pltpu.HBM), lists, wanted)
        results = [block(half + refs, samples), block(rows, samples)]
        sent, base = call(pick_kernel, "pick", results, own, first, send, keep)
        placed = call(place_four_kernel, "place", shapes, base, take, sent, paired(sent, (1, 2)))
    else:
        packed, panel = call(
            pack_kernel,
            "pack",
            [block(rows, samples), block(refs, samples)],
            records_owned,
            lists,
            wanted,
        )
        blocks = packed.reshape(peers, share, samples)
        blocks = lax.all_to_all(blocks, "chan", split_axis=0, concat_axis=0, tiled=True)
        step = 1
        while step < peers:
            panel = panel + across(panel, step)
            step *= 2
        pick = call(
            functools.partial(choose_kernel, peers),
            "choose",
            block(rows, rows, dtype=jnp.bfloat16),
            lists,
        )
        placed = call(place_kernel, "place", shapes, pick, panel, blocks.reshape(rows, samples))
    held = {(0, 0): placed[0]}
    for lag_step in range(0, lags, 2):
        for segment_step in range(segments):
            if lag_step or segment_step:
                held[lag_step, segment_step] = swapped(placed[segment_step], lag_step, segment_step)
    for lag_step, segment_step in list(held):
        held[lag_step + 1, segment_step] = swapped(held[lag_step, segment_step], 1, 0)
    return pl.pallas_call(
        functools.partial(corr_kernel, refs, lag_width),
        out_shape=jax.ShapeDtypeStruct((kept, lag_width * refs), jnp.float32),
        scratch_shapes=[
            pltpu.VMEM((kept + refs, lags * segments * samples), jnp.float32),
            pltpu.VMEM((2 * lag_width // PHASES * kept, lags * segments * samples), jnp.bfloat16),
            pltpu.VMEM((2 * PHASES * refs, lags * segments * samples), jnp.bfloat16),
        ],
        compiler_params=params,
        name="correlate",
    )(*[held[step] for step in steps(lags, segments)])


def solution(mesh):
    return jax.shard_map(
        shards,
        mesh=mesh,
        in_specs=(P("chan", "seg", "lag"), P(), P()),
        out_specs=P(("chan", "seg"), "lag"),
        check_vma=False,
    )
```

```python
import functools
import math

import jax
import jax.numpy as jnp
from jax import lax
from jax.experimental import pallas as pl
from jax.experimental.pallas import tpu as pltpu
from jax.sharding import PartitionSpec as P

LAGS = 128
SAMPLES = 2048
PHASES = 8
PARTS = 2


def halves(value):
    high = value.astype(jnp.bfloat16)
    low = (value - high.astype(jnp.float32)).astype(jnp.bfloat16)
    return high, low


def product(left, right):
    return jnp.dot(left, right, preferred_element_type=jnp.float32)


def product_nt(left, right):
    return lax.dot_general(
        left, right, (((1,), (1,)), ((), ())), preferred_element_type=jnp.float32
    )


def steps(lags, segments):
    return [(lag, segment) for lag in range(lags) for segment in range(segments)]


def swapped(value, lag_step, segment_step):
    lags, segments = lax.axis_size("lag"), lax.axis_size("seg")
    pairs = [
        (lag * segments + segment, (lag ^ lag_step) * segments + (segment ^ segment_step))
        for lag, segment in steps(lags, segments)
    ]
    return lax.ppermute(value, ("lag", "seg"), pairs)


def across(value, step):
    return lax.ppermute(value, "chan", [(i, i ^ step) for i in range(lax.axis_size("chan"))])


def paired(value, order):
    lags = lax.axis_size("lag")
    pairs = [
        (chan * lags + lag, (chan ^ order[lag % 2]) * lags + lag)
        for chan in range(lax.axis_size("chan"))
        for lag in range(lags)
    ]
    return lax.ppermute(value, ("chan", "lag"), pairs)


def choice(pick, rows):
    high, low = halves(rows)
    return product(pick, high) + product(pick, low)


def counts_before(present):
    rows = present.shape[0]
    line = lax.broadcasted_iota(jnp.int32, (rows, rows), 0)
    lane = lax.broadcasted_iota(jnp.int32, (rows, rows), 1)
    return product((lane < line).astype(jnp.bfloat16), present.astype(jnp.bfloat16))


def columns(refs_ref, width):
    return jnp.broadcast_to(refs_ref[...], (width, refs_ref.shape[1])).T


def choose_four_kernel(
    records_ref,
    lists_ref,
    refs_ref,
    own_ref,
    send_ref,
    keep_ref,
    take_ref,
    held_ref,
    done,
):
    copy = pltpu.make_async_copy(records_ref, held_ref, done)
    copy.start()
    rows = lists_ref.shape[1]
    kept = take_ref.shape[1]
    refs = refs_ref.shape[1]
    me = lax.axis_index("chan")
    odd = lax.rem(lax.axis_index("lag"), 2)
    near, far = 2 - odd, 1 + odd
    line = lax.broadcasted_iota(jnp.int32, (rows, 2 * rows), 0)

    def pool(owner):
        lists = [lists_ref[pl.ds(lax.bitwise_xor(owner, i), 1), :] for i in (0, near)]
        return jnp.concatenate(lists, axis=1)

    def where(owner, block):
        return pool(owner) == line + block * rows

    def ranks(found):
        present = jnp.max(found.astype(jnp.float32), axis=1, keepdims=True)
        return present, counts_before(jnp.broadcast_to(present, (rows, rows)))

    other = lax.bitwise_xor(me, far)
    found = where(me, other)
    _, rank = ranks(found)
    rank = jnp.concatenate([rank, rank], axis=1)
    slot = jnp.sum(jnp.where(found, rank + 1.0, 0.0), axis=0, keepdims=True).astype(jnp.int32)
    send = jnp.concatenate([line[:kept] + 1 == slot, columns(refs_ref, 2 * rows) == pool(me)], axis=0)
    send = send.astype(jnp.bfloat16)
    keep = where(me, me).astype(jnp.bfloat16)
    send_ref[...] = send
    keep_ref[...] = keep
    present, rank = ranks(where(other, me))
    lane = lax.broadcasted_iota(jnp.int32, (rows, kept), 1)
    slot = jnp.where(present > 0.0, rank[:, :kept], -1.0).astype(jnp.int32)
    take_ref[...] = (lane == slot).astype(jnp.bfloat16)
    copy.wait()
    own_ref[...] = held_ref[:, 0, :]


def pick_kernel(own_ref, arrived_ref, send_ref, keep_ref, sent_ref, base_ref):
    rows = jnp.concatenate([own_ref[...], arrived_ref[:, 0, :]], axis=0)
    high, low = halves(rows)
    sent_ref[...] = product(send_ref[...], high) + product(send_ref[...], low)
    base_ref[...] = product(keep_ref[...], high) + product(keep_ref[...], low)


def put(series, panel, out_refs):
    segments = len(out_refs)
    kept = series.shape[0] // segments
    own = lax.axis_index("seg")
    for part in range(segments):
        half = lax.bitwise_xor(own, part)
        chosen = series[:kept]
        for other in range(1, segments):
            chosen = jnp.where(half == other, series[other * kept : (other + 1) * kept], chosen)
        out_refs[part][:kept, :] = chosen
        out_refs[part][kept:, :] = panel


def place_four_kernel(base_ref, take_ref, sent_ref, arrived_ref, *out_refs):
    kept = take_ref.shape[1]
    series = base_ref[...] + choice(take_ref[...], arrived_ref[:kept, :])
    put(series, sent_ref[kept:, :] + arrived_ref[kept:, :], out_refs)


def pack_kernel(records_ref, lists_ref, refs_ref, out_ref, panel_ref):
    rows = records_ref.shape[0]
    refs = refs_ref.shape[1]
    own = jnp.broadcast_to(lists_ref[pl.ds(lax.axis_index("chan"), 1), :], (rows, rows))
    rank = jnp.sum((own.T < own).astype(jnp.int32), axis=0, keepdims=True)
    line = lax.broadcasted_iota(jnp.int32, (rows, rows), 0)
    records = records_ref[:, 0, :]
    panel_ref[...] = choice((columns(refs_ref, rows) == own[:refs]).astype(jnp.bfloat16), records)
    out_ref[...] = choice((line == rank).astype(jnp.bfloat16), records)


def choose_kernel(peers, lists_ref, pick_ref):
    rows = lists_ref.shape[1]
    share = rows // peers
    lane = lax.broadcasted_iota(jnp.int32, (rows, rows), 1)
    channel = lax.broadcasted_iota(jnp.int32, (rows, rows), 0) + lax.axis_index("chan") * rows
    owner = jnp.zeros((rows, 1), jnp.int32)
    for peer in range(peers):
        found = (lists_ref[pl.ds(peer, 1), :] == channel).astype(jnp.int32)
        owner = owner + jnp.sum(found, axis=1, keepdims=True) * peer
    same = lane == owner
    before = counts_before(same.astype(jnp.float32))
    rank = jnp.sum(jnp.where(same, before, 0.0), axis=1, keepdims=True).astype(jnp.int32)
    pick_ref[...] = (lane == owner * share + rank).astype(jnp.bfloat16)


def place_kernel(pick_ref, panel_ref, arrived_ref, *out_refs):
    put(choice(pick_ref[...], arrived_ref[...]), panel_ref[...], out_refs)


def corr_kernel(refs, lag_width, *rest):
    *chunk_refs, out_ref, joined_ref, series_ref, panel_ref, total_ref, done = rest
    kept = total_ref.shape[0]
    lags, segments = lax.axis_size("lag"), lax.axis_size("seg")
    width = chunk_refs[0].shape[1]
    for (lag_step, segment_step), chunk_ref in zip(steps(lags, segments), chunk_refs):
        lag = lax.bitwise_xor(lax.axis_index("lag"), lag_step)
        segment = lax.bitwise_xor(lax.axis_index("seg"), segment_step)
        start = pl.multiple_of((segment * lags + lag) * width, width)
        joined_ref[:, pl.ds(start, width)] = chunk_ref[...]
    series = joined_ref[:kept, :]
    panel = joined_ref[kept:, :]
    samples = panel.shape[1]
    terms = SAMPLES - LAGS
    times = lax.broadcasted_iota(jnp.int32, panel.shape, 1)
    panel = jnp.where(times < terms, panel, 0.0)
    series = pltpu.roll(series, samples - lax.axis_index("lag") * lag_width, 1)
    groups = lag_width // PHASES

    def spread(value, shifts, out_ref, base):
        lines = value.shape[0]
        for half in halves(value):
            for shift in shifts:
                out_ref[base : base + lines, :] = (
                    pltpu.roll(half, shift % samples, 1) if shift else half
                )
                base += lines

    spread(series, range(0, -lag_width, -PHASES), series_ref, 0)
    lines, each = groups * kept, PHASES // PARTS
    columns = each * refs
    copies = []
    for part in range(PARTS):
        base = part * 2 * columns
        spread(panel, range(part * each, (part + 1) * each), panel_ref, base)
        upper = product_nt(series_ref[...], panel_ref[base : base + columns, :])
        lower = product_nt(series_ref[:lines, :], panel_ref[base + columns : base + 2 * columns, :])
        total = (upper[:lines] + upper[lines:] + lower) * (1.0 / math.sqrt(terms))
        for group in range(groups):
            start = (group * PARTS + part) * columns
            place = slice(start, start + columns)
            total_ref[:, place] = total[group * kept : (group + 1) * kept]
            copy = pltpu.make_async_copy(
                total_ref.at[:, place], out_ref.at[:, place], done.at[part * groups + group]
            )
            copy.start()
            copies.append(copy)
    for copy in copies:
        copy.wait()


def shards(records_owned, section_list, ref_index):
    peers = lax.axis_size("chan")
    segments = lax.axis_size("seg")
    rows, _, samples = records_owned.shape
    refs = ref_index.shape[0]
    share = rows // peers
    kept = rows // segments
    lags = lax.axis_size("lag")
    lag_width = LAGS // lags
    lists = section_list.reshape(peers, rows)
    params = pltpu.CompilerParams(vmem_limit_bytes=48 * 1024 * 1024)
    wanted = ref_index.reshape(1, refs)

    def block(*shape, dtype=jnp.float32):
        return jax.ShapeDtypeStruct(shape, dtype)

    def call(kernel, name, shapes, *operands):
        return pl.pallas_call(kernel, out_shape=shapes, compiler_params=params, name=name)(*operands)

    shapes = [block(kept + refs, samples)] * segments
    if peers == 4:
        first = paired(records_owned, (2, 1))
        half = rows // 2
        whole = pl.BlockSpec(memory_space=pltpu.VMEM)
        own, send, keep, take = pl.pallas_call(
            choose_four_kernel,
            out_shape=[
                block(rows, samples),
                block(half + refs, 2 * rows, dtype=jnp.bfloat16),
                block(rows, 2 * rows, dtype=jnp.bfloat16),
                block(rows, half, dtype=jnp.bfloat16),
            ],
            in_specs=[pl.BlockSpec(memory_space=pl.ANY), whole, whole],
            scratch_shapes=[pltpu.VMEM(records_owned.shape, jnp.float32), pltpu.SemaphoreType.DMA],
            compiler_params=params,
            name="choose",
        )(pltpu.with_memory_space_constraint(records_owned, pltpu.HBM), lists, wanted)
        results = [block(half + refs, samples), block(rows, samples)]
        sent, base = call(pick_kernel, "pick", results, own, first, send, keep)
        placed = call(place_four_kernel, "place", shapes, base, take, sent, paired(sent, (1, 2)))
    else:
        packed, panel = call(
            pack_kernel,
            "pack",
            [block(rows, samples), block(refs, samples)],
            records_owned,
            lists,
            wanted,
        )
        blocks = packed.reshape(peers, share, samples)
        blocks = lax.all_to_all(blocks, "chan", split_axis=0, concat_axis=0, tiled=True)
        step = 1
        while step < peers:
            panel = panel + across(panel, step)
            step *= 2
        pick = call(
            functools.partial(choose_kernel, peers),
            "choose",
            block(rows, rows, dtype=jnp.bfloat16),
            lists,
        )
        placed = call(place_kernel, "place", shapes, pick, panel, blocks.reshape(rows, samples))
    held = {(0, 0): placed[0]}
    for lag_step in range(0, lags, 2):
        for segment_step in range(segments):
            if lag_step or segment_step:
                held[lag_step, segment_step] = swapped(placed[segment_step], lag_step, segment_step)
    for lag_step, segment_step in list(held):
        held[lag_step + 1, segment_step] = swapped(held[lag_step, segment_step], 1, 0)
    return pl.pallas_call(
        functools.partial(corr_kernel, refs, lag_width),
        out_shape=jax.ShapeDtypeStruct((kept, lag_width * refs), jnp.float32),
        out_specs=pl.BlockSpec(memory_space=pl.ANY),
        scratch_shapes=[
            pltpu.VMEM((kept + refs, lags * segments * samples), jnp.float32),
            pltpu.VMEM((2 * lag_width // PHASES * kept, lags * segments * samples), jnp.bfloat16),
            pltpu.VMEM((2 * PHASES * refs, lags * segments * samples), jnp.bfloat16),
            pltpu.VMEM((kept, lag_width * refs), jnp.float32),
            pltpu.SemaphoreType.DMA((lag_width // PHASES * PARTS,)),
        ],
        compiler_params=params,
        name="correlate",
    )(*[held[step] for step in steps(lags, segments)])


def solution(mesh):
    return jax.shard_map(
        shards,
        mesh=mesh,
        in_specs=(P("chan", "seg", "lag"), P(), P()),
        out_specs=P(("chan", "seg"), "lag"),
        check_vma=False,
    )
```

```python
import functools
import math

import jax
import jax.numpy as jnp
from jax import lax
from jax.experimental import pallas as pl
from jax.experimental.pallas import tpu as pltpu
from jax.sharding import PartitionSpec as P

LAGS = 128
SAMPLES = 2048
PHASES = 8


def halves(value):
    high = value.astype(jnp.bfloat16)
    low = (value - high.astype(jnp.float32)).astype(jnp.bfloat16)
    return high, low


def product(left, right):
    return jnp.dot(left, right, preferred_element_type=jnp.float32)


def product_nt(left, right):
    return lax.dot_general(
        left, right, (((1,), (1,)), ((), ())), preferred_element_type=jnp.float32
    )


def steps(lags, segments):
    return [(lag, segment) for lag in range(lags) for segment in range(segments)]


def swapped(value, lag_step, segment_step):
    lags, segments = lax.axis_size("lag"), lax.axis_size("seg")
    pairs = [
        (lag * segments + segment, (lag ^ lag_step) * segments + (segment ^ segment_step))
        for lag, segment in steps(lags, segments)
    ]
    return lax.ppermute(value, ("lag", "seg"), pairs)


def across(value, step):
    return lax.ppermute(value, "chan", [(i, i ^ step) for i in range(lax.axis_size("chan"))])


def paired(value, order):
    lags = lax.axis_size("lag")
    pairs = [
        (chan * lags + lag, (chan ^ order[lag % 2]) * lags + lag)
        for chan in range(lax.axis_size("chan"))
        for lag in range(lags)
    ]
    return lax.ppermute(value, ("chan", "lag"), pairs)


def choice(pick, rows):
    high, low = halves(rows)
    return product(pick, high) + product(pick, low)


def counts_before(present):
    rows = present.shape[0]
    line = lax.broadcasted_iota(jnp.int32, (rows, rows), 0)
    lane = lax.broadcasted_iota(jnp.int32, (rows, rows), 1)
    return product((lane < line).astype(jnp.bfloat16), present.astype(jnp.bfloat16))


def columns(refs_ref, width):
    return jnp.broadcast_to(refs_ref[...], (width, refs_ref.shape[1])).T


def choose_four_kernel(
    records_ref,
    lists_ref,
    refs_ref,
    own_ref,
    send_ref,
    keep_ref,
    take_ref,
    held_ref,
    done,
):
    copy = pltpu.make_async_copy(records_ref, held_ref, done)
    copy.start()
    rows = lists_ref.shape[1]
    kept = take_ref.shape[1]
    refs = refs_ref.shape[1]
    me = lax.axis_index("chan")
    odd = lax.rem(lax.axis_index("lag"), 2)
    near, far = 2 - odd, 1 + odd
    line = lax.broadcasted_iota(jnp.int32, (rows, 2 * rows), 0)

    def pool(owner):
        lists = [lists_ref[pl.ds(lax.bitwise_xor(owner, i), 1), :] for i in (0, near)]
        return jnp.concatenate(lists, axis=1)

    def where(owner, block):
        return pool(owner) == line + block * rows

    def ranks(found):
        present = jnp.max(found.astype(jnp.float32), axis=1, keepdims=True)
        return present, counts_before(jnp.broadcast_to(present, (rows, rows)))

    other = lax.bitwise_xor(me, far)
    found = where(me, other)
    _, rank = ranks(found)
    rank = jnp.concatenate([rank, rank], axis=1)
    slot = jnp.sum(jnp.where(found, rank + 1.0, 0.0), axis=0, keepdims=True).astype(jnp.int32)
    send = jnp.concatenate([line[:kept] + 1 == slot, columns(refs_ref, 2 * rows) == pool(me)], axis=0)
    send = send.astype(jnp.bfloat16)
    keep = where(me, me).astype(jnp.bfloat16)
    send_ref[...] = send
    keep_ref[...] = keep
    present, rank = ranks(where(other, me))
    lane = lax.broadcasted_iota(jnp.int32, (rows, kept), 1)
    slot = jnp.where(present > 0.0, rank[:, :kept], -1.0).astype(jnp.int32)
    take_ref[...] = (lane == slot).astype(jnp.bfloat16)
    copy.wait()
    own_ref[...] = held_ref[:, 0, :]


def pick_kernel(own_ref, arrived_ref, send_ref, keep_ref, sent_ref, base_ref):
    rows = jnp.concatenate([own_ref[...], arrived_ref[:, 0, :]], axis=0)
    high, low = halves(rows)
    sent_ref[...] = product(send_ref[...], high) + product(send_ref[...], low)
    base_ref[...] = product(keep_ref[...], high) + product(keep_ref[...], low)


def put(series, panel, out_refs):
    segments = len(out_refs)
    kept = series.shape[0] // segments
    own = lax.axis_index("seg")
    for part in range(segments):
        half = lax.bitwise_xor(own, part)
        chosen = series[:kept]
        for other in range(1, segments):
            chosen = jnp.where(half == other, series[other * kept : (other + 1) * kept], chosen)
        out_refs[part][:kept, :] = chosen
        out_refs[part][kept:, :] = panel


def place_four_kernel(base_ref, take_ref, sent_ref, arrived_ref, *out_refs):
    kept = take_ref.shape[1]
    series = base_ref[...] + choice(take_ref[...], arrived_ref[:kept, :])
    put(series, sent_ref[kept:, :] + arrived_ref[kept:, :], out_refs)


def pack_kernel(records_ref, lists_ref, refs_ref, out_ref, panel_ref):
    rows = records_ref.shape[0]
    refs = refs_ref.shape[1]
    own = jnp.broadcast_to(lists_ref[pl.ds(lax.axis_index("chan"), 1), :], (rows, rows))
    rank = jnp.sum((own.T < own).astype(jnp.int32), axis=0, keepdims=True)
    line = lax.broadcasted_iota(jnp.int32, (rows, rows), 0)
    records = records_ref[:, 0, :]
    panel_ref[...] = choice((columns(refs_ref, rows) == own[:refs]).astype(jnp.bfloat16), records)
    out_ref[...] = choice((line == rank).astype(jnp.bfloat16), records)


def choose_kernel(peers, lists_ref, pick_ref):
    rows = lists_ref.shape[1]
    share = rows // peers
    lane = lax.broadcasted_iota(jnp.int32, (rows, rows), 1)
    channel = lax.broadcasted_iota(jnp.int32, (rows, rows), 0) + lax.axis_index("chan") * rows
    owner = jnp.zeros((rows, 1), jnp.int32)
    for peer in range(peers):
        found = (lists_ref[pl.ds(peer, 1), :] == channel).astype(jnp.int32)
        owner = owner + jnp.sum(found, axis=1, keepdims=True) * peer
    same = lane == owner
    before = counts_before(same.astype(jnp.float32))
    rank = jnp.sum(jnp.where(same, before, 0.0), axis=1, keepdims=True).astype(jnp.int32)
    pick_ref[...] = (lane == owner * share + rank).astype(jnp.bfloat16)


def place_kernel(pick_ref, panel_ref, arrived_ref, *out_refs):
    put(choice(pick_ref[...], arrived_ref[...]), panel_ref[...], out_refs)


def corr_kernel(refs, lag_width, *rest):
    *chunk_refs, out_ref, joined_ref, series_ref, panel_ref = rest
    kept = out_ref.shape[0]
    lags, segments = lax.axis_size("lag"), lax.axis_size("seg")
    width = chunk_refs[0].shape[1]
    for (lag_step, segment_step), chunk_ref in zip(steps(lags, segments), chunk_refs):
        lag = lax.bitwise_xor(lax.axis_index("lag"), lag_step)
        segment = lax.bitwise_xor(lax.axis_index("seg"), segment_step)
        start = pl.multiple_of((segment * lags + lag) * width, width)
        joined_ref[:, pl.ds(start, width)] = chunk_ref[...]
    series = joined_ref[:kept, :]
    panel = joined_ref[kept:, :]
    samples = panel.shape[1]
    terms = SAMPLES - LAGS
    times = lax.broadcasted_iota(jnp.int32, panel.shape, 1)
    panel = jnp.where(times < terms, panel, 0.0)
    groups = lag_width // PHASES

    def spread(value, count, step, out_ref, begin=0):
        lines = value.shape[0]
        for half, part in enumerate(halves(value)):
            for i in range(count):
                start = (half * count + i) * lines
                out_ref[start : start + lines, :] = (
                    part
                    if not i and step > 0
                    else pltpu.roll(part, begin + i * step, 1)
                )

    spread(panel, PHASES, 1, panel_ref)
    begin = -lax.axis_index("lag") * lag_width
    spread(series, groups, -PHASES, series_ref, begin + samples)
    lines, columns = groups * kept, PHASES * refs
    upper = product_nt(series_ref[...], panel_ref[:columns, :])
    lower = product_nt(series_ref[:lines, :], panel_ref[columns:, :])
    total = (upper[:lines] + upper[lines:] + lower) * (1.0 / math.sqrt(terms))
    for group in range(groups):
        out_ref[:, group * columns : (group + 1) * columns] = total[
            group * kept : (group + 1) * kept
        ]


def shards(records_owned, section_list, ref_index):
    peers = lax.axis_size("chan")
    segments = lax.axis_size("seg")
    rows, _, samples = records_owned.shape
    refs = ref_index.shape[0]
    share = rows // peers
    kept = rows // segments
    lags = lax.axis_size("lag")
    lag_width = LAGS // lags
    lists = section_list.reshape(peers, rows)
    params = pltpu.CompilerParams(vmem_limit_bytes=48 * 1024 * 1024)
    wanted = ref_index.reshape(1, refs)

    def block(*shape, dtype=jnp.float32):
        return jax.ShapeDtypeStruct(shape, dtype)

    def call(kernel, name, shapes, *operands):
        return pl.pallas_call(kernel, out_shape=shapes, compiler_params=params, name=name)(*operands)

    shapes = [block(kept + refs, samples)] * segments
    if peers == 4:
        first = paired(records_owned, (2, 1))
        half = rows // 2
        whole = pl.BlockSpec(memory_space=pltpu.VMEM)
        own, send, keep, take = pl.pallas_call(
            choose_four_kernel,
            out_shape=[
                block(rows, samples),
                block(half + refs, 2 * rows, dtype=jnp.bfloat16),
                block(rows, 2 * rows, dtype=jnp.bfloat16),
                block(rows, half, dtype=jnp.bfloat16),
            ],
            in_specs=[pl.BlockSpec(memory_space=pl.ANY), whole, whole],
            scratch_shapes=[pltpu.VMEM(records_owned.shape, jnp.float32), pltpu.SemaphoreType.DMA],
            compiler_params=params,
            name="choose",
        )(pltpu.with_memory_space_constraint(records_owned, pltpu.HBM), lists, wanted)
        results = [block(half + refs, samples), block(rows, samples)]
        sent, base = call(pick_kernel, "pick", results, own, first, send, keep)
        placed = call(place_four_kernel, "place", shapes, base, take, sent, paired(sent, (1, 2)))
    else:
        packed, panel = call(
            pack_kernel,
            "pack",
            [block(rows, samples), block(refs, samples)],
            records_owned,
            lists,
            wanted,
        )
        blocks = packed.reshape(peers, share, samples)
        blocks = lax.all_to_all(blocks, "chan", split_axis=0, concat_axis=0, tiled=True)
        step = 1
        while step < peers:
            panel = panel + across(panel, step)
            step *= 2
        pick = call(
            functools.partial(choose_kernel, peers),
            "choose",
            block(rows, rows, dtype=jnp.bfloat16),
            lists,
        )
        placed = call(place_kernel, "place", shapes, pick, panel, blocks.reshape(rows, samples))
    held = {(0, 0): placed[0]}
    for lag_step in range(0, lags, 2):
        for segment_step in range(segments):
            if lag_step or segment_step:
                held[lag_step, segment_step] = swapped(placed[segment_step], lag_step, segment_step)
    for lag_step, segment_step in list(held):
        held[lag_step + 1, segment_step] = swapped(held[lag_step, segment_step], 1, 0)
    return pl.pallas_call(
        functools.partial(corr_kernel, refs, lag_width),
        out_shape=jax.ShapeDtypeStruct((kept, lag_width * refs), jnp.float32),
        scratch_shapes=[
            pltpu.VMEM((kept + refs, lags * segments * samples), jnp.float32),
            pltpu.VMEM((2 * lag_width // PHASES * kept, lags * segments * samples), jnp.bfloat16),
            pltpu.VMEM((2 * PHASES * refs, lags * segments * samples), jnp.bfloat16),
        ],
        compiler_params=params,
        name="correlate",
    )(*[held[step] for step in steps(lags, segments)])


def solution(mesh):
    return jax.shard_map(
        shards,
        mesh=mesh,
        in_specs=(P("chan", "seg", "lag"), P(), P()),
        out_specs=P(("chan", "seg"), "lag"),
        check_vma=False,
    )
```
